32 devices in a mesh: items: 16 (over z, y, x), seq: 2 (over core).
Axes of the slice: x: 2, y: 2, z: 4, core: 2. Of those that a mesh axis runs over, the one named last changes fastest.
Arguments:
- tokens: bfloat16 [16, 512, 1024], P('items', 'seq'), may hold values from -6 to 6
- lengths: int32 [16], P('items'), may hold values from 257 to 512, as said below
- cotangent: bfloat16 [16, 512, 1024], P('items', 'seq'), may hold values from -6 to 6
- qkv_weight: bfloat16 [2, 1024, 3072], P(None, 'items'), may hold values from -0.1875 to 0.1875
- out_weight: bfloat16 [2, 1024, 1024], P(None, 'items'), may hold values from -2 to 2
- up_weight: bfloat16 [2, 1024, 4096], P(None, 'items'), may hold values from -0.1875 to 0.1875
- down_weight: bfloat16 [2, 4096, 1024], P(None, 'items'), may hold values from -0.09375 to 0.09375
- norm_gain: float32 [2, 2, 1024], replicated, may hold values from 0.5 to 1.5
- bias_master: float32 [2, 10240], P(None, 'items'), may hold values from -1 to 1
- first_moment: float32 [2, 10240], P(None, 'items')
- second_moment: float32 [2, 10240], P(None, 'items'), as said below
Outputs:
- layer_out: bfloat16 [16, 512, 1024], P('items', 'seq')
- input_grad: bfloat16 [16, 512, 1024], P('items', 'seq')
- bias_grad: float32 [2, 10240], P(None, 'items')
- new_first: float32 [2, 10240], P(None, 'items')
- new_second: float32 [2, 10240], P(None, 'items')
- new_bias: float32 [2, 10240], P(None, 'items')
The draws below stay inside these ranges and needn't reach their ends.
Inputs may be any that keep to these rules, and one draw needn't show every extreme that they name: `lengths`: positions below an item's length are its tokens and the rest padding; every draw has an item at each bound. `second_moment`: positive.
All inputs are finite; a program needn't handle non-finite values.
Results may differ from the reference program's by a relative error of at most 0.02.
Values may be sent and summed in bfloat16 or wider, within the bound.
No kernel may reach another device: no remote copies, remote signals or barrier semaphores. Data moves between devices by JAX's collectives and lax.ppermute only.
A program may use at most 192 MiB of HBM per device.

```python
import math
import jax
import jax.numpy as jnp
from jax import lax

D = 1024
HEADS = 16
HEAD_DIM = 64
FF = 4096
LAYERS = 2
LENGTH = 512
STEP = 10
ITEMS = 16
NBL = 10240
N_SEQ = 2


def draw_lengths(key, part):
    key = jax.random.fold_in(key, 7)
    lowest = LENGTH - LENGTH // N_SEQ + 1
    span_size = LENGTH - lowest + 1
    key_list = jax.random.split(key, 4)
    first_draw = jax.random.randint(key_list[0], (ITEMS,), 0, span_size)
    second_draw = jax.random.randint(key_list[1], (ITEMS,), 0, span_size)
    third_draw = jax.random.randint(key_list[2], (ITEMS,), 0, span_size)
    picked = jnp.minimum(jnp.minimum(first_draw, second_draw), third_draw)
    result = lowest + picked
    order_draw = jax.random.permutation(key_list[3], ITEMS)
    result = result.at[order_draw[0]].set(LENGTH)
    result = result.at[order_draw[1]].set(lowest)
    return result.astype(jnp.int32)


def moment_scale():
    kind_factor = jnp.array([0.3, 0.5 * math.sqrt(LENGTH / 4.0), 0.55, 0.8, 0.2, 0.2, 0.2, 0.2, 0.7, 1.0], jnp.float32)
    factor = jnp.tile(kind_factor, D)
    depth_factor = 0.7 ** (LAYERS - 1 - jnp.arange(LAYERS, dtype=jnp.float32))
    token_root = math.sqrt(ITEMS * LENGTH * 0.6)
    return depth_factor[:, None] * factor[None, :] * token_root


def draw_first_moment(key, part):
    key = jax.random.fold_in(key, 17)
    noise = jax.random.normal(key, (LAYERS, NBL), jnp.float32)
    return 0.111 * moment_scale() * jnp.clip(noise, -4.0, 4.0)


def draw_second_moment(key, part):
    key = jax.random.fold_in(key, 29)
    exponent = jax.random.uniform(key, (LAYERS, NBL), jnp.float32, math.log(0.5), math.log(8.0))
    scale_grid = moment_scale()
    return 0.001 * scale_grid * scale_grid * jnp.exp(exponent)


def level_of(key, dims, cuts, smallest, largest):
    def one(position, shards_of):
        draws = jax.random.uniform(jax.random.fold_in(jax.random.fold_in(key, 6), position), (shards_of,), jnp.float32, smallest / len(cuts), largest / len(cuts))
        return jnp.repeat(jnp.exp(draws), dims[position] // shards_of).reshape((-1,) + (1,) * (len(dims) - position - 1))

    loudness = one(*cuts[0])
    for cut in cuts[1:]:
        loudness = loudness * one(*cut)
    return loudness


def centred(key, shape, scale, bound, cuts=(), kind=jnp.bfloat16):
    values = scale * jax.random.normal(key, shape, jnp.float32)
    if cuts:
        values = values * level_of(key, shape, cuts, -0.22, 0.18)
    return jnp.clip(values, -bound, bound).astype(kind)


def setup_inputs(seed: int = 0) -> dict:
    arg_keys = jax.random.split(jax.random.key(seed), 12)
    tokens = centred(arg_keys[0], (ITEMS, LENGTH, D), 1.0, 6.0, ((0, 16), (1, 2)))
    lengths = draw_lengths(jax.random.fold_in(arg_keys[11], 71), 0)
    cotangent = centred(arg_keys[2], (ITEMS, LENGTH, D), 1.0, 6.0, ((0, 16), (1, 2)))
    qkv_weight = centred(arg_keys[3], (LAYERS, D, 3 * D), D ** -0.5, 0.1875, ((1, 16),))
    out_weight = centred(arg_keys[4], (LAYERS, D, D), (D * 4 // LENGTH) ** -0.5, 2.0, ((1, 16),))
    up_weight = centred(arg_keys[5], (LAYERS, D, FF), D ** -0.5, 0.1875, ((1, 16),))
    down_weight = centred(arg_keys[6], (LAYERS, FF, D), FF ** -0.5, 0.09375, ((1, 16),))
    norm_gain = jnp.clip(1.0 + 0.1 * jax.random.normal(arg_keys[7], (LAYERS, 2, D), jnp.float32), 0.5, 1.5)
    bias_master = centred(arg_keys[8], (LAYERS, NBL), 0.2, 1.0, ((1, 16),), jnp.float32)
    first_moment = draw_first_moment(jax.random.fold_in(arg_keys[11], 71), 0)
    second_moment = draw_second_moment(jax.random.fold_in(arg_keys[11], 71), 0)
    return {"tokens": tokens, "lengths": lengths, "cotangent": cotangent, "qkv_weight": qkv_weight, "out_weight": out_weight, "up_weight": up_weight, "down_weight": down_weight, "norm_gain": norm_gain, "bias_master": bias_master, "first_moment": first_moment, "second_moment": second_moment}


@jax.custom_vjp
def low(v):
    return lax.optimization_barrier(v.astype(jnp.bfloat16)).astype(jnp.float32)

@jax.custom_vjp
def low_back(v):
    return v

def low_keep(v):
    return (low(v), None)

def low_pass(kept, grad):
    return (grad,)

def back_keep(v):
    return (v, None)

def back_low(kept, grad):
    return (low(grad),)
low.defvjp(low_keep, low_pass)
low_back.defvjp(back_keep, back_low)
ln_eps = 1e-12
beta_one = 0.9
beta_two = 0.999
adam_eps = 1e-08
learn_rate = 0.4
masked_score = -1000000000.0

def product(left_side, right_side):
    return jnp.dot(left_side, right_side, precision=lax.Precision.HIGHEST, preferred_element_type=jnp.float32)

def normalize(values_in, gain_row, shift_row):
    center = values_in - lax.optimization_barrier(jnp.mean(values_in, axis=-1, keepdims=True))
    spread = lax.optimization_barrier(jnp.mean(center * center, axis=-1, keepdims=True))
    return center * lax.rsqrt(spread + ln_eps) * gain_row + shift_row

def split_bias(bias_row):
    bias_grid = bias_row.reshape(D, 10)
    return (bias_grid[:, 0], bias_grid[:, 1], bias_grid[:, 2], bias_grid[:, 3], bias_grid[:, 4:8].reshape(FF), bias_grid[:, 8], bias_grid[:, 9])

def attend(block_in):
    queries, key_rows, values, length = block_in
    queries = queries.reshape(LENGTH, HEADS, HEAD_DIM)
    key_rows = key_rows.reshape(LENGTH, HEADS, HEAD_DIM)
    values = values.reshape(LENGTH, HEADS, HEAD_DIM)
    scores = jnp.einsum('qhd,khd->hqk', queries, key_rows, precision=lax.Precision.HIGHEST, preferred_element_type=jnp.float32) * (1.0 / math.sqrt(HEAD_DIM))
    live_keys = jnp.arange(LENGTH, dtype=jnp.int32) < length
    scores = low_back(jnp.where(live_keys[None, None, :], scores, masked_score))
    row_max = lax.optimization_barrier(jnp.max(scores, axis=-1, keepdims=True))
    weights = jnp.exp(scores - row_max)
    weights = low(weights / lax.optimization_barrier(jnp.sum(weights, axis=-1, keepdims=True)))
    mixed_out = jnp.einsum('hqk,khd->qhd', weights, values, precision=lax.Precision.HIGHEST, preferred_element_type=jnp.float32)
    return mixed_out.reshape(LENGTH, D)

def run_layer(inputs, bias_row, qkv_full, out_full, up_full, down_full, gain_pair, item_lengths):
    group_count = inputs.shape[0]
    row_block = inputs.reshape(group_count * LENGTH, D)
    bias_q, bias_v, bias_o, shift_one, bias_up, bias_down, shift_two = split_bias(bias_row)
    queries = low(low_back(product(row_block, qkv_full[:, :D])) + bias_q)
    key_rows = low(low_back(product(row_block, qkv_full[:, D:2 * D])))
    values = low(low_back(product(row_block, qkv_full[:, 2 * D:])) + bias_v)

    def shaped(t):
        return t.reshape(group_count, LENGTH, D)
    mixed_out = lax.map(jax.checkpoint(attend), (shaped(queries), shaped(key_rows), shaped(values), item_lengths))
    mixed_out = low_back(low(mixed_out.reshape(group_count * LENGTH, D)))
    summed = row_block + low_back(product(mixed_out, out_full)) + bias_o
    normed = low(normalize(summed, gain_pair[0], shift_one))
    hidden = low_back(product(normed, up_full)) + bias_up
    active = low(jax.nn.gelu(hidden, approximate=False))
    resid_sum = normed + low_back(product(active, down_full)) + bias_down
    return low(normalize(resid_sum, gain_pair[1], shift_two)).reshape(group_count, LENGTH, D)

def reference(tokens, lengths, cotangent, qkv_weight, out_weight, up_weight, down_weight, norm_gain, bias_master, first_moment, second_moment):
    group_size = 1
    for option in range(1, ITEMS + 1):
        if ITEMS % option == 0 and option * LENGTH <= 4096:
            group_size = option
    blocks = ITEMS // group_size
    qkv_wide = qkv_weight.astype(jnp.float32)
    out_wide = out_weight.astype(jnp.float32)
    up_wide = up_weight.astype(jnp.float32)
    down_wide = down_weight.astype(jnp.float32)

    def forward(bias_all, inputs, item_lengths):
        hidden_state = inputs
        for layer_num in range(LAYERS):
            hidden_state = run_layer(low_back(hidden_state), bias_all[layer_num], qkv_wide[layer_num], out_wide[layer_num], up_wide[layer_num], down_wide[layer_num], norm_gain[layer_num], item_lengths)
        return hidden_state

    def visit_block(grad_total, block_in):
        inputs, upstream, item_lengths = block_in
        live_rows = (jnp.arange(LENGTH, dtype=jnp.int32)[None, :] < item_lengths[:, None]).astype(jnp.float32)
        outputs, pull_back = jax.vjp(lambda b, x: forward(b, x, item_lengths), bias_master, inputs)
        grad_bias, grad_input = pull_back(upstream * live_rows[:, :, None])
        return (grad_total + grad_bias, (outputs.astype(jnp.bfloat16), grad_input.astype(jnp.bfloat16)))
    stacked = (tokens.astype(jnp.float32).reshape(blocks, group_size, LENGTH, D), cotangent.astype(jnp.float32).reshape(blocks, group_size, LENGTH, D), lengths.reshape(blocks, group_size))
    bias_grad, (layer_out, input_grad) = lax.scan(visit_block, jnp.zeros((LAYERS, NBL), jnp.float32), stacked)
    layer_out = layer_out.reshape(ITEMS, LENGTH, D)
    input_grad = input_grad.reshape(ITEMS, LENGTH, D)
    new_first = beta_one * first_moment + (1.0 - beta_one) * bias_grad
    new_second = beta_two * second_moment + (1.0 - beta_two) * bias_grad * bias_grad
    first_hat = new_first / (1.0 - beta_one ** STEP)
    second_hat = new_second / (1.0 - beta_two ** STEP)
    new_bias = bias_master - learn_rate * first_hat / (jnp.sqrt(second_hat) + adam_eps)
    return (layer_out, input_grad, bias_grad, new_first, new_second, new_bias)
```

```python
import functools
import math

import jax
import jax.numpy as jnp
from jax import lax
from jax.experimental import pallas as pl
from jax.experimental.pallas import tpu as pltpu
from jax.sharding import PartitionSpec as P

HEAD_DIM = 64
STEP = 10

ln_eps = 1e-12
beta_one = 0.9
beta_two = 0.999
adam_eps = 1e-08
learn_rate = 0.4
masked_score = -1000000000.0

CHIPS = {16: (4, 2, 2)}
CHUNKS = ((0, "attn"), (0, "up"), (0, "down"), (1, "attn"), (1, "up"), (1, "down"))
LAST = len(CHUNKS) - 1
KERNELS = {
    3: (("attention", 0),),
    4: (("up", 0),),
    5: (("down", 0), ("attention", 1)),
    6: (("up", 1), ("down", 1)),
}
SLOTS = 16
TILE = 256
WIDE = 512
STRIP = 32
F32 = jnp.float32
BF16 = jnp.bfloat16
VMEM_BYTES = 56 * 1024 * 1024

VMEM = pl.BlockSpec(memory_space=pltpu.VMEM)
SMEM = pl.BlockSpec(memory_space=pltpu.SMEM)
ANY = pl.BlockSpec(memory_space=pl.ANY)


def own_blocks(qkv_weight, out_weight, up_weight, down_weight):
    levels, rows, width = out_weight.shape
    keys = [(level, kind) for level in range(levels) for kind in ("attn", "up", "down")]
    core = lax.axis_index("seq").astype(jnp.int32).reshape(1)

    def kernel(core_ref, qkv, out, up, down, *refs):
        targets, (held, come, go) = refs[: len(keys)], refs[len(keys) :]
        here = core_ref[0]

        def copies(number, core):
            level, kind = keys[number]
            for half in range(2):
                if kind == "attn" and core == 0:
                    source = qkv.at[level, :, pl.ds(half * width, width)]
                elif kind == "attn":
                    source = out.at[level] if half else qkv.at[level, :, pl.ds(2 * width, width)]
                elif kind == "up":
                    column = pl.multiple_of((2 * here + half) * width, width)
                    source = up.at[level, :, pl.ds(column, width)]
                else:
                    row = pl.multiple_of((2 * here + half) * rows, rows)
                    source = down.at[level, pl.ds(row, rows), :]
                target = held.at[number, pl.ds(half * rows, rows), :]
                yield pltpu.make_async_copy(source, target, come.at[number, half])

        def each(act):
            for number, (_, kind) in enumerate(keys):
                if kind != "attn":
                    act(number, 0)
                    continue
                for side in range(2):
                    pl.when(here == side)(functools.partial(act, number, side))

        def begin(number, side):
            for copy in copies(number, side):
                copy.start()

        def finish(number, side):
            for copy in copies(number, side):
                copy.wait()

        each(begin)
        each(finish)
        leaving = [
            pltpu.make_async_copy(held.at[n], target, go.at[n]) for n, target in enumerate(targets)
        ]
        for copy in leaving:
            copy.start()
        for copy in leaving:
            copy.wait()

    blocks = pl.pallas_call(
        kernel,
        name="own_blocks",
        out_shape=[jax.ShapeDtypeStruct((2 * rows, width), BF16)] * len(keys),
        in_specs=[SMEM] + [ANY] * 4,
        out_specs=[ANY] * len(keys),
        scratch_shapes=[
            pltpu.VMEM((len(keys), 2 * rows, width), BF16),
            pltpu.SemaphoreType.DMA((len(keys), 2)),
            pltpu.SemaphoreType.DMA((len(keys),)),
        ],
        compiler_params=pltpu.CompilerParams(vmem_limit_bytes=VMEM_BYTES),
        cost_estimate=pl.CostEstimate(
            flops=0, bytes_accessed=8 * rows * width * len(keys), transcendentals=0
        ),
    )(core, qkv_weight, out_weight, up_weight, down_weight)
    return dict(zip(keys, blocks))


class Chunk:
    def __init__(self, arrays, runs, order):
        self.arrays, self.runs, self.order = arrays, runs, order
        self.count = sum(len(quarter) for quarter in runs)


def join(blocks, places=None):
    width = blocks[0].shape[1]
    total = sum(block.shape[0] for block in blocks)
    starts = [sum(block.shape[0] for block in blocks[:n]) for n in range(len(blocks))]
    table = [] if places is None else [places]

    def kernel(*refs):
        table_ref, refs = refs[: len(table)], refs[len(table) :]
        sources, (target, held, come, go) = refs[: len(blocks)], refs[len(blocks) :]
        ins, outs = [], []
        for n, (source, start) in enumerate(zip(sources, starts)):
            rows = blocks[n].shape[0]
            span = there = pl.ds(start, rows)
            if table:
                there = pl.ds(pl.multiple_of(table_ref[0][n] * rows, rows), rows)
            ins.append(pltpu.make_async_copy(source, held.at[span], come.at[n]))
            outs.append(pltpu.make_async_copy(held.at[span], target.at[there], go.at[n]))
            ins[-1].start()
        for come_in, go_out in zip(ins, outs):
            come_in.wait()
            go_out.start()
        for go_out in outs:
            go_out.wait()

    return pl.pallas_call(
        kernel,
        name="join",
        out_shape=jax.ShapeDtypeStruct((total, width), BF16),
        in_specs=[SMEM] * len(table) + [ANY] * len(blocks),
        out_specs=ANY,
        scratch_shapes=[
            pltpu.VMEM((total, width), BF16),
            pltpu.SemaphoreType.DMA((len(blocks),)),
            pltpu.SemaphoreType.DMA((len(blocks),)),
        ],
        compiler_params=pltpu.CompilerParams(vmem_limit_bytes=VMEM_BYTES),
        cost_estimate=pl.CostEstimate(
            flops=0, bytes_accessed=4 * total * width, transcendentals=0
        ),
    )(*table, *blocks)


class Gather:
    def __init__(self, *weights):
        self.total = lax.axis_size("items")
        self.depth, _, _ = CHIPS[self.total]
        self.plane = self.total // self.depth
        self.rows = weights[1].shape[1]
        self.mine = own_blocks(*weights)
        here = lax.axis_index("items") % self.plane
        core = lax.axis_index("seq")
        order = [here ^ side for side in range(4)]
        order += [core * 2, core * 2 + 1, 2 - core * 2, 3 - core * 2]
        self.order = jnp.stack(order).astype(jnp.int32)
        self.stages = [{} for _ in CHUNKS]
        self.last, self.computed = [], []

    def over_z(self, block):
        lines = [
            [place + self.plane * z for z in range(self.depth)] for place in range(self.plane)
        ]
        return lax.all_gather(block, "items", axis=0, tiled=True, axis_index_groups=lines)

    def step_z(self, block, step):
        pairs = [(item, (item + step * self.plane) % self.total) for item in range(self.total)]
        return lax.ppermute(block, "items", pairs)

    def line_of(self, parts):
        here = lax.axis_index("items") // self.plane
        places = [(here - step + self.depth) % self.depth for step in range(self.depth)]
        return join(parts, jnp.stack(places).astype(jnp.int32))

    def over(self, bit, block):
        return lax.ppermute(block, "items", [(item, item ^ bit) for item in range(self.total)])

    def across(self, x, y):
        half = x.shape[0] // 2
        return self.over(2, x[:half]), self.over(1, y[half:])

    def joined(self, stage):
        return join([stage[name] for name in ("z", "x", "y", "xy", "yx")])

    def cycle(self, number):
        wanted = {}
        if number == 0:
            wanted["corner"] = self.stages[LAST]["sides"][1:]
        if number == 1:
            wanted["sides"] = self.stages[LAST]["sides"]
        if 0 <= number < LAST - 1:
            wanted["block"] = self.mine[CHUNKS[number + 1]]
        if number == -1:
            wanted["first"] = self.mine[CHUNKS[0]]
            wanted["plane"] = self.mine[CHUNKS[LAST]]
        if LAST - 1 <= number <= LAST:
            wanted["line"] = self.stages[LAST]["lines"][number - LAST + 1]
        for lag in range(4):
            if 0 <= number - lag < LAST:
                wanted["lag%d" % lag] = self.stages[number - lag]
        def put(stage, name, value):
            stage[name] = value
            self.last.append(value)

        if 0 <= number <= LAST:
            self.before = self.last + self.computed
            wanted, _ = lax.optimization_barrier((wanted, self.before))
            self.last, self.computed = [], []
        elif number == -1:
            first = wanted["first"]
            steps = [self.step_z(first, step) for step in range(1, self.depth)]
            put(self.stages[0], "z", self.line_of([first, *steps]))

        if "lag3" in wanted:
            stage = self.stages[number - 3]
            if "joined" not in stage:
                put(stage, "joined", self.joined(wanted["lag3"]))
                wanted["lag3"] = stage
            put(stage, "other", swap_cores(wanted["lag3"]["joined"]))
        if "lag0" in wanted:
            along, stage = wanted["lag0"]["z"], self.stages[number]
            put(stage, "x", self.over(1, along))
            put(stage, "y", self.over(2, along))
        if "lag1" in wanted:
            held, stage = wanted["lag1"], self.stages[number - 1]
            stage["xy"], stage["yx"] = self.across(held["x"], held["y"])
            self.last += [stage["xy"], stage["yx"]]
        if "lag2" in wanted and number < LAST:
            put(self.stages[number - 2], "joined", self.joined(wanted["lag2"]))
        if "block" in wanted:
            put(self.stages[number + 1], "z", self.over_z(wanted["block"]))
        stage = self.stages[LAST]
        if LAST - 1 <= number <= LAST:
            stage.setdefault("z", []).append(self.over_z(wanted["line"]))
            if number < LAST:
                self.last.append(stage["z"][-1])
        if "plane" in wanted:
            own = wanted["plane"]
            x, y = self.over(1, own), self.over(2, own)
            stage["sides"] = [own, x, y]
            self.last += [x, y]
        if number == 0:
            x, y = wanted["corner"]
            stage["sides"] += self.across(x, y)
            self.last += stage["sides"][3:]
        if number == 1:
            _, x, y, xy, yx = wanted["sides"]
            stage["lines"] = [join([x, y[: self.rows]]), join([y[self.rows :], xy, yx])]
            self.last += stage["lines"]
        if 0 <= number < self.depth - 1:
            stage.setdefault("steps", [stage["sides"][0]])
            own, _ = lax.optimization_barrier((stage["steps"][0], self.before))
            stage["steps"].append(self.step_z(own, number + 1))
            self.last.append(stage["steps"][-1])
        if number == self.depth - 1:
            stage["z"] = [self.line_of(stage["steps"])]
            self.last.append(stage["z"][0])
    def swap_far(self, number, after):
        stage = self.stages[number]
        far, _ = lax.optimization_barrier(((stage["xy"], stage["yx"]), after))
        stage["xy2"], stage["yx2"] = [swap_cores(part) for part in far]
        return stage["xy2"], stage["yx2"]

    def swap_last(self, number, after):
        stage = self.stages[LAST]
        block, _ = lax.optimization_barrier((stage["z"][number], after))
        stage.setdefault("z2", []).append(swap_cores(block))
        return stage["z2"][-1]

    def chunk(self, key):
        number = CHUNKS.index(key)
        stage = self.stages[number]
        order = self.order
        if number == LAST:
            arrays = stage["z"] + stage["z2"]
            arrays = [a.reshape(self.depth, -1, self.rows, a.shape[1]) for a in arrays]
            spots = [(0, 0), (0, 1)] + [(1, n) for n in range(3)] + [(2, n) for n in range(3)]
            runs = [
                [
                    (array + spots[2 * side + part][0], spots[2 * side + part][1], 0, side, 0, self.depth)
                    for side in range(4)
                ]
                for array in (0, 3)
                for part in range(2)
            ]
            return Chunk(arrays, runs, order)
        half = self.depth // 2
        places = [(0, 0, self.depth), (1, 0, self.depth), (2, 0, self.depth)]
        places += [(3, 0, half), (3, half, self.depth - half)]
        own = [(n, 0, *place) for n, place in enumerate(places)]
        block = 2 * self.rows
        first = [0, self.depth, 2 * self.depth, 3 * self.depth, 3 * self.depth + half]
        other = [(5, *pair) for pair in ((first[n], *places[n]) for n in range(5))]
        names = ["z", "x", "y", "xy", "yx", "other"]
        if number == LAST - 1:
            late, _ = lax.optimization_barrier(
                (join([stage[name] for name in names[:3]]), self.after)
            )
            stage["other"] = swap_cores(late)
            other[3:] = [(6, 0, *places[3]), (7, 0, *places[4])]
            names += ["xy2", "yx2"]
        elif "other" not in stage:
            stage["other"] = swap_cores(self.joined(stage))
        arrays = [stage[name] for name in names]
        runs = [
            [(array, part, first, side, z, number) for array, first, side, z, number in spans]
            for spans in (own, other)
            for part in range(2)
        ]
        arrays = [a.reshape(a.shape[0] // block, 2, self.rows, a.shape[1]) for a in arrays]
        return Chunk(arrays, runs, order)


def gather_plainly(qkv_weight, out_weight, up_weight, down_weight):
    shards = {}
    for level in range(out_weight.shape[0]):
        shards[level, "attn"] = [qkv_weight[level], out_weight[level]]
        shards[level, "up"] = [up_weight[level]]
        shards[level, "down"] = [down_weight[level]]
    width = out_weight.shape[-1]
    plain = jnp.concatenate([jnp.arange(4), jnp.arange(4)]).astype(jnp.int32)
    rows = width // SLOTS
    runs = [[(c, side, 0, side, 0, 4) for side in range(4)] for c in range(4)]
    done = {}
    for key, parts in shards.items():
        whole = [lax.all_gather(part, "items", axis=0, tiled=True) for part in parts]
        if key[1] == "down":
            cut = whole[0].reshape(4, 4, 4, rows, width)
            arrays = [cut[:, :, c] for c in range(4)]
        else:
            joined = jnp.concatenate(whole, axis=1)
            arrays = [joined[:, width * c : width * (c + 1)] for c in range(4)]
            arrays = [array.reshape(4, 4, rows, width) for array in arrays]
        done[key] = Chunk(arrays, runs, plain)
    return done


def weight_shape(kind, width):
    rows = width // SLOTS
    return {
        "down": (4, 4, 4, rows, width),
        "up": (4, 4, 4, rows, width),
        "attn": (4, 4, 4, rows, width),
        "qkv": (3, 4, 4, rows, width),
        "out": (4, 4, rows, width),
    }[kind]


class Loads:
    def __init__(self, order, chunk, refs, kind, target, sems, first=0):
        self.order, self.chunk, self.refs, self.kind = order, chunk, refs, kind
        self.target, self.sems, self.first = target, sems, first

    def visit(self, act, only=None):
        number = self.first
        for quarter, runs in enumerate(self.chunk.runs):
            if only not in (None, quarter):
                number += len(runs)
                continue
            which = self.order[4 + quarter]

            def run(number=number, runs=runs, which=which):
                for n, (array, part, first, side, z, depth) in enumerate(runs):
                    source = self.refs[array].at[pl.ds(first, depth), part]
                    span, place = pl.ds(z, depth), self.order[side]
                    if self.kind == "down":
                        target = self.target.at[span, place, which]
                    elif self.kind == "out":
                        target = self.target.at[span, place]
                    else:
                        target = self.target.at[which, span, place]
                    act(pltpu.make_async_copy(source, target, self.sems.at[number + n]))

            if self.kind == "out":
                pl.when(which == 3)(run)
            elif self.kind == "qkv":
                pl.when(which != 3)(run)
            else:
                run()
            number += len(runs)

    def start(self):
        self.visit(lambda copy: copy.start())

    def wait(self, only=None):
        self.visit(lambda copy: copy.wait(), only)


def call(kernel, name, operands, outs, scratch, flops, transcendentals=0, far=()):
    moved = sum(a.size * a.dtype.itemsize for a, _ in operands)
    moved += sum(math.prod(s) * jnp.dtype(d).itemsize for s, d in outs)
    return pl.pallas_call(
        kernel,
        name=name,
        out_shape=[jax.ShapeDtypeStruct(s, d) for s, d in outs],
        in_specs=[spec for _, spec in operands],
        out_specs=[ANY if n in far else VMEM for n in range(len(outs))],
        scratch_shapes=scratch,
        compiler_params=pltpu.CompilerParams(vmem_limit_bytes=VMEM_BYTES),
        cost_estimate=pl.CostEstimate(
            flops=int(flops), bytes_accessed=int(moved), transcendentals=int(transcendentals)
        ),
    )(*[a for a, _ in operands])


def nt(left, right):
    return lax.dot_general(left, right, (((1,), (1,)), ((), ())), preferred_element_type=F32)


def tn(left, right):
    return lax.dot_general(left, right, (((0,), (0,)), ((), ())), preferred_element_type=F32)


def nn(left, right):
    return jnp.dot(left, right, preferred_element_type=F32)


def swap_cores(block):
    return lax.ppermute(block, "seq", [(0, 1), (1, 0)])


def tile_at(index, size=TILE):
    return pl.ds(pl.multiple_of(index * size, size), size)


def fold_rows(values):
    return jnp.sum(values.reshape(-1, 8, values.shape[-1]), axis=0)


def column_loop(width, body):
    for index in range(width // WIDE):
        body(pl.ds(index * WIDE, WIDE))


def matrix(weight, *index):
    blocks = weight[index] if index else weight[...]
    return blocks.reshape(-1, blocks.shape[-1])


def columns_of(weight, at, *index):
    rest = weight.ndim - len(index) - 1
    blocks = weight[(*index, *[slice(None)] * rest, at)]
    return blocks.reshape(-1, blocks.shape[-1])


def token_sums(values, counted=None):
    if counted is None:
        counted = jnp.ones((1, values.shape[1]), BF16)
    return nt(jnp.broadcast_to(counted, (8, values.shape[1])), values)[0:1]


def turn(source, target):
    for index in range(source.shape[1] // 128):
        span = pl.ds(index * 128, 128)
        target[span, :] = source[:, span].T


def normalize_strips(rows, source, gain, shift, unit, inverse, result):
    def strip(index, carry):
        at = tile_at(index, STRIP)
        values = source[at, :]
        center = values - jnp.mean(values, axis=-1, keepdims=True)
        spread = jnp.mean(center * center, axis=-1, keepdims=True)
        scale = lax.rsqrt(spread + ln_eps)
        normal = center * scale
        unit[at, :] = normal
        inverse[at, :] = jnp.broadcast_to(scale, (STRIP, inverse.shape[1]))
        result[at, :] = (normal * gain + shift).astype(BF16)
        return carry

    lax.fori_loop(0, rows // STRIP, strip, 0, unroll=4)


def attention_forward(place, state, state_other, chunk, bias_rows):
    rows, width = state.shape
    heads = width // HEAD_DIM
    arrays, count = len(chunk.arrays), chunk.count
    score_scale = 1.0 / math.sqrt(HEAD_DIM)

    def kernel(order, place_ref, state_ref, other_state, bias_ref, *refs):
        prob_hbm, result, unit_out, inverse_out, o_out, q_out, k_out, value = refs[
            arrays : arrays + 8
        ]
        prob_ref, query, key, mixed, total, unit, inverse, states, weight, sems, leave = refs[
            arrays + 8 :
        ]
        loads = Loads(order, chunk, refs[:arrays], "attn", weight, sems)
        loads.start()
        states[:rows, :] = state_ref[...]
        states[rows:, :] = other_state[...]
        spot = lax.broadcasted_iota(jnp.int32, (2 * rows, 1), 0)
        position = jnp.where(spot < rows, place_ref[1] + spot, place_ref[2] + spot - rows)
        live = position < place_ref[0]
        line = lax.broadcasted_iota(jnp.int32, (2 * HEAD_DIM, 1), 0)
        loads.wait()

        def project(at):
            query[:, at] = (
                nn(state_ref[...], columns_of(weight, at, 0)) + bias_ref[0:1, at]
            ).astype(BF16)
            key[:, at] = nn(states[...], columns_of(weight, at, 1)).astype(BF16)
            value[:, at] = (nn(states[...], columns_of(weight, at, 2)) + bias_ref[1:2, at]).astype(
                BF16
            )

        column_loop(width, project)
        turn(query, q_out)
        turn(key, k_out)

        spans = [slice(start, start + 128) for start in range(0, 2 * rows, 128)]

        def leaving(index):
            span = pl.ds(2 * index, 2)
            return pltpu.make_async_copy(prob_ref.at[span], prob_hbm.at[span], leave.at[index])

        def pair(index, carry):
            at = tile_at(index, 2 * HEAD_DIM)
            turned = value[:, at].T
            outs = []
            for side in range(2):
                mine = (line // HEAD_DIM == side).astype(F32) * score_scale
                asked = q_out[at, :] * mine.astype(BF16)
                blocks = [nn(key[span, at], asked) for span in spans]
                blocks = [jnp.where(live[s], b, masked_score) for s, b in zip(spans, blocks)]
                tops = [jnp.max(block, axis=0, keepdims=True) for block in blocks]
                top = functools.reduce(jnp.maximum, tops)
                blocks = [jnp.exp(block - top) for block in blocks]
                norm = sum(jnp.sum(block, axis=0, keepdims=True) for block in blocks)
                norm = 1.0 / norm
                weights = jnp.concatenate([(b * norm).astype(BF16) for b in blocks], axis=0)
                prob_ref[2 * index + side] = weights
                outs.append(nn(turned[HEAD_DIM * side : HEAD_DIM * (side + 1)], weights))
            outs = jnp.concatenate(outs, axis=0)
            o_out[at, :] = outs
            mixed[:, at] = outs.T.astype(BF16)
            leaving(index).start()
            return carry

        lax.fori_loop(0, heads // 2, pair, 0, unroll=4)

        def column(at):
            total[:, at] = (
                state_ref[:, at].astype(F32)
                + nn(mixed[...], columns_of(weight, at, 3))
                + bias_ref[2:3, at]
            )

        column_loop(width, column)
        normalize_strips(rows, total, bias_ref[10:11, :], bias_ref[3:4, :], unit, inverse, result)
        turn(unit, unit_out)
        inverse_out[...] = inverse[...].T[:8]
        for index in range(heads // 2):
            leaving(index).wait()

    return call(
        kernel,
        "attention_forward",
        [
            (chunk.order, SMEM),
            (place, SMEM),
            (state, VMEM),
            (state_other, VMEM),
            (bias_rows, VMEM),
        ]
        + [(a, ANY) for a in chunk.arrays],
        [
            ((heads, 2 * rows, rows), BF16),
            ((rows, width), BF16),
            ((width, rows), F32),
            ((8, rows), F32),
            ((width, rows), F32),
            ((width, rows), BF16),
            ((width, 2 * rows), BF16),
            ((2 * rows, width), BF16),
        ],
        [
            pltpu.VMEM((heads, 2 * rows, rows), BF16),
            pltpu.VMEM((rows, width), BF16),
            pltpu.VMEM((2 * rows, width), BF16),
            pltpu.VMEM((rows, width), BF16),
            pltpu.VMEM((rows, width), F32),
            pltpu.VMEM((rows, width), F32),
            pltpu.VMEM((rows, 128), F32),
            pltpu.VMEM((2 * rows, width), BF16),
            pltpu.VMEM(weight_shape("attn", width), BF16),
            pltpu.SemaphoreType.DMA((count,)),
            pltpu.SemaphoreType.DMA((heads // 2,)),
        ],
        2 * rows * width * width * 6 + 8 * rows * rows * width,
        heads * rows * rows * 2,
        far=(0,),
    )


def up_part(order, loads, normed_ref, bias_ref, weight, active, slope):
    width = normed_ref.shape[1]
    for quarter in range(4):
        which = order[4 + quarter]
        loads.wait(quarter)

        def column(index, carry, which=which):
            at = tile_at(index)
            there = pl.ds(pl.multiple_of(which * width + index * TILE, TILE), TILE)
            whole = nn(normed_ref[...], columns_of(weight, at, which))
            for start in range(0, whole.shape[0], 128):
                span = slice(start, start + 128)
                hidden = whole[span] + bias_ref[pl.ds(4 + which, 1), at]
                normal = 0.5 * (1.0 + lax.erf(hidden * (1.0 / math.sqrt(2.0))))
                density = jnp.exp(-0.5 * hidden * hidden) * (1.0 / math.sqrt(2.0 * math.pi))
                active[span, there] = (hidden * normal).astype(BF16)
                slope[there, span] = (normal + hidden * density).T
            return carry

        lax.fori_loop(0, width // TILE, column, 0, unroll=4)


def up_forward(normed, chunk, bias_rows):
    rows, width = normed.shape
    arrays, count = len(chunk.arrays), chunk.count
    hidden_width = 4 * width

    def kernel(order, normed_ref, bias_ref, *refs):
        active, slope, weight, sems = refs[arrays:]
        loads = Loads(order, chunk, refs[:arrays], "up", weight, sems)
        loads.start()
        up_part(order, loads, normed_ref, bias_ref, weight, active, slope)

    return call(
        kernel,
        "up_forward",
        [(chunk.order, SMEM), (normed, VMEM), (bias_rows, VMEM)] + [(a, ANY) for a in chunk.arrays],
        [((rows, hidden_width), BF16), ((hidden_width, rows), F32)],
        [pltpu.VMEM(weight_shape("up", width), BF16), pltpu.SemaphoreType.DMA((count,))],
        2 * rows * width * hidden_width,
        2 * rows * hidden_width,
    )


def down_part(
    normed_ref, active_ref, bias_ref, weight, total, unit, inverse, result, unit_out, inverse_out
):
    rows, width = normed_ref.shape

    def column(at):
        total[:, at] = (
            normed_ref[:, at].astype(F32)
            + nn(active_ref[...], columns_of(weight, at))
            + bias_ref[8:9, at]
        )

    column_loop(width, column)
    normalize_strips(rows, total, bias_ref[11:12, :], bias_ref[9:10, :], unit, inverse, result)
    turn(unit, unit_out)
    inverse_out[...] = inverse[...].T[:8]


def down_forward(normed, active, chunk, bias_rows):
    rows, width = normed.shape
    arrays, count = len(chunk.arrays), chunk.count

    def kernel(order, normed_ref, active_ref, bias_ref, *refs):
        result, unit_out, inverse_out, total, unit, inverse, weight, sems = refs[arrays:]
        loads = Loads(order, chunk, refs[:arrays], "down", weight, sems)
        loads.start()
        loads.wait()
        down_part(
            normed_ref,
            active_ref,
            bias_ref,
            weight,
            total,
            unit,
            inverse,
            result,
            unit_out,
            inverse_out,
        )

    return call(
        kernel,
        "down_forward",
        [(chunk.order, SMEM), (normed, VMEM), (active, VMEM), (bias_rows, VMEM)]
        + [(a, ANY) for a in chunk.arrays],
        [((rows, width), BF16), ((width, rows), F32), ((8, rows), F32)],
        [
            pltpu.VMEM((rows, width), F32),
            pltpu.VMEM((rows, width), F32),
            pltpu.VMEM((rows, 128), F32),
            pltpu.VMEM(weight_shape("down", width), BF16),
            pltpu.SemaphoreType.DMA((count,)),
        ],
        2 * rows * width * width * 4,
    )


def norm_backward(upstream, gain, unit, inverse, wide, narrow):
    width, rows = unit.shape
    strips = [pl.ds(index * 128, 128) for index in range(width // 128)]
    mean = jnp.zeros((8, rows), F32)
    lean = jnp.zeros((8, rows), F32)
    for at in strips:
        scaled = upstream(at) * gain(at)
        mean = mean + fold_rows(scaled)
        lean = lean + fold_rows(scaled * unit[at, :])
    mean = jnp.sum(mean, axis=0, keepdims=True) * (1.0 / width)
    lean = jnp.sum(lean, axis=0, keepdims=True) * (1.0 / width)
    for at in strips:
        below = inverse[0:1, :] * (upstream(at) * gain(at) - mean - unit[at, :] * lean)
        wide[at, :] = below
        narrow[at, :] = below.astype(BF16)


def through_qkv(order, loads, da, dq, own, received, weight, grads, total):
    width, rows = da.shape
    grads[0] = dq[...]
    for part in range(2):
        span = pl.ds(part * width, width)
        grads[1 + part] = (own[span, :].astype(F32) + received[span, :].astype(F32)).astype(BF16)
    total[...] = da[...]
    for quarter in range(4):
        which = order[4 + quarter]

        def add(quarter=quarter, which=which):
            loads.wait(quarter)
            for index in range(8):
                at = pl.ds(index * (width // 8), width // 8)
                half = slice(index % 2 * 2, index % 2 * 2 + 2)
                total[at, :] += nn(matrix(weight, which, index // 2, half), grads[which])

        pl.when(which != 3)(add)


def layer_backward(top, place, before, saved, chunks, columns, bias_rows, axes):
    queries, keys, values, prob, mixed = (saved[name] for name in ("q", "k", "v", "p", "o"))
    width, rows = queries.shape
    heads = width // HEAD_DIM
    hidden_width = 4 * width
    score_scale = 1.0 / math.sqrt(HEAD_DIM)
    used = [(chunks["down"], "down"), (chunks["up"], "up"), (chunks["attn"], "out")]
    if top:
        first = [before["normed"], before["cotangent"], bias_rows]
        slope = []
    else:
        used = [(before["chunk"], "qkv")] + used
        first = [*before["grads"], saved["unit2"], saved["inverse2"]]
        slope = [saved["slope"]]
    cutting = not top and axes is not None
    first += [columns, saved["unit1"], saved["inverse1"], mixed, queries, keys, values, prob]
    first += slope
    blocks = [a for chunk, _ in used for a in chunk.arrays]
    counts = [chunk.count for chunk, _ in used]
    fetched = [a.size * a.dtype.itemsize > 2**17 for a in first]

    def kernel(place_ref, *refs):
        refs = list(refs)

        def take(number):
            taken, refs[:] = refs[:number], refs[number:]
            return taken

        orders = take(len(used))
        given = take(len(first))
        sources = [take(len(chunk.arrays)) for chunk, _ in used]
        if cutting:
            (above_sums,) = take(1)
        if top:
            (state_out,) = take(1)
        targets = take(4)
        (sums,) = take(1)
        sent = take(1) if cutting else None
        weights = take(len(used))
        copies = []
        for number, far in enumerate(fetched):
            if far:
                (held,) = take(1)
                copies.append((given[number], held))
                given[number] = held
            else:
                copies.append(None)
        da, dq, kv_own, kv_other, wide, narrow, hidden, sems, extra, leave = take(10)
        loads = []
        for number, (chunk, kind) in enumerate(used):
            loads.append(
                Loads(
                    orders[number],
                    chunk,
                    sources[number],
                    kind,
                    weights[number],
                    sems,
                    sum(counts[:number]),
                )
            )
        copies = [
            pltpu.make_async_copy(*pair, extra.at[number]) if pair else None
            for number, pair in enumerate(copies)
        ]
        start = len(first) - 8 - len(slope)
        late = [start + 3, start + 4, start + 5, start + 6, start + 7]
        if top:
            stages = [([loads[1]], [0]), ([loads[0]], [1, start, start + 1]), ([loads[2]], late)]
        else:
            stages = [
                ([loads[0]], [0, 1, 2, 3]),
                ([loads[1]], [4, start, start + 8]),
                ([loads[2]], [start + 1]),
                ([loads[3]], late),
            ]
        stages = [
            [*weights_in, *[copies[n] for n in numbers if copies[n] is not None]]
            for weights_in, numbers in stages
        ]

        def begin(number):
            if number < len(stages):
                for item in stages[number]:
                    item.start()

        def finish(number, skipped=0):
            for item in stages[number][skipped:]:
                item.wait()
            begin(number + 2)

        begin(0)
        begin(1)
        down, up, out = weights[-3:]

        if top:
            normed_ref, cotangent_ref, bias_ref = given[:3]
            column_ref, unit1, inverse1, o_ref, q_ref, k_ref, v_ref, prob_ref = given[3:]
            slope_ref, active_ref, total, unit, inverse, unit2, inverse2 = take(7)
            finish(0, 1)
            up_part(orders[1], loads[1], normed_ref, bias_ref, up, active_ref, slope_ref)
            finish(1)
            down_part(
                normed_ref,
                active_ref,
                bias_ref,
                    down,
                total,
                unit,
                inverse,
                state_out,
                unit2,
                inverse2,
            )
            token = lax.broadcasted_iota(jnp.int32, (1, rows), 1) + place_ref[1]
            row_live = (token < place_ref[0]).astype(F32)

            def above_two(at):
                return cotangent_ref[at, :].astype(F32) * row_live

            sums[9:10, :] = token_sums(cotangent_ref[...], row_live.astype(BF16))
        else:
            da_above, dq_above, kv_above, kv_received, unit2, inverse2 = given[:6]
            column_ref, unit1, inverse1, o_ref, q_ref, k_ref, v_ref, prob_ref, slope_ref = given[6:]
            above_ref, both = take(2)
            finish(0, 1)
            through_qkv(
                orders[0],
                loads[0],
                da_above,
                dq_above,
                kv_above,
                kv_received,
                weights[0],
                both,
                wide,
            )
            above_ref[...] = wide[...].astype(BF16)
            finish(1)

            def above_two(at):
                return above_ref[at, :].astype(F32)

            sums[9:10, :] = token_sums(above_ref[...])

        norm_backward(above_two, lambda at: column_ref[at, 11:12], unit2, inverse2, wide, narrow)
        sums[8:9, :] = token_sums(narrow[...])
        piece = width // 8
        for part in range(4):
            for index in range(8):
                there = pl.ds(part * width + index * piece, piece)
                half = slice(index % 2 * 2, index % 2 * 2 + 2)
                grad = nn(matrix(down, part, index // 2, half), narrow[...])
                hidden[there, :] = (grad * slope_ref[there, :]).astype(BF16)
        for part in range(4):
            sums[4 + part : 5 + part, :] = token_sums(hidden[part * width : (part + 1) * width, :])
        if not top:
            finish(len(stages) - 2)
        for index in range(8):
            at = pl.ds(index * piece, piece)
            half = slice(index % 2 * 2, index % 2 * 2 + 2)
            rows_up = [matrix(up, part, index // 2, half) for part in range(4)]
            grad = wide[at, :] + nn(jnp.concatenate(rows_up, axis=1), hidden[...])
            wide[at, :] = grad
            narrow[at, :] = grad.astype(BF16)
        sums[3:4, :] = token_sums(narrow[...])
        norm_backward(
            lambda at: wide[at, :], lambda at: column_ref[at, 10:11], unit1, inverse1, da, narrow
        )
        leaving = [
            pltpu.make_async_copy(held, target, leave.at[n])
            for n, (held, target) in enumerate(zip((da, dq, kv_own, kv_other), targets))
        ]
        leaving[0].start()
        sums[2:3, :] = token_sums(narrow[...])
        finish(len(stages) - 1)
        mixed = hidden.at[pl.ds(0, width)]
        for index in range(8):
            half = slice(index % 2 * 2, index % 2 * 2 + 2)
            made = nn(matrix(out, index // 2, half), narrow[...])
            mixed[pl.ds(index * piece, piece), :] = made.astype(BF16)
        line = lax.broadcasted_iota(jnp.int32, (2 * HEAD_DIM, 1), 0)

        def pair(index, carry):
            at = tile_at(index, 2 * HEAD_DIM)
            grad_out = mixed[at, :]
            value = v_ref[:, at]
            for side in range(2):
                here = pl.ds(
                    pl.multiple_of(index * 2 * HEAD_DIM + side * HEAD_DIM, HEAD_DIM), HEAD_DIM
                )
                low = pl.ds(
                    pl.multiple_of(width + index * 2 * HEAD_DIM + side * HEAD_DIM, HEAD_DIM),
                    HEAD_DIM,
                )
                probs = prob_ref[2 * index + side]
                inner = jnp.sum(mixed[here, :].astype(F32) * o_ref[here, :], axis=0, keepdims=True)
                masked = grad_out * (line // HEAD_DIM == side).astype(F32).astype(BF16)
                grad_s = []
                for block in range(2 * rows // 128):
                    span = slice(block * 128, (block + 1) * 128)
                    grad_p = nn(value[span], masked)
                    grad_s.append((probs[span].astype(F32) * (grad_p - inner)).astype(BF16))
                grad_s = jnp.concatenate(grad_s, axis=0)
                dq[here, :] = (nn(k_ref[here, :], grad_s) * score_scale).astype(BF16)
                grad_k = (nt(q_ref[here, :], grad_s) * score_scale).astype(BF16)
                grad_v = nt(mixed[here, :], probs).astype(BF16)
                kv_own[here, :] = grad_k[:, :rows]
                kv_other[here, :] = grad_k[:, rows:]
                kv_own[low, :] = grad_v[:, :rows]
                kv_other[low, :] = grad_v[:, rows:]
            under = pl.ds(pl.multiple_of(width + index * 2 * HEAD_DIM, HEAD_DIM), 2 * HEAD_DIM)
            for n, held, spans in ((1, dq, (at,)), (2, kv_own, (at, under)), (3, kv_other, (at, under))):
                for span in spans:
                    pltpu.make_async_copy(held.at[span], targets[n].at[span], leave.at[n]).start()
            return carry

        lax.fori_loop(0, heads // 2, pair, 0, unroll=4)
        sums[0:1, :] = token_sums(dq[...])
        sums[1:2, :] = token_sums(kv_own[width:, :]) + token_sums(kv_other[width:, :])
        if cutting:
            cut_sums(sums, sent[0], 0, *axes)
            cut_sums(above_sums, sent[0], 1, *axes)
        for copy in leaving:
            copy.wait()

    outs = [((width, rows), F32), ((width, rows), BF16)]
    outs += [((2 * width, rows), BF16)] * 2 + [((16, width), F32)]
    scratch = [pltpu.VMEM(a.shape, a.dtype) for a, far in zip(first, fetched) if far]
    scratch += [pltpu.VMEM(*out) for out in outs[:4]]
    scratch += [
        pltpu.VMEM((width, rows), F32),
        pltpu.VMEM((width, rows), BF16),
        pltpu.VMEM((hidden_width, rows), BF16),
        pltpu.SemaphoreType.DMA((sum(counts),)),
        pltpu.SemaphoreType.DMA((len(first),)),
        pltpu.SemaphoreType.DMA((4,)),
    ]
    if cutting:
        outs += [((axes[0] * axes[1], 2, 10 * width // axes[0]), F32)]
    if top:
        outs = [((rows, width), BF16)] + outs
        scratch += [
            pltpu.VMEM((hidden_width, rows), F32),
            pltpu.VMEM((rows, hidden_width), BF16),
            pltpu.VMEM((rows, width), F32),
            pltpu.VMEM((rows, width), F32),
            pltpu.VMEM((rows, 128), F32),
            pltpu.VMEM((width, rows), F32),
            pltpu.VMEM((8, rows), F32),
        ]
    else:
        scratch += [pltpu.VMEM((width, rows), BF16), pltpu.VMEM((3, width, rows), BF16)]
    return call(
        kernel,
        "layer_backward",
        [(place, SMEM)]
        + [(chunk.order, SMEM) for chunk, _ in used]
        + [(a, ANY if far else VMEM) for a, far in zip(first, fetched)]
        + [(a, ANY) for a in blocks]
        + ([(before["sums"], VMEM)] if cutting else []),
        outs,
        [pltpu.VMEM(weight_shape(kind, width), BF16) for _, kind in used] + scratch,
        2 * rows * width * width * 13 + 16 * rows * rows * width,
        far=range(1, 5) if top else range(4),
    )


def qkv_backward(grads, chunk):
    width, rows = grads[0].shape
    arrays, count = len(chunk.arrays), chunk.count

    def kernel(order, da, dq, own, received, *refs):
        result, both, total, weight, sems = refs[arrays:]
        loads = Loads(order, chunk, refs[:arrays], "qkv", weight, sems)
        loads.start()
        through_qkv(order, loads, da, dq, own, received, weight, both, total)
        grad = total[...].astype(BF16)
        for index in range(width // 128):
            at = pl.ds(index * 128, 128)
            result[:, at] = grad[index * 128 : (index + 1) * 128].T

    return call(
        kernel,
        "qkv_backward",
        [(chunk.order, SMEM)] + [(g, VMEM) for g in grads] + [(a, ANY) for a in chunk.arrays],
        [((rows, width), BF16)],
        [
            pltpu.VMEM((3, width, rows), BF16),
            pltpu.VMEM((width, rows), F32),
            pltpu.VMEM(weight_shape("qkv", width), BF16),
            pltpu.SemaphoreType.DMA((count,)),
        ],
        2 * rows * width * width * 3,
    )[0]


def everywhere(values):
    total = lax.axis_size("items")
    return lax.all_to_all(jnp.broadcast_to(values, (total, *values.shape)), "items", 0, 0)


def in_rows(entries, cut):
    layers = entries.shape[0]
    grid = entries.reshape(layers, cut, 10)
    singles = jnp.concatenate([grid[..., :4], grid[..., 8:]], axis=2).swapaxes(1, 2)
    hidden = grid[..., 4:8].reshape(layers, -1)
    return jnp.concatenate([singles.reshape(layers, -1), hidden], axis=1)


SINGLES = (0, 1, 2, 3, 8, 9)


def bias_table(parts, norm_gain, width):
    total, layers, _ = parts.shape
    cut = width // total
    if total not in CHIPS:
        singles = parts[..., : 6 * cut].reshape(total, layers, 6, cut)
        singles = singles.transpose(1, 2, 0, 3).reshape(layers, 6, width)
        hidden = parts[..., 6 * cut :].swapaxes(0, 1).reshape(layers, 4, width)
        rows = jnp.concatenate([singles[:, :4], hidden, singles[:, 4:], norm_gain], axis=1)
        rows = jnp.pad(rows, ((0, 0), (0, 116), (0, 0)))
        return list(rows[:, :16]), list(rows.swapaxes(1, 2))

    def kernel(parts_ref, gain_ref, *refs):
        tables, columns, held = refs[:layers], refs[layers : 2 * layers], refs[-1]
        held[...] = jnp.zeros_like(held)
        for layer in range(layers):
            for item in range(total):
                for n, row in enumerate(SINGLES):
                    held[row : row + 1, item * cut : (item + 1) * cut] = parts_ref[
                        item, layer : layer + 1, n * cut : (n + 1) * cut
                    ]
                row, column = divmod(item * 4 * cut, width)
                held[4 + row : 5 + row, column : column + 4 * cut] = parts_ref[
                    item, layer : layer + 1, 6 * cut :
                ]
            held[10:12, :] = gain_ref[layer]
            tables[layer][...] = held[:16, :]
            turn(held, columns[layer])

    outs = call(
        kernel,
        "bias_table",
        [(parts, VMEM), (norm_gain, VMEM)],
        [((16, width), F32)] * layers + [((width, 128), F32)] * layers,
        [pltpu.VMEM((128, width), F32)],
        0,
    )
    return outs[:layers], outs[layers:]


def cut_sums(sums, sent, layer, total, cores):
    cut = sums.shape[1] // total
    for item in range(total):
        row, column = divmod(item * 4 * cut, sums.shape[1])
        for core in range(cores):
            for n, single in enumerate(SINGLES):
                sent[item * cores + core, layer : layer + 1, n * cut : (n + 1) * cut] = sums[
                    single : single + 1, item * cut : (item + 1) * cut
                ]
            sent[item * cores + core, layer : layer + 1, 6 * cut :] = sums[
                4 + row : 5 + row, column : column + 4 * cut
            ]


def bias_parts(sums, width):
    total = lax.axis_size("items")
    singles = jnp.concatenate([sums[:4], sums[8:10]], axis=0)
    singles = singles.reshape(6, total, width // total).swapaxes(0, 1).reshape(total, -1)
    return jnp.concatenate([singles, sums[4:8].reshape(total, -1)], axis=1)


def to_owners(parts):
    total, cores = lax.axis_size("items"), lax.axis_size("seq")
    sent = jnp.broadcast_to(parts.swapaxes(0, 1)[:, None], (total, cores, *parts.shape[::2]))
    return sent.reshape(total * cores, *parts.shape[::2])


def arrange_bias(owned, width):
    layers = owned.shape[0]
    cut = width // lax.axis_size("items")
    singles = owned[:, : 6 * cut].reshape(layers, 6, cut).swapaxes(1, 2)
    hidden = owned[:, 6 * cut :].reshape(layers, cut, 4)
    whole = jnp.concatenate([singles[..., :4], hidden, singles[..., 4:]], axis=2)
    return whole.reshape(layers, -1)


def on_device(
    tokens,
    lengths,
    cotangent,
    qkv_weight,
    out_weight,
    up_weight,
    down_weight,
    norm_gain,
    bias_master,
    first_moment,
    second_moment,
):
    item_count, part_len, width = tokens.shape
    levels = norm_gain.shape[0]
    rows = item_count * part_len
    core = lax.axis_index("seq")
    place = jnp.stack([lengths[0], core * part_len, (1 - core) * part_len]).astype(jnp.int32)
    turned = cotangent.reshape(rows, width).T

    chipped = lax.axis_size("items") in CHIPS
    if chipped:
        gather = Gather(qkv_weight, out_weight, up_weight, down_weight)
    else:
        plain = gather_plainly(qkv_weight, out_weight, up_weight, down_weight)
    state = tokens.reshape(rows, width)
    first = state
    if chipped:
        first, _ = lax.optimization_barrier((state, gather.mine[CHUNKS[0]]))
    state_other = swap_cores(first)
    if chipped:
        gather.computed.append(state_other)
    kept = [{} for _ in range(levels)]
    chunks = {}
    cycles = range(-1, 1 + max(KERNELS))
    for number, (action, level) in [(n, k) for n in cycles for k in (("", 0), *KERNELS.get(n, ()))]:
        if not action:
            if chipped:
                gather.cycle(number)
            if number == 0:
                master = in_rows(bias_master, bias_master.shape[1] // 10)
                if chipped:
                    master, _ = lax.optimization_barrier((master, gather.stages[0]["z"]))
                all_bias = everywhere(master)
                if chipped:
                    gather.computed.append(all_bias)
            if number == 1:
                bias_rows, columns = bias_table(all_bias, norm_gain, width)
                if chipped:
                    gather.computed += [*bias_rows, *columns, turned, place, gather.order]
            continue
        saved, bias = kept[level], bias_rows[level]
        kind = "attn" if action == "attention" else action
        chunk = gather.chunk((level, kind)) if chipped else plain[level, kind]
        chunks[level, kind] = chunk
        if action == "attention":
            (
                saved["p"],
                normed,
                saved["unit1"],
                saved["inverse1"],
                saved["o"],
                saved["q"],
                saved["k"],
                saved["v"],
            ) = attention_forward(place, state, state_other, chunk, bias)
            last = normed
        elif action == "up" and level < levels - 1:
            active, saved["slope"] = up_forward(normed, chunk, bias)
            last = active
        elif level < levels - 1:
            state, saved["unit2"], saved["inverse2"] = down_forward(
                normed, active, chunk, bias
            )
            last = state
            if chipped:
                stage = gather.stages[LAST - 1]
                waits = (stage["xy"], stage["yx"], gather.chunk((1, "attn")).arrays[-1])
                waits += (gather.swap_last(0, ()),)
                last, _ = lax.optimization_barrier((state, waits))
            last = state_other = swap_cores(last)
        if chipped:
            gather.computed.append(last)
            if (action, level) == ("down", 0):
                gather.swap_last(1, state_other)
                gather.swap_far(LAST - 1, state_other)
                gather.after = state_other
            if (action, level) == ("attention", 1):
                gather.swap_last(2, normed)

    axes = (lax.axis_size("items"), lax.axis_size("seq")) if chipped else None
    grads = [None] * levels
    for level in reversed(range(levels)):
        mine = {kind: chunks[level, kind] for kind in ("attn", "up", "down")}
        top = level == levels - 1
        if top:
            before = {"normed": normed, "cotangent": turned}
        else:
            before = {"grads": passed, "chunk": chunks[level + 1, "attn"], "sums": sums}
        outs = layer_backward(
            top,
            place,
            before,
            kept[level],
            mine,
            columns[level],
            bias_rows[level],
            axes,
        )
        if top:
            state, outs = outs[0], outs[1:]
        grad_sum, grad_q, kv_own, kv_other, sums = outs[:5]
        passed = [grad_sum, grad_q, kv_own, swap_cores(kv_other)]
        grads[level] = sums
    if chipped:
        sent = outs[5]
    else:
        sent = to_owners(jnp.stack([bias_parts(sums, width) for sums in grads]))
    layer_out = state.reshape(item_count, part_len, width)
    received = lax.all_to_all(sent, ("items", "seq"), 0, 0)
    input_grad = qkv_backward(passed, mine["attn"])
    received, _ = lax.optimization_barrier((received, input_grad))
    input_grad = input_grad.reshape(item_count, part_len, width)

    bias_grad = arrange_bias(jnp.sum(received, axis=0), width)
    new_first = beta_one * first_moment + (1.0 - beta_one) * bias_grad
    new_second = beta_two * second_moment + (1.0 - beta_two) * bias_grad * bias_grad
    first_hat = new_first / (1.0 - beta_one**STEP)
    second_hat = new_second / (1.0 - beta_two**STEP)
    new_bias = bias_master - learn_rate * first_hat / (jnp.sqrt(second_hat) + adam_eps)
    return (layer_out, input_grad, bias_grad, new_first, new_second, new_bias)


def solution(mesh):
    placed = (
        P("items", "seq", None),
        P("items"),
        P("items", "seq", None),
        P(None, "items", None),
        P(None, "items", None),
        P(None, "items", None),
        P(None, "items", None),
        P(),
        P(None, "items"),
        P(None, "items"),
        P(None, "items"),
    )
    return jax.shard_map(
        on_device,
        mesh=mesh,
        in_specs=placed,
        out_specs=(
            P("items", "seq", None),
            P("items", "seq", None),
            P(None, "items"),
            P(None, "items"),
            P(None, "items"),
            P(None, "items"),
        ),
        check_vma=False,
    )
```

```python
import functools
import math

import jax
import jax.numpy as jnp
from jax import lax
from jax.experimental import pallas as pl
from jax.experimental.pallas import tpu as pltpu
from jax.sharding import PartitionSpec as P

HEAD_DIM = 64
STEP = 10

ln_eps = 1e-12
beta_one = 0.9
beta_two = 0.999
adam_eps = 1e-08
learn_rate = 0.4
masked_score = -1000000000.0

CHIPS = {16: (4, 2, 2)}
CHUNKS = ((0, "attn"), (0, "up"), (0, "down"), (1, "attn"), (1, "up"), (1, "down"))
LAST = len(CHUNKS) - 1
KERNELS = {
    3: (("attention", 0),),
    4: (("up", 0),),
    5: (("down", 0), ("attention", 1)),
    6: (("up", 1), ("down", 1)),
}
SLOTS = 16
TILE = 256
STRIP = 32
F32 = jnp.float32
BF16 = jnp.bfloat16
VMEM_BYTES = 56 * 1024 * 1024

VMEM = pl.BlockSpec(memory_space=pltpu.VMEM)
SMEM = pl.BlockSpec(memory_space=pltpu.SMEM)
ANY = pl.BlockSpec(memory_space=pl.ANY)


def own_blocks(qkv_weight, out_weight, up_weight, down_weight):
    levels, rows, width = out_weight.shape
    keys = [(level, kind) for level in range(levels) for kind in ("attn", "up", "down")]
    core = lax.axis_index("seq").astype(jnp.int32).reshape(1)

    def kernel(core_ref, qkv, out, up, down, *refs):
        targets, (held, come, go) = refs[: len(keys)], refs[len(keys) :]
        here = core_ref[0]

        def copies(number, core):
            level, kind = keys[number]
            for half in range(2):
                if kind == "attn" and core == 0:
                    source = qkv.at[level, :, pl.ds(half * width, width)]
                elif kind == "attn":
                    source = out.at[level] if half else qkv.at[level, :, pl.ds(2 * width, width)]
                elif kind == "up":
                    column = pl.multiple_of((2 * here + half) * width, width)
                    source = up.at[level, :, pl.ds(column, width)]
                else:
                    row = pl.multiple_of((2 * here + half) * rows, rows)
                    source = down.at[level, pl.ds(row, rows), :]
                target = held.at[number, pl.ds(half * rows, rows), :]
                yield pltpu.make_async_copy(source, target, come.at[number, half])

        def each(act):
            for number, (_, kind) in enumerate(keys):
                if kind != "attn":
                    act(number, 0)
                    continue
                for side in range(2):
                    pl.when(here == side)(functools.partial(act, number, side))

        def begin(number, side):
            for copy in copies(number, side):
                copy.start()

        def finish(number, side):
            for copy in copies(number, side):
                copy.wait()

        each(begin)
        each(finish)
        leaving = [
            pltpu.make_async_copy(held.at[n], target, go.at[n]) for n, target in enumerate(targets)
        ]
        for copy in leaving:
            copy.start()
        for copy in leaving:
            copy.wait()

    blocks = pl.pallas_call(
        kernel,
        name="own_blocks",
        out_shape=[jax.ShapeDtypeStruct((2 * rows, width), BF16)] * len(keys),
        in_specs=[SMEM] + [ANY] * 4,
        out_specs=[ANY] * len(keys),
        scratch_shapes=[
            pltpu.VMEM((len(keys), 2 * rows, width), BF16),
            pltpu.SemaphoreType.DMA((len(keys), 2)),
            pltpu.SemaphoreType.DMA((len(keys),)),
        ],
        compiler_params=pltpu.CompilerParams(vmem_limit_bytes=VMEM_BYTES),
        cost_estimate=pl.CostEstimate(
            flops=0, bytes_accessed=8 * rows * width * len(keys), transcendentals=0
        ),
    )(core, qkv_weight, out_weight, up_weight, down_weight)
    return dict(zip(keys, blocks))


class Chunk:
    def __init__(self, arrays, runs, order):
        self.arrays, self.runs, self.order = arrays, runs, order
        self.count = sum(len(quarter) for quarter in runs)


def join(blocks, places=None):
    width = blocks[0].shape[1]
    total = sum(block.shape[0] for block in blocks)
    starts = [sum(block.shape[0] for block in blocks[:n]) for n in range(len(blocks))]
    table = [] if places is None else [places]

    def kernel(*refs):
        table_ref, refs = refs[: len(table)], refs[len(table) :]
        sources, (target, held, come, go) = refs[: len(blocks)], refs[len(blocks) :]
        ins, outs = [], []
        for n, (source, start) in enumerate(zip(sources, starts)):
            rows = blocks[n].shape[0]
            span = there = pl.ds(start, rows)
            if table:
                there = pl.ds(pl.multiple_of(table_ref[0][n] * rows, rows), rows)
            ins.append(pltpu.make_async_copy(source, held.at[span], come.at[n]))
            outs.append(pltpu.make_async_copy(held.at[span], target.at[there], go.at[n]))
            ins[-1].start()
        for come_in, go_out in zip(ins, outs):
            come_in.wait()
            go_out.start()
        for go_out in outs:
            go_out.wait()

    return pl.pallas_call(
        kernel,
        name="join",
        out_shape=jax.ShapeDtypeStruct((total, width), BF16),
        in_specs=[SMEM] * len(table) + [ANY] * len(blocks),
        out_specs=ANY,
        scratch_shapes=[
            pltpu.VMEM((total, width), BF16),
            pltpu.SemaphoreType.DMA((len(blocks),)),
            pltpu.SemaphoreType.DMA((len(blocks),)),
        ],
        compiler_params=pltpu.CompilerParams(vmem_limit_bytes=VMEM_BYTES),
        cost_estimate=pl.CostEstimate(
            flops=0, bytes_accessed=4 * total * width, transcendentals=0
        ),
    )(*table, *blocks)


class Gather:
    def __init__(self, *weights):
        self.total = lax.axis_size("items")
        self.depth, _, _ = CHIPS[self.total]
        self.plane = self.total // self.depth
        self.rows = weights[1].shape[1]
        self.mine = own_blocks(*weights)
        here = lax.axis_index("items") % self.plane
        core = lax.axis_index("seq")
        order = [here ^ side for side in range(4)]
        order += [core * 2, core * 2 + 1, 2 - core * 2, 3 - core * 2]
        self.order = jnp.stack(order).astype(jnp.int32)
        self.stages = [{} for _ in CHUNKS]
        self.last, self.computed = [], []

    def over_z(self, block):
        lines = [
            [place + self.plane * z for z in range(self.depth)] for place in range(self.plane)
        ]
        return lax.all_gather(block, "items", axis=0, tiled=True, axis_index_groups=lines)

    def step_z(self, block, step):
        pairs = [(item, (item + step * self.plane) % self.total) for item in range(self.total)]
        return lax.ppermute(block, "items", pairs)

    def line_of(self, parts):
        here = lax.axis_index("items") // self.plane
        places = [(here - step + self.depth) % self.depth for step in range(self.depth)]
        return join(parts, jnp.stack(places).astype(jnp.int32))

    def over(self, bit, block):
        return lax.ppermute(block, "items", [(item, item ^ bit) for item in range(self.total)])

    def across(self, x, y):
        half = x.shape[0] // 2
        return self.over(2, x[:half]), self.over(1, y[half:])

    def joined(self, stage):
        return join([stage[name] for name in ("z", "x", "y", "xy", "yx")])

    def cycle(self, number):
        wanted = {}
        if number == 0:
            wanted["corner"] = self.stages[LAST]["sides"][1:]
        if number == 1:
            wanted["sides"] = self.stages[LAST]["sides"]
        if 0 <= number < LAST - 1:
            wanted["block"] = self.mine[CHUNKS[number + 1]]
        if number == -1:
            wanted["first"] = self.mine[CHUNKS[0]]
            wanted["plane"] = self.mine[CHUNKS[LAST]]
        if LAST - 1 <= number <= LAST:
            wanted["line"] = self.stages[LAST]["lines"][number - LAST + 1]
        for lag in range(4):
            if 0 <= number - lag < LAST:
                wanted["lag%d" % lag] = self.stages[number - lag]
        def put(stage, name, value):
            stage[name] = value
            self.last.append(value)

        if 0 <= number <= LAST:
            self.before = self.last + self.computed
            wanted, _ = lax.optimization_barrier((wanted, self.before))
            self.last, self.computed = [], []
        elif number == -1:
            first = wanted["first"]
            steps = [self.step_z(first, step) for step in range(1, self.depth)]
            put(self.stages[0], "z", self.line_of([first, *steps]))

        if "lag3" in wanted:
            stage = self.stages[number - 3]
            if "joined" not in stage:
                put(stage, "joined", self.joined(wanted["lag3"]))
                wanted["lag3"] = stage
            put(stage, "other", swap_cores(wanted["lag3"]["joined"]))
        if "lag0" in wanted:
            along, stage = wanted["lag0"]["z"], self.stages[number]
            put(stage, "x", self.over(1, along))
            put(stage, "y", self.over(2, along))
        if "lag1" in wanted:
            held, stage = wanted["lag1"], self.stages[number - 1]
            stage["xy"], stage["yx"] = self.across(held["x"], held["y"])
            self.last += [stage["xy"], stage["yx"]]
        if "lag2" in wanted and number < LAST:
            put(self.stages[number - 2], "joined", self.joined(wanted["lag2"]))
        if "block" in wanted:
            put(self.stages[number + 1], "z", self.over_z(wanted["block"]))
        stage = self.stages[LAST]
        if LAST - 1 <= number <= LAST:
            stage.setdefault("z", []).append(self.over_z(wanted["line"]))
            if number < LAST:
                self.last.append(stage["z"][-1])
        if "plane" in wanted:
            own = wanted["plane"]
            x, y = self.over(1, own), self.over(2, own)
            stage["sides"] = [own, x, y]
            self.last += [x, y]
        if number == 0:
            x, y = wanted["corner"]
            stage["sides"] += self.across(x, y)
            self.last += stage["sides"][3:]
        if number == 1:
            _, x, y, xy, yx = wanted["sides"]
            stage["lines"] = [join([x, y[: self.rows]]), join([y[self.rows :], xy, yx])]
            self.last += stage["lines"]
        if 0 <= number < self.depth - 1:
            stage.setdefault("steps", [stage["sides"][0]])
            own, _ = lax.optimization_barrier((stage["steps"][0], self.before))
            stage["steps"].append(self.step_z(own, number + 1))
            self.last.append(stage["steps"][-1])
        if number == self.depth - 1:
            stage["z"] = [self.line_of(stage["steps"])]
            self.last.append(stage["z"][0])
    def swap_far(self, number, after):
        stage = self.stages[number]
        far, _ = lax.optimization_barrier(((stage["xy"], stage["yx"]), after))
        stage["xy2"], stage["yx2"] = [swap_cores(part) for part in far]
        return stage["xy2"], stage["yx2"]

    def swap_last(self, number, after):
        stage = self.stages[LAST]
        block, _ = lax.optimization_barrier((stage["z"][number], after))
        stage.setdefault("z2", []).append(swap_cores(block))
        return stage["z2"][-1]

    def chunk(self, key):
        number = CHUNKS.index(key)
        stage = self.stages[number]
        order = self.order
        if number == LAST:
            arrays = stage["z"] + stage["z2"]
            arrays = [a.reshape(self.depth, -1, self.rows, a.shape[1]) for a in arrays]
            spots = [(0, 0), (0, 1)] + [(1, n) for n in range(3)] + [(2, n) for n in range(3)]
            runs = [
                [
                    (array + spots[2 * side + part][0], spots[2 * side + part][1], 0, side, 0, self.depth)
                    for side in range(4)
                ]
                for array in (0, 3)
                for part in range(2)
            ]
            return Chunk(arrays, runs, order)
        half = self.depth // 2
        places = [(0, 0, self.depth), (1, 0, self.depth), (2, 0, self.depth)]
        places += [(3, 0, half), (3, half, self.depth - half)]
        own = [(n, 0, *place) for n, place in enumerate(places)]
        block = 2 * self.rows
        first = [0, self.depth, 2 * self.depth, 3 * self.depth, 3 * self.depth + half]
        other = [(5, *pair) for pair in ((first[n], *places[n]) for n in range(5))]
        names = ["z", "x", "y", "xy", "yx", "other"]
        if number == LAST - 1:
            late, _ = lax.optimization_barrier(
                (join([stage[name] for name in names[:3]]), self.after)
            )
            stage["other"] = swap_cores(late)
            other[3:] = [(6, 0, *places[3]), (7, 0, *places[4])]
            names += ["xy2", "yx2"]
        elif "other" not in stage:
            stage["other"] = swap_cores(self.joined(stage))
        arrays = [stage[name] for name in names]
        runs = [
            [(array, part, first, side, z, number) for array, first, side, z, number in spans]
            for spans in (own, other)
            for part in range(2)
        ]
        arrays = [a.reshape(a.shape[0] // block, 2, self.rows, a.shape[1]) for a in arrays]
        return Chunk(arrays, runs, order)


def gather_plainly(qkv_weight, out_weight, up_weight, down_weight):
    shards = {}
    for level in range(out_weight.shape[0]):
        shards[level, "attn"] = [qkv_weight[level], out_weight[level]]
        shards[level, "up"] = [up_weight[level]]
        shards[level, "down"] = [down_weight[level]]
    width = out_weight.shape[-1]
    plain = jnp.concatenate([jnp.arange(4), jnp.arange(4)]).astype(jnp.int32)
    rows = width // SLOTS
    runs = [[(c, side, 0, side, 0, 4) for side in range(4)] for c in range(4)]
    done = {}
    for key, parts in shards.items():
        whole = [lax.all_gather(part, "items", axis=0, tiled=True) for part in parts]
        if key[1] == "down":
            cut = whole[0].reshape(4, 4, 4, rows, width)
            arrays = [cut[:, :, c] for c in range(4)]
        else:
            joined = jnp.concatenate(whole, axis=1)
            arrays = [joined[:, width * c : width * (c + 1)] for c in range(4)]
            arrays = [array.reshape(4, 4, rows, width) for array in arrays]
        done[key] = Chunk(arrays, runs, plain)
    return done


def weight_shape(kind, width):
    rows = width // SLOTS
    return {
        "down": (4, 4, 4, rows, width),
        "up": (4, 4, 4, rows, width),
        "attn": (4, 4, 4, rows, width),
        "qkv": (3, 4, 4, rows, width),
        "out": (4, 4, rows, width),
    }[kind]


class Loads:
    def __init__(self, order, chunk, refs, kind, target, sems, first=0):
        self.order, self.chunk, self.refs, self.kind = order, chunk, refs, kind
        self.target, self.sems, self.first = target, sems, first

    def visit(self, act, only=None):
        number = self.first
        for quarter, runs in enumerate(self.chunk.runs):
            if only not in (None, quarter):
                number += len(runs)
                continue
            which = self.order[4 + quarter]

            def run(number=number, runs=runs, which=which):
                for n, (array, part, first, side, z, depth) in enumerate(runs):
                    source = self.refs[array].at[pl.ds(first, depth), part]
                    span, place = pl.ds(z, depth), self.order[side]
                    if self.kind == "down":
                        target = self.target.at[span, place, which]
                    elif self.kind == "out":
                        target = self.target.at[span, place]
                    else:
                        target = self.target.at[which, span, place]
                    act(pltpu.make_async_copy(source, target, self.sems.at[number + n]))

            if self.kind == "out":
                pl.when(which == 3)(run)
            elif self.kind == "qkv":
                pl.when(which != 3)(run)
            else:
                run()
            number += len(runs)

    def start(self):
        self.visit(lambda copy: copy.start())

    def wait(self, only=None):
        self.visit(lambda copy: copy.wait(), only)


def call(kernel, name, operands, outs, scratch, flops, transcendentals=0, far=()):
    moved = sum(a.size * a.dtype.itemsize for a, _ in operands)
    moved += sum(math.prod(s) * jnp.dtype(d).itemsize for s, d in outs)
    return pl.pallas_call(
        kernel,
        name=name,
        out_shape=[jax.ShapeDtypeStruct(s, d) for s, d in outs],
        in_specs=[spec for _, spec in operands],
        out_specs=[ANY if n in far else VMEM for n in range(len(outs))],
        scratch_shapes=scratch,
        compiler_params=pltpu.CompilerParams(vmem_limit_bytes=VMEM_BYTES),
        cost_estimate=pl.CostEstimate(
            flops=int(flops), bytes_accessed=int(moved), transcendentals=int(transcendentals)
        ),
    )(*[a for a, _ in operands])


def nt(left, right):
    return lax.dot_general(left, right, (((1,), (1,)), ((), ())), preferred_element_type=F32)


def tn(left, right):
    return lax.dot_general(left, right, (((0,), (0,)), ((), ())), preferred_element_type=F32)


def nn(left, right):
    return jnp.dot(left, right, preferred_element_type=F32)


def swap_cores(block):
    return lax.ppermute(block, "seq", [(0, 1), (1, 0)])


def tile_at(index, size=TILE):
    return pl.ds(pl.multiple_of(index * size, size), size)


def fold_rows(values):
    return jnp.sum(values.reshape(-1, 8, values.shape[-1]), axis=0)


def column_loop(width, body):
    for index in range(width // TILE):
        body(pl.ds(index * TILE, TILE))


def matrix(weight, *index):
    blocks = weight[index] if index else weight[...]
    return blocks.reshape(-1, blocks.shape[-1])


def columns_of(weight, at, *index):
    rest = weight.ndim - len(index) - 1
    blocks = weight[(*index, *[slice(None)] * rest, at)]
    return blocks.reshape(-1, blocks.shape[-1])


def token_sums(values, counted=None):
    if counted is None:
        counted = jnp.ones((1, values.shape[1]), BF16)
    return nt(jnp.broadcast_to(counted, (8, values.shape[1])), values)[0:1]


def turn(source, target):
    for index in range(source.shape[1] // 128):
        span = pl.ds(index * 128, 128)
        target[span, :] = source[:, span].T


def normalize_strips(rows, source, gain, shift, unit, inverse, result):
    def strip(index, carry):
        at = tile_at(index, STRIP)
        values = source[at, :]
        center = values - jnp.mean(values, axis=-1, keepdims=True)
        spread = jnp.mean(center * center, axis=-1, keepdims=True)
        scale = lax.rsqrt(spread + ln_eps)
        normal = center * scale
        unit[at, :] = normal
        inverse[at, :] = jnp.broadcast_to(scale, (STRIP, inverse.shape[1]))
        result[at, :] = (normal * gain + shift).astype(BF16)
        return carry

    lax.fori_loop(0, rows // STRIP, strip, 0, unroll=4)


def attention_forward(place, state, state_other, chunk, bias_rows):
    rows, width = state.shape
    heads = width // HEAD_DIM
    arrays, count = len(chunk.arrays), chunk.count
    score_scale = 1.0 / math.sqrt(HEAD_DIM)

    def kernel(order, place_ref, state_ref, other_state, bias_ref, *refs):
        prob_hbm, result, unit_out, inverse_out, o_out, q_out, k_out, value = refs[
            arrays : arrays + 8
        ]
        prob_ref, query, key, mixed, total, unit, inverse, states, weight, sems, leave = refs[
            arrays + 8 :
        ]
        loads = Loads(order, chunk, refs[:arrays], "attn", weight, sems)
        loads.start()
        states[:rows, :] = state_ref[...]
        states[rows:, :] = other_state[...]
        spot = lax.broadcasted_iota(jnp.int32, (2 * rows, 1), 0)
        position = jnp.where(spot < rows, place_ref[1] + spot, place_ref[2] + spot - rows)
        live = position < place_ref[0]
        line = lax.broadcasted_iota(jnp.int32, (2 * HEAD_DIM, 1), 0)
        loads.wait()

        def project(at):
            query[:, at] = (
                nn(state_ref[...], columns_of(weight, at, 0)) + bias_ref[0:1, at]
            ).astype(BF16)
            for start in range(0, 2 * rows, TILE):
                span = slice(start, start + TILE)
                key[span, at] = nn(states[span, :], columns_of(weight, at, 1)).astype(BF16)
                value[span, at] = (
                    nn(states[span, :], columns_of(weight, at, 2)) + bias_ref[1:2, at]
                ).astype(BF16)

        column_loop(width, project)
        turn(query, q_out)
        turn(key, k_out)

        spans = [slice(start, start + 128) for start in range(0, 2 * rows, 128)]

        def leaving(index):
            span = pl.ds(2 * index, 2)
            return pltpu.make_async_copy(prob_ref.at[span], prob_hbm.at[span], leave.at[index])

        def pair(index, carry):
            at = tile_at(index, 2 * HEAD_DIM)
            turned = value[:, at].T
            outs = []
            for side in range(2):
                mine = (line // HEAD_DIM == side).astype(F32) * score_scale
                asked = q_out[at, :] * mine.astype(BF16)
                blocks = [nn(key[span, at], asked) for span in spans]
                blocks = [jnp.where(live[s], b, masked_score) for s, b in zip(spans, blocks)]
                tops = [jnp.max(block, axis=0, keepdims=True) for block in blocks]
                top = functools.reduce(jnp.maximum, tops)
                blocks = [jnp.exp(block - top) for block in blocks]
                norm = sum(jnp.sum(block, axis=0, keepdims=True) for block in blocks)
                norm = 1.0 / norm
                weights = jnp.concatenate([(b * norm).astype(BF16) for b in blocks], axis=0)
                prob_ref[2 * index + side] = weights
                outs.append(nn(turned[HEAD_DIM * side : HEAD_DIM * (side + 1)], weights))
            outs = jnp.concatenate(outs, axis=0)
            o_out[at, :] = outs
            mixed[:, at] = outs.T.astype(BF16)
            leaving(index).start()
            return carry

        lax.fori_loop(0, heads // 2, pair, 0, unroll=4)

        def column(at):
            total[:, at] = (
                state_ref[:, at].astype(F32)
                + nn(mixed[...], columns_of(weight, at, 3))
                + bias_ref[2:3, at]
            )

        column_loop(width, column)
        normalize_strips(rows, total, bias_ref[10:11, :], bias_ref[3:4, :], unit, inverse, result)
        turn(unit, unit_out)
        inverse_out[...] = inverse[...].T[:8]
        for index in range(heads // 2):
            leaving(index).wait()

    return call(
        kernel,
        "attention_forward",
        [
            (chunk.order, SMEM),
            (place, SMEM),
            (state, VMEM),
            (state_other, VMEM),
            (bias_rows, VMEM),
        ]
        + [(a, ANY) for a in chunk.arrays],
        [
            ((heads, 2 * rows, rows), BF16),
            ((rows, width), BF16),
            ((width, rows), F32),
            ((8, rows), F32),
            ((width, rows), F32),
            ((width, rows), BF16),
            ((width, 2 * rows), BF16),
            ((2 * rows, width), BF16),
        ],
        [
            pltpu.VMEM((heads, 2 * rows, rows), BF16),
            pltpu.VMEM((rows, width), BF16),
            pltpu.VMEM((2 * rows, width), BF16),
            pltpu.VMEM((rows, width), BF16),
            pltpu.VMEM((rows, width), F32),
            pltpu.VMEM((rows, width), F32),
            pltpu.VMEM((rows, 128), F32),
            pltpu.VMEM((2 * rows, width), BF16),
            pltpu.VMEM(weight_shape("attn", width), BF16),
            pltpu.SemaphoreType.DMA((count,)),
            pltpu.SemaphoreType.DMA((heads // 2,)),
        ],
        2 * rows * width * width * 6 + 8 * rows * rows * width,
        heads * rows * rows * 2,
        far=(0,),
    )


def up_part(order, loads, normed_ref, bias_ref, weight, active, slope):
    width = normed_ref.shape[1]
    for quarter in range(4):
        which = order[4 + quarter]
        loads.wait(quarter)

        def column(index, carry, which=which):
            at = tile_at(index)
            there = pl.ds(pl.multiple_of(which * width + index * TILE, TILE), TILE)
            whole = nn(normed_ref[...], columns_of(weight, at, which))
            for start in range(0, whole.shape[0], 128):
                span = slice(start, start + 128)
                hidden = whole[span] + bias_ref[pl.ds(4 + which, 1), at]
                normal = 0.5 * (1.0 + lax.erf(hidden * (1.0 / math.sqrt(2.0))))
                density = jnp.exp(-0.5 * hidden * hidden) * (1.0 / math.sqrt(2.0 * math.pi))
                active[span, there] = (hidden * normal).astype(BF16)
                slope[there, span] = (normal + hidden * density).T
            return carry

        lax.fori_loop(0, width // TILE, column, 0, unroll=4)


def up_forward(normed, chunk, bias_rows):
    rows, width = normed.shape
    arrays, count = len(chunk.arrays), chunk.count
    hidden_width = 4 * width

    def kernel(order, normed_ref, bias_ref, *refs):
        active, slope, weight, sems = refs[arrays:]
        loads = Loads(order, chunk, refs[:arrays], "up", weight, sems)
        loads.start()
        up_part(order, loads, normed_ref, bias_ref, weight, active, slope)

    return call(
        kernel,
        "up_forward",
        [(chunk.order, SMEM), (normed, VMEM), (bias_rows, VMEM)] + [(a, ANY) for a in chunk.arrays],
        [((rows, hidden_width), BF16), ((hidden_width, rows), F32)],
        [pltpu.VMEM(weight_shape("up", width), BF16), pltpu.SemaphoreType.DMA((count,))],
        2 * rows * width * hidden_width,
        2 * rows * hidden_width,
    )


def down_part(
    normed_ref, active_ref, bias_ref, weight, total, unit, inverse, result, unit_out, inverse_out
):
    rows, width = normed_ref.shape

    def column(at):
        total[:, at] = (
            normed_ref[:, at].astype(F32)
            + nn(active_ref[...], columns_of(weight, at))
            + bias_ref[8:9, at]
        )

    column_loop(width, column)
    normalize_strips(rows, total, bias_ref[11:12, :], bias_ref[9:10, :], unit, inverse, result)
    turn(unit, unit_out)
    inverse_out[...] = inverse[...].T[:8]


def down_forward(normed, active, chunk, bias_rows):
    rows, width = normed.shape
    arrays, count = len(chunk.arrays), chunk.count

    def kernel(order, normed_ref, active_ref, bias_ref, *refs):
        result, unit_out, inverse_out, total, unit, inverse, weight, sems = refs[arrays:]
        loads = Loads(order, chunk, refs[:arrays], "down", weight, sems)
        loads.start()
        loads.wait()
        down_part(
            normed_ref,
            active_ref,
            bias_ref,
            weight,
            total,
            unit,
            inverse,
            result,
            unit_out,
            inverse_out,
        )

    return call(
        kernel,
        "down_forward",
        [(chunk.order, SMEM), (normed, VMEM), (active, VMEM), (bias_rows, VMEM)]
        + [(a, ANY) for a in chunk.arrays],
        [((rows, width), BF16), ((width, rows), F32), ((8, rows), F32)],
        [
            pltpu.VMEM((rows, width), F32),
            pltpu.VMEM((rows, width), F32),
            pltpu.VMEM((rows, 128), F32),
            pltpu.VMEM(weight_shape("down", width), BF16),
            pltpu.SemaphoreType.DMA((count,)),
        ],
        2 * rows * width * width * 4,
    )


def norm_backward(upstream, gain, unit, inverse, wide, narrow):
    width, rows = unit.shape
    strips = [pl.ds(index * 128, 128) for index in range(width // 128)]
    mean = jnp.zeros((8, rows), F32)
    lean = jnp.zeros((8, rows), F32)
    for at in strips:
        scaled = upstream(at) * gain(at)
        mean = mean + fold_rows(scaled)
        lean = lean + fold_rows(scaled * unit[at, :])
    mean = jnp.sum(mean, axis=0, keepdims=True) * (1.0 / width)
    lean = jnp.sum(lean, axis=0, keepdims=True) * (1.0 / width)
    for at in strips:
        below = inverse[0:1, :] * (upstream(at) * gain(at) - mean - unit[at, :] * lean)
        wide[at, :] = below
        narrow[at, :] = below.astype(BF16)


def through_qkv(order, loads, da, dq, own, received, weight, grads, total):
    width, rows = da.shape
    grads[0] = dq[...]
    for part in range(2):
        span = pl.ds(part * width, width)
        grads[1 + part] = (own[span, :].astype(F32) + received[span, :].astype(F32)).astype(BF16)
    total[...] = da[...]
    for quarter in range(4):
        which = order[4 + quarter]

        def add(quarter=quarter, which=which):
            loads.wait(quarter)
            for index in range(8):
                at = pl.ds(index * (width // 8), width // 8)
                half = slice(index % 2 * 2, index % 2 * 2 + 2)
                total[at, :] += nn(matrix(weight, which, index // 2, half), grads[which])

        pl.when(which != 3)(add)


def layer_backward(top, place, before, saved, chunks, columns, bias_rows, axes):
    queries, keys, values, prob, mixed = (saved[name] for name in ("q", "k", "v", "p", "o"))
    width, rows = queries.shape
    heads = width // HEAD_DIM
    hidden_width = 4 * width
    score_scale = 1.0 / math.sqrt(HEAD_DIM)
    used = [(chunks["down"], "down"), (chunks["up"], "up"), (chunks["attn"], "out")]
    if top:
        first = [before["normed"], before["cotangent"], bias_rows]
        slope = []
    else:
        used = [(before["chunk"], "qkv")] + used
        first = [*before["grads"], saved["unit2"], saved["inverse2"]]
        slope = [saved["slope"]]
    cutting = not top and axes is not None
    first += [columns, saved["unit1"], saved["inverse1"], mixed, queries, keys, values, prob]
    first += slope
    blocks = [a for chunk, _ in used for a in chunk.arrays]
    counts = [chunk.count for chunk, _ in used]
    fetched = [a.size * a.dtype.itemsize > 2**17 for a in first]

    def kernel(place_ref, *refs):
        refs = list(refs)

        def take(number):
            taken, refs[:] = refs[:number], refs[number:]
            return taken

        orders = take(len(used))
        given = take(len(first))
        sources = [take(len(chunk.arrays)) for chunk, _ in used]
        if cutting:
            (above_sums,) = take(1)
        if top:
            (state_out,) = take(1)
        targets = take(4)
        (sums,) = take(1)
        sent = take(1) if cutting else None
        weights = take(len(used))
        copies = []
        for number, far in enumerate(fetched):
            if far:
                (held,) = take(1)
                copies.append((given[number], held))
                given[number] = held
            else:
                copies.append(None)
        da, dq, kv_own, kv_other, wide, narrow, hidden, sems, extra, leave = take(10)
        loads = []
        for number, (chunk, kind) in enumerate(used):
            loads.append(
                Loads(
                    orders[number],
                    chunk,
                    sources[number],
                    kind,
                    weights[number],
                    sems,
                    sum(counts[:number]),
                )
            )
        copies = [
            pltpu.make_async_copy(*pair, extra.at[number]) if pair else None
            for number, pair in enumerate(copies)
        ]
        start = len(first) - 8 - len(slope)
        late = [start + 3, start + 4, start + 5, start + 6, start + 7]
        if top:
            stages = [([loads[1]], [0]), ([loads[0]], [1, start, start + 1]), ([loads[2]], late)]
        else:
            stages = [
                ([loads[0]], [0, 1, 2, 3]),
                ([loads[1]], [4, start, start + 8]),
                ([loads[2]], [start + 1]),
                ([loads[3]], late),
            ]
        stages = [
            [*weights_in, *[copies[n] for n in numbers if copies[n] is not None]]
            for weights_in, numbers in stages
        ]

        def begin(number):
            if number < len(stages):
                for item in stages[number]:
                    item.start()

        def finish(number, skipped=0):
            for item in stages[number][skipped:]:
                item.wait()
            begin(number + 2)

        begin(0)
        begin(1)
        down, up, out = weights[-3:]

        if top:
            normed_ref, cotangent_ref, bias_ref = given[:3]
            column_ref, unit1, inverse1, o_ref, q_ref, k_ref, v_ref, prob_ref = given[3:]
            slope_ref, active_ref, total, unit, inverse, unit2, inverse2 = take(7)
            finish(0, 1)
            up_part(orders[1], loads[1], normed_ref, bias_ref, up, active_ref, slope_ref)
            finish(1)
            down_part(
                normed_ref,
                active_ref,
                bias_ref,
                    down,
                total,
                unit,
                inverse,
                state_out,
                unit2,
                inverse2,
            )
            token = lax.broadcasted_iota(jnp.int32, (1, rows), 1) + place_ref[1]
            row_live = (token < place_ref[0]).astype(F32)

            def above_two(at):
                return cotangent_ref[at, :].astype(F32) * row_live

            sums[9:10, :] = token_sums(cotangent_ref[...], row_live.astype(BF16))
        else:
            da_above, dq_above, kv_above, kv_received, unit2, inverse2 = given[:6]
            column_ref, unit1, inverse1, o_ref, q_ref, k_ref, v_ref, prob_ref, slope_ref = given[6:]
            above_ref, both = take(2)
            finish(0, 1)
            through_qkv(
                orders[0],
                loads[0],
                da_above,
                dq_above,
                kv_above,
                kv_received,
                weights[0],
                both,
                wide,
            )
            above_ref[...] = wide[...].astype(BF16)
            finish(1)

            def above_two(at):
                return above_ref[at, :].astype(F32)

            sums[9:10, :] = token_sums(above_ref[...])

        norm_backward(above_two, lambda at: column_ref[at, 11:12], unit2, inverse2, wide, narrow)
        sums[8:9, :] = token_sums(narrow[...])
        piece = width // 8
        for part in range(4):
            for index in range(8):
                there = pl.ds(part * width + index * piece, piece)
                half = slice(index % 2 * 2, index % 2 * 2 + 2)
                grad = nn(matrix(down, part, index // 2, half), narrow[...])
                hidden[there, :] = (grad * slope_ref[there, :]).astype(BF16)
        for part in range(4):
            sums[4 + part : 5 + part, :] = token_sums(hidden[part * width : (part + 1) * width, :])
        if not top:
            finish(len(stages) - 2)
        for index in range(8):
            at = pl.ds(index * piece, piece)
            half = slice(index % 2 * 2, index % 2 * 2 + 2)
            rows_up = [matrix(up, part, index // 2, half) for part in range(4)]
            grad = wide[at, :] + nn(jnp.concatenate(rows_up, axis=1), hidden[...])
            wide[at, :] = grad
            narrow[at, :] = grad.astype(BF16)
        sums[3:4, :] = token_sums(narrow[...])
        norm_backward(
            lambda at: wide[at, :], lambda at: column_ref[at, 10:11], unit1, inverse1, da, narrow
        )
        leaving = [
            pltpu.make_async_copy(held, target, leave.at[n])
            for n, (held, target) in enumerate(zip((da, dq, kv_own, kv_other), targets))
        ]
        leaving[0].start()
        sums[2:3, :] = token_sums(narrow[...])
        finish(len(stages) - 1)
        mixed = hidden.at[pl.ds(0, width)]
        for index in range(8):
            half = slice(index % 2 * 2, index % 2 * 2 + 2)
            made = nn(matrix(out, index // 2, half), narrow[...])
            mixed[pl.ds(index * piece, piece), :] = made.astype(BF16)
        line = lax.broadcasted_iota(jnp.int32, (2 * HEAD_DIM, 1), 0)

        def pair(index, carry):
            at = tile_at(index, 2 * HEAD_DIM)
            grad_out = mixed[at, :]
            value = v_ref[:, at]
            for side in range(2):
                here = pl.ds(
                    pl.multiple_of(index * 2 * HEAD_DIM + side * HEAD_DIM, HEAD_DIM), HEAD_DIM
                )
                low = pl.ds(
                    pl.multiple_of(width + index * 2 * HEAD_DIM + side * HEAD_DIM, HEAD_DIM),
                    HEAD_DIM,
                )
                probs = prob_ref[2 * index + side]
                inner = jnp.sum(mixed[here, :].astype(F32) * o_ref[here, :], axis=0, keepdims=True)
                masked = grad_out * (line // HEAD_DIM == side).astype(F32).astype(BF16)
                grad_s = []
                for block in range(2 * rows // 128):
                    span = slice(block * 128, (block + 1) * 128)
                    grad_p = nn(value[span], masked)
                    grad_s.append((probs[span].astype(F32) * (grad_p - inner)).astype(BF16))
                grad_s = jnp.concatenate(grad_s, axis=0)
                dq[here, :] = (nn(k_ref[here, :], grad_s) * score_scale).astype(BF16)
                grad_k = (nt(q_ref[here, :], grad_s) * score_scale).astype(BF16)
                grad_v = nt(mixed[here, :], probs).astype(BF16)
                kv_own[here, :] = grad_k[:, :rows]
                kv_other[here, :] = grad_k[:, rows:]
                kv_own[low, :] = grad_v[:, :rows]
                kv_other[low, :] = grad_v[:, rows:]
            under = pl.ds(pl.multiple_of(width + index * 2 * HEAD_DIM, HEAD_DIM), 2 * HEAD_DIM)
            for n, held, spans in ((1, dq, (at,)), (2, kv_own, (at, under)), (3, kv_other, (at, under))):
                for span in spans:
                    pltpu.make_async_copy(held.at[span], targets[n].at[span], leave.at[n]).start()
            return carry

        lax.fori_loop(0, heads // 2, pair, 0, unroll=4)
        sums[0:1, :] = token_sums(dq[...])
        sums[1:2, :] = token_sums(kv_own[width:, :]) + token_sums(kv_other[width:, :])
        if cutting:
            cut_sums(sums, sent[0], 0, *axes)
            cut_sums(above_sums, sent[0], 1, *axes)
        for copy in leaving:
            copy.wait()

    outs = [((width, rows), F32), ((width, rows), BF16)]
    outs += [((2 * width, rows), BF16)] * 2 + [((16, width), F32)]
    scratch = [pltpu.VMEM(a.shape, a.dtype) for a, far in zip(first, fetched) if far]
    scratch += [pltpu.VMEM(*out) for out in outs[:4]]
    scratch += [
        pltpu.VMEM((width, rows), F32),
        pltpu.VMEM((width, rows), BF16),
        pltpu.VMEM((hidden_width, rows), BF16),
        pltpu.SemaphoreType.DMA((sum(counts),)),
        pltpu.SemaphoreType.DMA((len(first),)),
        pltpu.SemaphoreType.DMA((4,)),
    ]
    if cutting:
        outs += [((axes[0] * axes[1], 2, 10 * width // axes[0]), F32)]
    if top:
        outs = [((rows, width), BF16)] + outs
        scratch += [
            pltpu.VMEM((hidden_width, rows), F32),
            pltpu.VMEM((rows, hidden_width), BF16),
            pltpu.VMEM((rows, width), F32),
            pltpu.VMEM((rows, width), F32),
            pltpu.VMEM((rows, 128), F32),
            pltpu.VMEM((width, rows), F32),
            pltpu.VMEM((8, rows), F32),
        ]
    else:
        scratch += [pltpu.VMEM((width, rows), BF16), pltpu.VMEM((3, width, rows), BF16)]
    return call(
        kernel,
        "layer_backward",
        [(place, SMEM)]
        + [(chunk.order, SMEM) for chunk, _ in used]
        + [(a, ANY if far else VMEM) for a, far in zip(first, fetched)]
        + [(a, ANY) for a in blocks]
        + ([(before["sums"], VMEM)] if cutting else []),
        outs,
        [pltpu.VMEM(weight_shape(kind, width), BF16) for _, kind in used] + scratch,
        2 * rows * width * width * 13 + 16 * rows * rows * width,
        far=range(1, 5) if top else range(4),
    )


def qkv_backward(grads, chunk):
    width, rows = grads[0].shape
    arrays, count = len(chunk.arrays), chunk.count

    def kernel(order, da, dq, own, received, *refs):
        result, both, total, weight, sems = refs[arrays:]
        loads = Loads(order, chunk, refs[:arrays], "qkv", weight, sems)
        loads.start()
        through_qkv(order, loads, da, dq, own, received, weight, both, total)
        grad = total[...].astype(BF16)
        for index in range(width // 128):
            at = pl.ds(index * 128, 128)
            result[:, at] = grad[index * 128 : (index + 1) * 128].T

    return call(
        kernel,
        "qkv_backward",
        [(chunk.order, SMEM)] + [(g, VMEM) for g in grads] + [(a, ANY) for a in chunk.arrays],
        [((rows, width), BF16)],
        [
            pltpu.VMEM((3, width, rows), BF16),
            pltpu.VMEM((width, rows), F32),
            pltpu.VMEM(weight_shape("qkv", width), BF16),
            pltpu.SemaphoreType.DMA((count,)),
        ],
        2 * rows * width * width * 3,
    )[0]


def everywhere(values):
    total = lax.axis_size("items")
    return lax.all_to_all(jnp.broadcast_to(values, (total, *values.shape)), "items", 0, 0)


def in_rows(entries, cut):
    layers = entries.shape[0]
    grid = entries.reshape(layers, cut, 10)
    singles = jnp.concatenate([grid[..., :4], grid[..., 8:]], axis=2).swapaxes(1, 2)
    hidden = grid[..., 4:8].reshape(layers, -1)
    return jnp.concatenate([singles.reshape(layers, -1), hidden], axis=1)


SINGLES = (0, 1, 2, 3, 8, 9)


def bias_table(parts, norm_gain, width):
    total, layers, _ = parts.shape
    cut = width // total
    if total not in CHIPS:
        singles = parts[..., : 6 * cut].reshape(total, layers, 6, cut)
        singles = singles.transpose(1, 2, 0, 3).reshape(layers, 6, width)
        hidden = parts[..., 6 * cut :].swapaxes(0, 1).reshape(layers, 4, width)
        rows = jnp.concatenate([singles[:, :4], hidden, singles[:, 4:], norm_gain], axis=1)
        rows = jnp.pad(rows, ((0, 0), (0, 116), (0, 0)))
        return list(rows[:, :16]), list(rows.swapaxes(1, 2))

    def kernel(parts_ref, gain_ref, *refs):
        tables, columns, held = refs[:layers], refs[layers : 2 * layers], refs[-1]
        held[...] = jnp.zeros_like(held)
        for layer in range(layers):
            for item in range(total):
                for n, row in enumerate(SINGLES):
                    held[row : row + 1, item * cut : (item + 1) * cut] = parts_ref[
                        item, layer : layer + 1, n * cut : (n + 1) * cut
                    ]
                row, column = divmod(item * 4 * cut, width)
                held[4 + row : 5 + row, column : column + 4 * cut] = parts_ref[
                    item, layer : layer + 1, 6 * cut :
                ]
            held[10:12, :] = gain_ref[layer]
            tables[layer][...] = held[:16, :]
            turn(held, columns[layer])

    outs = call(
        kernel,
        "bias_table",
        [(parts, VMEM), (norm_gain, VMEM)],
        [((16, width), F32)] * layers + [((width, 128), F32)] * layers,
        [pltpu.VMEM((128, width), F32)],
        0,
    )
    return outs[:layers], outs[layers:]


def cut_sums(sums, sent, layer, total, cores):
    cut = sums.shape[1] // total
    for item in range(total):
        row, column = divmod(item * 4 * cut, sums.shape[1])
        for core in range(cores):
            for n, single in enumerate(SINGLES):
                sent[item * cores + core, layer : layer + 1, n * cut : (n + 1) * cut] = sums[
                    single : single + 1, item * cut : (item + 1) * cut
                ]
            sent[item * cores + core, layer : layer + 1, 6 * cut :] = sums[
                4 + row : 5 + row, column : column + 4 * cut
            ]


def bias_parts(sums, width):
    total = lax.axis_size("items")
    singles = jnp.concatenate([sums[:4], sums[8:10]], axis=0)
    singles = singles.reshape(6, total, width // total).swapaxes(0, 1).reshape(total, -1)
    return jnp.concatenate([singles, sums[4:8].reshape(total, -1)], axis=1)


def to_owners(parts):
    total, cores = lax.axis_size("items"), lax.axis_size("seq")
    sent = jnp.broadcast_to(parts.swapaxes(0, 1)[:, None], (total, cores, *parts.shape[::2]))
    return sent.reshape(total * cores, *parts.shape[::2])


def arrange_bias(owned, width):
    layers = owned.shape[0]
    cut = width // lax.axis_size("items")
    singles = owned[:, : 6 * cut].reshape(layers, 6, cut).swapaxes(1, 2)
    hidden = owned[:, 6 * cut :].reshape(layers, cut, 4)
    whole = jnp.concatenate([singles[..., :4], hidden, singles[..., 4:]], axis=2)
    return whole.reshape(layers, -1)


def on_device(
    tokens,
    lengths,
    cotangent,
    qkv_weight,
    out_weight,
    up_weight,
    down_weight,
    norm_gain,
    bias_master,
    first_moment,
    second_moment,
):
    item_count, part_len, width = tokens.shape
    levels = norm_gain.shape[0]
    rows = item_count * part_len
    core = lax.axis_index("seq")
    place = jnp.stack([lengths[0], core * part_len, (1 - core) * part_len]).astype(jnp.int32)
    turned = cotangent.reshape(rows, width).T

    chipped = lax.axis_size("items") in CHIPS
    if chipped:
        gather = Gather(qkv_weight, out_weight, up_weight, down_weight)
    else:
        plain = gather_plainly(qkv_weight, out_weight, up_weight, down_weight)
    state = tokens.reshape(rows, width)
    first = state
    if chipped:
        first, _ = lax.optimization_barrier((state, gather.mine[CHUNKS[0]]))
    state_other = swap_cores(first)
    if chipped:
        gather.computed.append(state_other)
    kept = [{} for _ in range(levels)]
    chunks = {}
    cycles = range(-1, 1 + max(KERNELS))
    for number, (action, level) in [(n, k) for n in cycles for k in (("", 0), *KERNELS.get(n, ()))]:
        if not action:
            if chipped:
                gather.cycle(number)
            if number == 0:
                master = in_rows(bias_master, bias_master.shape[1] // 10)
                if chipped:
                    master, _ = lax.optimization_barrier((master, gather.stages[0]["z"]))
                all_bias = everywhere(master)
                if chipped:
                    gather.computed.append(all_bias)
            if number == 1:
                bias_rows, columns = bias_table(all_bias, norm_gain, width)
                if chipped:
                    gather.computed += [*bias_rows, *columns, turned, place, gather.order]
            continue
        saved, bias = kept[level], bias_rows[level]
        kind = "attn" if action == "attention" else action
        chunk = gather.chunk((level, kind)) if chipped else plain[level, kind]
        chunks[level, kind] = chunk
        if action == "attention":
            (
                saved["p"],
                normed,
                saved["unit1"],
                saved["inverse1"],
                saved["o"],
                saved["q"],
                saved["k"],
                saved["v"],
            ) = attention_forward(place, state, state_other, chunk, bias)
            last = normed
        elif action == "up" and level < levels - 1:
            active, saved["slope"] = up_forward(normed, chunk, bias)
            last = active
        elif level < levels - 1:
            state, saved["unit2"], saved["inverse2"] = down_forward(
                normed, active, chunk, bias
            )
            last = state
            if chipped:
                stage = gather.stages[LAST - 1]
                waits = (stage["xy"], stage["yx"], gather.chunk((1, "attn")).arrays[-1])
                waits += (gather.swap_last(0, ()),)
                last, _ = lax.optimization_barrier((state, waits))
            last = state_other = swap_cores(last)
        if chipped:
            gather.computed.append(last)
            if (action, level) == ("down", 0):
                gather.swap_last(1, state_other)
                gather.swap_far(LAST - 1, state_other)
                gather.after = state_other
            if (action, level) == ("attention", 1):
                gather.swap_last(2, normed)

    axes = (lax.axis_size("items"), lax.axis_size("seq")) if chipped else None
    grads = [None] * levels
    for level in reversed(range(levels)):
        mine = {kind: chunks[level, kind] for kind in ("attn", "up", "down")}
        top = level == levels - 1
        if top:
            before = {"normed": normed, "cotangent": turned}
        else:
            before = {"grads": passed, "chunk": chunks[level + 1, "attn"], "sums": sums}
        outs = layer_backward(
            top,
            place,
            before,
            kept[level],
            mine,
            columns[level],
            bias_rows[level],
            axes,
        )
        if top:
            state, outs = outs[0], outs[1:]
        grad_sum, grad_q, kv_own, kv_other, sums = outs[:5]
        passed = [grad_sum, grad_q, kv_own, swap_cores(kv_other)]
        grads[level] = sums
    if chipped:
        sent = outs[5]
    else:
        sent = to_owners(jnp.stack([bias_parts(sums, width) for sums in grads]))
    layer_out = state.reshape(item_count, part_len, width)
    received = lax.all_to_all(sent, ("items", "seq"), 0, 0)
    input_grad = qkv_backward(passed, mine["attn"])
    received, _ = lax.optimization_barrier((received, input_grad))
    input_grad = input_grad.reshape(item_count, part_len, width)

    bias_grad = arrange_bias(jnp.sum(received, axis=0), width)
    new_first = beta_one * first_moment + (1.0 - beta_one) * bias_grad
    new_second = beta_two * second_moment + (1.0 - beta_two) * bias_grad * bias_grad
    first_hat = new_first / (1.0 - beta_one**STEP)
    second_hat = new_second / (1.0 - beta_two**STEP)
    new_bias = bias_master - learn_rate * first_hat / (jnp.sqrt(second_hat) + adam_eps)
    return (layer_out, input_grad, bias_grad, new_first, new_second, new_bias)


def solution(mesh):
    placed = (
        P("items", "seq", None),
        P("items"),
        P("items", "seq", None),
        P(None, "items", None),
        P(None, "items", None),
        P(None, "items", None),
        P(None, "items", None),
        P(),
        P(None, "items"),
        P(None, "items"),
        P(None, "items"),
    )
    return jax.shard_map(
        on_device,
        mesh=mesh,
        in_specs=placed,
        out_specs=(
            P("items", "seq", None),
            P("items", "seq", None),
            P(None, "items"),
            P(None, "items"),
            P(None, "items"),
            P(None, "items"),
        ),
        check_vma=False,
    )
```

```python
import functools
import math

import jax
import jax.numpy as jnp
from jax import lax
from jax.experimental import pallas as pl
from jax.experimental.pallas import tpu as pltpu
from jax.sharding import PartitionSpec as P

HEAD_DIM = 64
STEP = 10

ln_eps = 1e-12
beta_one = 0.9
beta_two = 0.999
adam_eps = 1e-08
learn_rate = 0.4
masked_score = -1000000000.0

CHIPS = {16: (4, 2, 2)}
CHUNKS = ((0, "attn"), (0, "up"), (0, "down"), (1, "attn"), (1, "up"), (1, "down"))
LAST = len(CHUNKS) - 1
KERNELS = {
    3: (("attention", 0),),
    4: (("up", 0),),
    5: (("down", 0), ("attention", 1)),
    6: (("up", 1), ("down", 1)),
}
SLOTS = 16
TILE = 256
WIDE = 512
STRIP = 32
F32 = jnp.float32
BF16 = jnp.bfloat16
VMEM_BYTES = 56 * 1024 * 1024

VMEM = pl.BlockSpec(memory_space=pltpu.VMEM)
SMEM = pl.BlockSpec(memory_space=pltpu.SMEM)
ANY = pl.BlockSpec(memory_space=pl.ANY)


def own_blocks(qkv_weight, out_weight, up_weight, down_weight):
    levels, rows, width = out_weight.shape
    keys = [(level, kind) for level in range(levels) for kind in ("attn", "up", "down")]
    core = lax.axis_index("seq").astype(jnp.int32).reshape(1)

    def kernel(core_ref, qkv, out, up, down, *refs):
        targets, (held, come, go) = refs[: len(keys)], refs[len(keys) :]
        here = core_ref[0]

        def copies(number, core):
            level, kind = keys[number]
            for half in range(2):
                if kind == "attn" and core == 0:
                    source = qkv.at[level, :, pl.ds(half * width, width)]
                elif kind == "attn":
                    source = out.at[level] if half else qkv.at[level, :, pl.ds(2 * width, width)]
                elif kind == "up":
                    column = pl.multiple_of((2 * here + half) * width, width)
                    source = up.at[level, :, pl.ds(column, width)]
                else:
                    row = pl.multiple_of((2 * here + half) * rows, rows)
                    source = down.at[level, pl.ds(row, rows), :]
                target = held.at[number, pl.ds(half * rows, rows), :]
                yield pltpu.make_async_copy(source, target, come.at[number, half])

        def each(act):
            for number, (_, kind) in enumerate(keys):
                if kind != "attn":
                    act(number, 0)
                    continue
                for side in range(2):
                    pl.when(here == side)(functools.partial(act, number, side))

        def begin(number, side):
            for copy in copies(number, side):
                copy.start()

        def finish(number, side):
            for copy in copies(number, side):
                copy.wait()

        each(begin)
        each(finish)
        leaving = [
            pltpu.make_async_copy(held.at[n], target, go.at[n]) for n, target in enumerate(targets)
        ]
        for copy in leaving:
            copy.start()
        for copy in leaving:
            copy.wait()

    blocks = pl.pallas_call(
        kernel,
        name="own_blocks",
        out_shape=[jax.ShapeDtypeStruct((2 * rows, width), BF16)] * len(keys),
        in_specs=[SMEM] + [ANY] * 4,
        out_specs=[ANY] * len(keys),
        scratch_shapes=[
            pltpu.VMEM((len(keys), 2 * rows, width), BF16),
            pltpu.SemaphoreType.DMA((len(keys), 2)),
            pltpu.SemaphoreType.DMA((len(keys),)),
        ],
        compiler_params=pltpu.CompilerParams(vmem_limit_bytes=VMEM_BYTES),
        cost_estimate=pl.CostEstimate(
            flops=0, bytes_accessed=8 * rows * width * len(keys), transcendentals=0
        ),
    )(core, qkv_weight, out_weight, up_weight, down_weight)
    return dict(zip(keys, blocks))


class Chunk:
    def __init__(self, arrays, runs, order):
        self.arrays, self.runs, self.order = arrays, runs, order
        self.count = sum(len(quarter) for quarter in runs)


def join(blocks, places=None):
    width = blocks[0].shape[1]
    total = sum(block.shape[0] for block in blocks)
    starts = [sum(block.shape[0] for block in blocks[:n]) for n in range(len(blocks))]
    table = [] if places is None else [places]

    def kernel(*refs):
        table_ref, refs = refs[: len(table)], refs[len(table) :]
        sources, (target, held, come, go) = refs[: len(blocks)], refs[len(blocks) :]
        ins, outs = [], []
        for n, (source, start) in enumerate(zip(sources, starts)):
            rows = blocks[n].shape[0]
            span = there = pl.ds(start, rows)
            if table:
                there = pl.ds(pl.multiple_of(table_ref[0][n] * rows, rows), rows)
            ins.append(pltpu.make_async_copy(source, held.at[span], come.at[n]))
            outs.append(pltpu.make_async_copy(held.at[span], target.at[there], go.at[n]))
            ins[-1].start()
        for come_in, go_out in zip(ins, outs):
            come_in.wait()
            go_out.start()
        for go_out in outs:
            go_out.wait()

    return pl.pallas_call(
        kernel,
        name="join",
        out_shape=jax.ShapeDtypeStruct((total, width), BF16),
        in_specs=[SMEM] * len(table) + [ANY] * len(blocks),
        out_specs=ANY,
        scratch_shapes=[
            pltpu.VMEM((total, width), BF16),
            pltpu.SemaphoreType.DMA((len(blocks),)),
            pltpu.SemaphoreType.DMA((len(blocks),)),
        ],
        compiler_params=pltpu.CompilerParams(vmem_limit_bytes=VMEM_BYTES),
        cost_estimate=pl.CostEstimate(
            flops=0, bytes_accessed=4 * total * width, transcendentals=0
        ),
    )(*table, *blocks)


class Gather:
    def __init__(self, *weights):
        self.total = lax.axis_size("items")
        self.depth, _, _ = CHIPS[self.total]
        self.plane = self.total // self.depth
        self.rows = weights[1].shape[1]
        self.mine = own_blocks(*weights)
        here = lax.axis_index("items") % self.plane
        core = lax.axis_index("seq")
        order = [here ^ side for side in range(4)]
        order += [core * 2, core * 2 + 1, 2 - core * 2, 3 - core * 2]
        self.order = jnp.stack(order).astype(jnp.int32)
        self.stages = [{} for _ in CHUNKS]
        self.last, self.computed = [], []

    def over_z(self, block):
        lines = [
            [place + self.plane * z for z in range(self.depth)] for place in range(self.plane)
        ]
        return lax.all_gather(block, "items", axis=0, tiled=True, axis_index_groups=lines)

    def step_z(self, block, step):
        pairs = [(item, (item + step * self.plane) % self.total) for item in range(self.total)]
        return lax.ppermute(block, "items", pairs)

    def line_of(self, parts):
        here = lax.axis_index("items") // self.plane
        places = [(here - step + self.depth) % self.depth for step in range(self.depth)]
        return join(parts, jnp.stack(places).astype(jnp.int32))

    def over(self, bit, block):
        return lax.ppermute(block, "items", [(item, item ^ bit) for item in range(self.total)])

    def across(self, x, y):
        half = x.shape[0] // 2
        return self.over(2, x[:half]), self.over(1, y[half:])

    def joined(self, stage):
        return join([stage[name] for name in ("z", "x", "y", "xy", "yx")])

    def cycle(self, number):
        wanted = {}
        if number == 0:
            wanted["corner"] = self.stages[LAST]["sides"][1:]
        if number == 1:
            wanted["sides"] = self.stages[LAST]["sides"]
        if 0 <= number < LAST - 1:
            wanted["block"] = self.mine[CHUNKS[number + 1]]
        if number == -1:
            wanted["first"] = self.mine[CHUNKS[0]]
            wanted["plane"] = self.mine[CHUNKS[LAST]]
        if LAST - 1 <= number <= LAST:
            wanted["line"] = self.stages[LAST]["lines"][number - LAST + 1]
        for lag in range(4):
            if 0 <= number - lag < LAST:
                wanted["lag%d" % lag] = self.stages[number - lag]
        def put(stage, name, value):
            stage[name] = value
            self.last.append(value)

        if 0 <= number <= LAST:
            self.before = self.last + self.computed
            wanted, _ = lax.optimization_barrier((wanted, self.before))
            self.last, self.computed = [], []
        elif number == -1:
            first = wanted["first"]
            steps = [self.step_z(first, step) for step in range(1, self.depth)]
            put(self.stages[0], "z", self.line_of([first, *steps]))

        if "lag3" in wanted:
            stage = self.stages[number - 3]
            if "joined" not in stage:
                put(stage, "joined", self.joined(wanted["lag3"]))
                wanted["lag3"] = stage
            put(stage, "other", swap_cores(wanted["lag3"]["joined"]))
        if "lag0" in wanted:
            along, stage = wanted["lag0"]["z"], self.stages[number]
            put(stage, "x", self.over(1, along))
            put(stage, "y", self.over(2, along))
        if "lag1" in wanted:
            held, stage = wanted["lag1"], self.stages[number - 1]
            stage["xy"], stage["yx"] = self.across(held["x"], held["y"])
            self.last += [stage["xy"], stage["yx"]]
        if "lag2" in wanted and number < LAST:
            put(self.stages[number - 2], "joined", self.joined(wanted["lag2"]))
        if "block" in wanted:
            put(self.stages[number + 1], "z", self.over_z(wanted["block"]))
        stage = self.stages[LAST]
        if LAST - 1 <= number <= LAST:
            stage.setdefault("z", []).append(self.over_z(wanted["line"]))
            if number < LAST:
                self.last.append(stage["z"][-1])
        if "plane" in wanted:
            own = wanted["plane"]
            x, y = self.over(1, own), self.over(2, own)
            stage["sides"] = [own, x, y]
            self.last += [x, y]
        if number == 0:
            x, y = wanted["corner"]
            stage["sides"] += self.across(x, y)
            self.last += stage["sides"][3:]
        if number == 1:
            _, x, y, xy, yx = wanted["sides"]
            stage["lines"] = [join([x, y[: self.rows]]), join([y[self.rows :], xy, yx])]
            self.last += stage["lines"]
        if 0 <= number < self.depth - 1:
            stage.setdefault("steps", [stage["sides"][0]])
            own, _ = lax.optimization_barrier((stage["steps"][0], self.before))
            stage["steps"].append(self.step_z(own, number + 1))
            self.last.append(stage["steps"][-1])
        if number == self.depth - 1:
            stage["z"] = [self.line_of(stage["steps"])]
            self.last.append(stage["z"][0])
    def swap_far(self, number, after):
        stage = self.stages[number]
        far, _ = lax.optimization_barrier(((stage["xy"], stage["yx"]), after))
        stage["xy2"], stage["yx2"] = [swap_cores(part) for part in far]
        return stage["xy2"], stage["yx2"]

    def swap_last(self, number, after):
        stage = self.stages[LAST]
        block, _ = lax.optimization_barrier((stage["z"][number], after))
        stage.setdefault("z2", []).append(swap_cores(block))
        return stage["z2"][-1]

    def chunk(self, key):
        number = CHUNKS.index(key)
        stage = self.stages[number]
        order = self.order
        if number == LAST:
            arrays = stage["z"] + stage["z2"]
            arrays = [a.reshape(self.depth, -1, self.rows, a.shape[1]) for a in arrays]
            spots = [(0, 0), (0, 1)] + [(1, n) for n in range(3)] + [(2, n) for n in range(3)]
            runs = [
                [
                    (array + spots[2 * side + part][0], spots[2 * side + part][1], 0, side, 0, self.depth)
                    for side in range(4)
                ]
                for array in (0, 3)
                for part in range(2)
            ]
            return Chunk(arrays, runs, order)
        half = self.depth // 2
        places = [(0, 0, self.depth), (1, 0, self.depth), (2, 0, self.depth)]
        places += [(3, 0, half), (3, half, self.depth - half)]
        own = [(n, 0, *place) for n, place in enumerate(places)]
        block = 2 * self.rows
        first = [0, self.depth, 2 * self.depth, 3 * self.depth, 3 * self.depth + half]
        other = [(5, *pair) for pair in ((first[n], *places[n]) for n in range(5))]
        names = ["z", "x", "y", "xy", "yx", "other"]
        if number == LAST - 1:
            late, _ = lax.optimization_barrier(
                (join([stage[name] for name in names[:3]]), self.after)
            )
            stage["other"] = swap_cores(late)
            other[3:] = [(6, 0, *places[3]), (7, 0, *places[4])]
            names += ["xy2", "yx2"]
        elif "other" not in stage:
            stage["other"] = swap_cores(self.joined(stage))
        arrays = [stage[name] for name in names]
        runs = [
            [(array, part, first, side, z, number) for array, first, side, z, number in spans]
            for spans in (own, other)
            for part in range(2)
        ]
        arrays = [a.reshape(a.shape[0] // block, 2, self.rows, a.shape[1]) for a in arrays]
        return Chunk(arrays, runs, order)


def gather_plainly(qkv_weight, out_weight, up_weight, down_weight):
    shards = {}
    for level in range(out_weight.shape[0]):
        shards[level, "attn"] = [qkv_weight[level], out_weight[level]]
        shards[level, "up"] = [up_weight[level]]
        shards[level, "down"] = [down_weight[level]]
    width = out_weight.shape[-1]
    plain = jnp.concatenate([jnp.arange(4), jnp.arange(4)]).astype(jnp.int32)
    rows = width // SLOTS
    runs = [[(c, side, 0, side, 0, 4) for side in range(4)] for c in range(4)]
    done = {}
    for key, parts in shards.items():
        whole = [lax.all_gather(part, "items", axis=0, tiled=True) for part in parts]
        if key[1] == "down":
            cut = whole[0].reshape(4, 4, 4, rows, width)
            arrays = [cut[:, :, c] for c in range(4)]
        else:
            joined = jnp.concatenate(whole, axis=1)
            arrays = [joined[:, width * c : width * (c + 1)] for c in range(4)]
            arrays = [array.reshape(4, 4, rows, width) for array in arrays]
        done[key] = Chunk(arrays, runs, plain)
    return done


def weight_shape(kind, width):
    rows = width // SLOTS
    return {
        "down": (4, 4, 4, rows, width),
        "up": (4, 4, 4, rows, width),
        "attn": (4, 4, 4, rows, width),
        "qkv": (3, 4, 4, rows, width),
        "out": (4, 4, rows, width),
    }[kind]


class Loads:
    def __init__(self, order, chunk, refs, kind, target, sems, first=0):
        self.order, self.chunk, self.refs, self.kind = order, chunk, refs, kind
        self.target, self.sems, self.first = target, sems, first

    def visit(self, act, only=None):
        number = self.first
        for quarter, runs in enumerate(self.chunk.runs):
            if only not in (None, quarter):
                number += len(runs)
                continue
            which = self.order[4 + quarter]

            def run(number=number, runs=runs, which=which):
                for n, (array, part, first, side, z, depth) in enumerate(runs):
                    source = self.refs[array].at[pl.ds(first, depth), part]
                    span, place = pl.ds(z, depth), self.order[side]
                    if self.kind == "down":
                        target = self.target.at[span, place, which]
                    elif self.kind == "out":
                        target = self.target.at[span, place]
                    else:
                        target = self.target.at[which, span, place]
                    act(pltpu.make_async_copy(source, target, self.sems.at[number + n]))

            if self.kind == "out":
                pl.when(which == 3)(run)
            elif self.kind == "qkv":
                pl.when(which != 3)(run)
            else:
                run()
            number += len(runs)

    def start(self):
        self.visit(lambda copy: copy.start())

    def wait(self, only=None):
        self.visit(lambda copy: copy.wait(), only)


def call(kernel, name, operands, outs, scratch, flops, transcendentals=0, far=()):
    moved = sum(a.size * a.dtype.itemsize for a, _ in operands)
    moved += sum(math.prod(s) * jnp.dtype(d).itemsize for s, d in outs)
    return pl.pallas_call(
        kernel,
        name=name,
        out_shape=[jax.ShapeDtypeStruct(s, d) for s, d in outs],
        in_specs=[spec for _, spec in operands],
        out_specs=[ANY if n in far else VMEM for n in range(len(outs))],
        scratch_shapes=scratch,
        compiler_params=pltpu.CompilerParams(vmem_limit_bytes=VMEM_BYTES),
        cost_estimate=pl.CostEstimate(
            flops=int(flops), bytes_accessed=int(moved), transcendentals=int(transcendentals)
        ),
    )(*[a for a, _ in operands])


def nt(left, right):
    return lax.dot_general(left, right, (((1,), (1,)), ((), ())), preferred_element_type=F32)


def tn(left, right):
    return lax.dot_general(left, right, (((0,), (0,)), ((), ())), preferred_element_type=F32)


def nn(left, right):
    return jnp.dot(left, right, preferred_element_type=F32)


def swap_cores(block):
    return lax.ppermute(block, "seq", [(0, 1), (1, 0)])


def tile_at(index, size=TILE):
    return pl.ds(pl.multiple_of(index * size, size), size)


def fold_rows(values):
    return jnp.sum(values.reshape(-1, 8, values.shape[-1]), axis=0)


def column_loop(width, body):
    for index in range(width // WIDE):
        body(pl.ds(index * WIDE, WIDE))


def matrix(weight, *index):
    blocks = weight[index] if index else weight[...]
    return blocks.reshape(-1, blocks.shape[-1])


def columns_of(weight, at, *index):
    rest = weight.ndim - len(index) - 1
    blocks = weight[(*index, *[slice(None)] * rest, at)]
    return blocks.reshape(-1, blocks.shape[-1])


def token_sums(values, counted=None):
    if counted is None:
        counted = jnp.ones((1, values.shape[1]), BF16)
    return nt(jnp.broadcast_to(counted, (8, values.shape[1])), values)[0:1]


def turn(source, target):
    for index in range(source.shape[1] // 128):
        span = pl.ds(index * 128, 128)
        target[span, :] = source[:, span].T


def normalize_strips(rows, source, gain, shift, unit, inverse, result):
    def strip(index, carry):
        at = tile_at(index, STRIP)
        values = source[at, :]
        center = values - jnp.mean(values, axis=-1, keepdims=True)
        spread = jnp.mean(center * center, axis=-1, keepdims=True)
        scale = lax.rsqrt(spread + ln_eps)
        normal = center * scale
        unit[at, :] = normal
        inverse[at, :] = jnp.broadcast_to(scale, (STRIP, inverse.shape[1]))
        result[at, :] = (normal * gain + shift).astype(BF16)
        return carry

    lax.fori_loop(0, rows // STRIP, strip, 0, unroll=4)


def attention_forward(place, state, state_other, chunk, bias_rows):
    rows, width = state.shape
    heads = width // HEAD_DIM
    arrays, count = len(chunk.arrays), chunk.count
    score_scale = 1.0 / math.sqrt(HEAD_DIM)

    def kernel(order, place_ref, state_ref, other_state, bias_ref, *refs):
        prob_hbm, result, unit_out, inverse_out, o_out, q_out, k_out, value = refs[
            arrays : arrays + 8
        ]
        prob_ref, query, key, mixed, total, unit, inverse, states, weight, sems, leave = refs[
            arrays + 8 :
        ]
        loads = Loads(order, chunk, refs[:arrays], "attn", weight, sems)
        loads.start()
        states[:rows, :] = state_ref[...]
        states[rows:, :] = other_state[...]
        spot = lax.broadcasted_iota(jnp.int32, (2 * rows, 1), 0)
        position = jnp.where(spot < rows, place_ref[1] + spot, place_ref[2] + spot - rows)
        live = position < place_ref[0]
        line = lax.broadcasted_iota(jnp.int32, (2 * HEAD_DIM, 1), 0)
        loads.wait(0)
        loads.wait(2)
        pl.when(order[5] != 3)(lambda: loads.wait(1))
        pl.when(order[5] == 3)(lambda: loads.wait(3))

        def project(at):
            query[:, at] = (
                nn(state_ref[...], columns_of(weight, at, 0)) + bias_ref[0:1, at]
            ).astype(BF16)
            key[:, at] = nn(states[...], columns_of(weight, at, 1)).astype(BF16)
            value[:, at] = (nn(states[...], columns_of(weight, at, 2)) + bias_ref[1:2, at]).astype(
                BF16
            )

        column_loop(width, project)
        turn(query, q_out)
        turn(key, k_out)

        spans = [slice(start, start + 128) for start in range(0, 2 * rows, 128)]

        def leaving(index):
            span = pl.ds(2 * index, 2)
            return pltpu.make_async_copy(prob_ref.at[span], prob_hbm.at[span], leave.at[index])

        def pair(index, carry):
            at = tile_at(index, 2 * HEAD_DIM)
            turned = value[:, at].T
            outs = []
            for side in range(2):
                mine = (line // HEAD_DIM == side).astype(F32) * score_scale
                asked = q_out[at, :] * mine.astype(BF16)
                blocks = [nn(key[span, at], asked) for span in spans]
                blocks = [jnp.where(live[s], b, masked_score) for s, b in zip(spans, blocks)]
                tops = [jnp.max(block, axis=0, keepdims=True) for block in blocks]
                top = functools.reduce(jnp.maximum, tops)
                blocks = [jnp.exp(block - top) for block in blocks]
                norm = sum(jnp.sum(block, axis=0, keepdims=True) for block in blocks)
                norm = 1.0 / norm
                weights = jnp.concatenate([(b * norm).astype(BF16) for b in blocks], axis=0)
                prob_ref[2 * index + side] = weights
                outs.append(nn(turned[HEAD_DIM * side : HEAD_DIM * (side + 1)], weights))
            outs = jnp.concatenate(outs, axis=0)
            o_out[at, :] = outs
            mixed[:, at] = outs.T.astype(BF16)
            leaving(index).start()
            return carry

        lax.fori_loop(0, heads // 2, pair, 0, unroll=4)
        pl.when(order[5] != 3)(lambda: loads.wait(3))
        pl.when(order[5] == 3)(lambda: loads.wait(1))

        def column(at):
            total[:, at] = (
                state_ref[:, at].astype(F32)
                + nn(mixed[...], columns_of(weight, at, 3))
                + bias_ref[2:3, at]
            )

        column_loop(width, column)
        normalize_strips(rows, total, bias_ref[10:11, :], bias_ref[3:4, :], unit, inverse, result)
        turn(unit, unit_out)
        inverse_out[...] = inverse[...].T[:8]
        for index in range(heads // 2):
            leaving(index).wait()

    return call(
        kernel,
        "attention_forward",
        [
            (chunk.order, SMEM),
            (place, SMEM),
            (state, VMEM),
            (state_other, VMEM),
            (bias_rows, VMEM),
        ]
        + [(a, ANY) for a in chunk.arrays],
        [
            ((heads, 2 * rows, rows), BF16),
            ((rows, width), BF16),
            ((width, rows), F32),
            ((8, rows), F32),
            ((width, rows), F32),
            ((width, rows), BF16),
            ((width, 2 * rows), BF16),
            ((2 * rows, width), BF16),
        ],
        [
            pltpu.VMEM((heads, 2 * rows, rows), BF16),
            pltpu.VMEM((rows, width), BF16),
            pltpu.VMEM((2 * rows, width), BF16),
            pltpu.VMEM((rows, width), BF16),
            pltpu.VMEM((rows, width), F32),
            pltpu.VMEM((rows, width), F32),
            pltpu.VMEM((rows, 128), F32),
            pltpu.VMEM((2 * rows, width), BF16),
            pltpu.VMEM(weight_shape("attn", width), BF16),
            pltpu.SemaphoreType.DMA((count,)),
            pltpu.SemaphoreType.DMA((heads // 2,)),
        ],
        2 * rows * width * width * 6 + 8 * rows * rows * width,
        heads * rows * rows * 2,
        far=(0,),
    )


def up_part(order, loads, normed_ref, bias_ref, weight, active, slope, then=None):
    width = normed_ref.shape[1]
    for quarter in range(4):
        which = order[4 + quarter]
        loads.wait(quarter)
        if quarter == 1 and then is not None:
            then()

        def column(index, carry, which=which):
            at = tile_at(index)
            there = pl.ds(pl.multiple_of(which * width + index * TILE, TILE), TILE)
            whole = nn(normed_ref[...], columns_of(weight, at, which))
            for start in range(0, whole.shape[0], 128):
                span = slice(start, start + 128)
                hidden = whole[span] + bias_ref[pl.ds(4 + which, 1), at]
                normal = 0.5 * (1.0 + lax.erf(hidden * (1.0 / math.sqrt(2.0))))
                density = jnp.exp(-0.5 * hidden * hidden) * (1.0 / math.sqrt(2.0 * math.pi))
                active[span, there] = (hidden * normal).astype(BF16)
                slope[there, span] = (normal + hidden * density).T
            return carry

        lax.fori_loop(0, width // TILE, column, 0, unroll=4)


def up_forward(normed, chunk, bias_rows):
    rows, width = normed.shape
    arrays, count = len(chunk.arrays), chunk.count
    hidden_width = 4 * width

    def kernel(order, normed_ref, bias_ref, *refs):
        active, slope, weight, sems = refs[arrays:]
        loads = Loads(order, chunk, refs[:arrays], "up", weight, sems)
        loads.start()
        up_part(order, loads, normed_ref, bias_ref, weight, active, slope)

    return call(
        kernel,
        "up_forward",
        [(chunk.order, SMEM), (normed, VMEM), (bias_rows, VMEM)] + [(a, ANY) for a in chunk.arrays],
        [((rows, hidden_width), BF16), ((hidden_width, rows), F32)],
        [pltpu.VMEM(weight_shape("up", width), BF16), pltpu.SemaphoreType.DMA((count,))],
        2 * rows * width * hidden_width,
        2 * rows * hidden_width,
    )


def down_part(
    normed_ref, active_ref, bias_ref, weight, total, unit, inverse, result, unit_out, inverse_out
):
    rows, width = normed_ref.shape

    def column(at):
        total[:, at] = (
            normed_ref[:, at].astype(F32)
            + nn(active_ref[...], columns_of(weight, at))
            + bias_ref[8:9, at]
        )

    column_loop(width, column)
    normalize_strips(rows, total, bias_ref[11:12, :], bias_ref[9:10, :], unit, inverse, result)
    turn(unit, unit_out)
    inverse_out[...] = inverse[...].T[:8]


def down_forward(normed, active, chunk, bias_rows):
    rows, width = normed.shape
    arrays, count = len(chunk.arrays), chunk.count

    def kernel(order, normed_ref, active_ref, bias_ref, *refs):
        result, unit_out, inverse_out, total, unit, inverse, weight, sems = refs[arrays:]
        loads = Loads(order, chunk, refs[:arrays], "down", weight, sems)
        loads.start()
        loads.wait()
        down_part(
            normed_ref,
            active_ref,
            bias_ref,
            weight,
            total,
            unit,
            inverse,
            result,
            unit_out,
            inverse_out,
        )

    return call(
        kernel,
        "down_forward",
        [(chunk.order, SMEM), (normed, VMEM), (active, VMEM), (bias_rows, VMEM)]
        + [(a, ANY) for a in chunk.arrays],
        [((rows, width), BF16), ((width, rows), F32), ((8, rows), F32)],
        [
            pltpu.VMEM((rows, width), F32),
            pltpu.VMEM((rows, width), F32),
            pltpu.VMEM((rows, 128), F32),
            pltpu.VMEM(weight_shape("down", width), BF16),
            pltpu.SemaphoreType.DMA((count,)),
        ],
        2 * rows * width * width * 4,
    )


def norm_backward(upstream, gain, unit, inverse, wide, narrow):
    width, rows = unit.shape
    strips = [pl.ds(index * 128, 128) for index in range(width // 128)]
    mean = jnp.zeros((8, rows), F32)
    lean = jnp.zeros((8, rows), F32)
    for at in strips:
        scaled = upstream(at) * gain(at)
        mean = mean + fold_rows(scaled)
        lean = lean + fold_rows(scaled * unit[at, :])
    mean = jnp.sum(mean, axis=0, keepdims=True) * (1.0 / width)
    lean = jnp.sum(lean, axis=0, keepdims=True) * (1.0 / width)
    for at in strips:
        below = inverse[0:1, :] * (upstream(at) * gain(at) - mean - unit[at, :] * lean)
        wide[at, :] = below
        narrow[at, :] = below.astype(BF16)


def through_qkv(order, loads, da, dq, own, received, weight, grads, total):
    width, rows = da.shape
    grads[0] = dq[...]
    for part in range(2):
        span = pl.ds(part * width, width)
        grads[1 + part] = (own[span, :].astype(F32) + received[span, :].astype(F32)).astype(BF16)
    total[...] = da[...]
    for quarter in range(4):
        which = order[4 + quarter]

        def add(quarter=quarter, which=which):
            loads.wait(quarter)
            for index in range(8):
                at = pl.ds(index * (width // 8), width // 8)
                half = slice(index % 2 * 2, index % 2 * 2 + 2)
                total[at, :] += nn(matrix(weight, which, index // 2, half), grads[which])

        pl.when(which != 3)(add)


def layer_backward(top, place, before, saved, chunks, columns, bias_rows, axes):
    queries, keys, values, prob, mixed = (saved[name] for name in ("q", "k", "v", "p", "o"))
    width, rows = queries.shape
    heads = width // HEAD_DIM
    hidden_width = 4 * width
    score_scale = 1.0 / math.sqrt(HEAD_DIM)
    used = [(chunks["down"], "down"), (chunks["up"], "up"), (chunks["attn"], "out")]
    if top:
        first = [before["normed"], before["cotangent"], bias_rows]
        slope = []
    else:
        used = [(before["chunk"], "qkv")] + used
        first = [*before["grads"], saved["unit2"], saved["inverse2"]]
        slope = [saved["slope"]]
    cutting = not top and axes is not None
    first += [columns, saved["unit1"], saved["inverse1"], mixed, queries, keys, values, prob]
    first += slope
    blocks = [a for chunk, _ in used for a in chunk.arrays]
    counts = [chunk.count for chunk, _ in used]
    fetched = [a.size * a.dtype.itemsize > 2**17 for a in first]

    def kernel(place_ref, *refs):
        refs = list(refs)

        def take(number):
            taken, refs[:] = refs[:number], refs[number:]
            return taken

        orders = take(len(used))
        given = take(len(first))
        sources = [take(len(chunk.arrays)) for chunk, _ in used]
        if cutting:
            (above_sums,) = take(1)
        if top:
            (state_out,) = take(1)
        targets = take(4)
        (sums,) = take(1)
        sent = take(1) if cutting else None
        weights = take(len(used))
        copies = []
        for number, far in enumerate(fetched):
            if far:
                (held,) = take(1)
                copies.append((given[number], held))
                given[number] = held
            else:
                copies.append(None)
        da, dq, kv_own, kv_other, wide, narrow, hidden, sems, extra, leave = take(10)
        loads = []
        for number, (chunk, kind) in enumerate(used):
            loads.append(
                Loads(
                    orders[number],
                    chunk,
                    sources[number],
                    kind,
                    weights[number],
                    sems,
                    sum(counts[:number]),
                )
            )
        copies = [
            pltpu.make_async_copy(*pair, extra.at[number]) if pair else None
            for number, pair in enumerate(copies)
        ]
        start = len(first) - 8 - len(slope)
        late = [start + 3, start + 4, start + 5, start + 6, start + 7]
        if top:
            stages = [([loads[1]], [0]), ([loads[0]], [1, start, start + 1]), ([loads[2]], late)]
        else:
            stages = [
                ([loads[0]], [0, 1, 2, 3]),
                ([loads[1]], [4, start, start + 8]),
                ([loads[2]], [start + 1]),
                ([loads[3]], late),
            ]
        stages = [
            [*weights_in, *[copies[n] for n in numbers if copies[n] is not None]]
            for weights_in, numbers in stages
        ]

        def begin(number):
            if number < len(stages):
                for item in stages[number]:
                    item.start()

        def finish(number, skipped=0):
            for item in stages[number][skipped:]:
                item.wait()
            begin(number + (1 if top else 2))

        begin(0)
        if not top:
            begin(1)
        down, up, out = weights[-3:]

        if top:
            normed_ref, cotangent_ref, bias_ref = given[:3]
            column_ref, unit1, inverse1, o_ref, q_ref, k_ref, v_ref, prob_ref = given[3:]
            slope_ref, active_ref, total, unit, inverse, unit2, inverse2 = take(7)
            for item in stages[0][1:]:
                item.wait()
            up_part(
                orders[1],
                loads[1],
                normed_ref,
                bias_ref,
                up,
                active_ref,
                slope_ref,
                lambda: begin(1),
            )
            finish(1)
            down_part(
                normed_ref,
                active_ref,
                bias_ref,
                    down,
                total,
                unit,
                inverse,
                state_out,
                unit2,
                inverse2,
            )
            token = lax.broadcasted_iota(jnp.int32, (1, rows), 1) + place_ref[1]
            row_live = (token < place_ref[0]).astype(F32)

            def above_two(at):
                return cotangent_ref[at, :].astype(F32) * row_live

            sums[9:10, :] = token_sums(cotangent_ref[...], row_live.astype(BF16))
        else:
            da_above, dq_above, kv_above, kv_received, unit2, inverse2 = given[:6]
            column_ref, unit1, inverse1, o_ref, q_ref, k_ref, v_ref, prob_ref, slope_ref = given[6:]
            above_ref, both = take(2)
            finish(0, 1)
            through_qkv(
                orders[0],
                loads[0],
                da_above,
                dq_above,
                kv_above,
                kv_received,
                weights[0],
                both,
                wide,
            )
            above_ref[...] = wide[...].astype(BF16)
            finish(1)

            def above_two(at):
                return above_ref[at, :].astype(F32)

            sums[9:10, :] = token_sums(above_ref[...])

        norm_backward(above_two, lambda at: column_ref[at, 11:12], unit2, inverse2, wide, narrow)
        sums[8:9, :] = token_sums(narrow[...])
        piece = width // 8
        for part in range(4):
            for index in range(8):
                there = pl.ds(part * width + index * piece, piece)
                half = slice(index % 2 * 2, index % 2 * 2 + 2)
                grad = nn(matrix(down, part, index // 2, half), narrow[...])
                hidden[there, :] = (grad * slope_ref[there, :]).astype(BF16)
        for part in range(4):
            sums[4 + part : 5 + part, :] = token_sums(hidden[part * width : (part + 1) * width, :])
        if not top:
            finish(len(stages) - 2)
        for index in range(8):
            at = pl.ds(index * piece, piece)
            half = slice(index % 2 * 2, index % 2 * 2 + 2)
            rows_up = [matrix(up, part, index // 2, half) for part in range(4)]
            grad = wide[at, :] + nn(jnp.concatenate(rows_up, axis=1), hidden[...])
            wide[at, :] = grad
            narrow[at, :] = grad.astype(BF16)
        sums[3:4, :] = token_sums(narrow[...])
        norm_backward(
            lambda at: wide[at, :], lambda at: column_ref[at, 10:11], unit1, inverse1, da, narrow
        )
        leaving = [
            pltpu.make_async_copy(held, target, leave.at[n])
            for n, (held, target) in enumerate(zip((da, dq, kv_own, kv_other), targets))
        ]
        leaving[0].start()
        sums[2:3, :] = token_sums(narrow[...])
        finish(len(stages) - 1)
        mixed = hidden.at[pl.ds(0, width)]
        for index in range(8):
            half = slice(index % 2 * 2, index % 2 * 2 + 2)
            made = nn(matrix(out, index // 2, half), narrow[...])
            mixed[pl.ds(index * piece, piece), :] = made.astype(BF16)
        line = lax.broadcasted_iota(jnp.int32, (2 * HEAD_DIM, 1), 0)

        def pair(index, carry):
            at = tile_at(index, 2 * HEAD_DIM)
            grad_out = mixed[at, :]
            value = v_ref[:, at]
            for side in range(2):
                here = pl.ds(
                    pl.multiple_of(index * 2 * HEAD_DIM + side * HEAD_DIM, HEAD_DIM), HEAD_DIM
                )
                low = pl.ds(
                    pl.multiple_of(width + index * 2 * HEAD_DIM + side * HEAD_DIM, HEAD_DIM),
                    HEAD_DIM,
                )
                probs = prob_ref[2 * index + side]
                inner = jnp.sum(mixed[here, :].astype(F32) * o_ref[here, :], axis=0, keepdims=True)
                masked = grad_out * (line // HEAD_DIM == side).astype(F32).astype(BF16)
                grad_s = []
                for block in range(2 * rows // 128):
                    span = slice(block * 128, (block + 1) * 128)
                    grad_p = nn(value[span], masked)
                    grad_s.append((probs[span].astype(F32) * (grad_p - inner)).astype(BF16))
                grad_s = jnp.concatenate(grad_s, axis=0)
                dq[here, :] = (nn(k_ref[here, :], grad_s) * score_scale).astype(BF16)
                grad_k = (nt(q_ref[here, :], grad_s) * score_scale).astype(BF16)
                grad_v = nt(mixed[here, :], probs).astype(BF16)
                kv_own[here, :] = grad_k[:, :rows]
                kv_other[here, :] = grad_k[:, rows:]
                kv_own[low, :] = grad_v[:, :rows]
                kv_other[low, :] = grad_v[:, rows:]
            under = pl.ds(pl.multiple_of(width + index * 2 * HEAD_DIM, HEAD_DIM), 2 * HEAD_DIM)
            for n, held, spans in ((1, dq, (at,)), (2, kv_own, (at, under)), (3, kv_other, (at, under))):
                for span in spans:
                    pltpu.make_async_copy(held.at[span], targets[n].at[span], leave.at[n]).start()
            return carry

        lax.fori_loop(0, heads // 2, pair, 0, unroll=4)
        sums[0:1, :] = token_sums(dq[...])
        sums[1:2, :] = token_sums(kv_own[width:, :]) + token_sums(kv_other[width:, :])
        if cutting:
            cut_sums(sums, sent[0], 0, *axes)
            cut_sums(above_sums, sent[0], 1, *axes)
        for copy in leaving:
            copy.wait()

    outs = [((width, rows), F32), ((width, rows), BF16)]
    outs += [((2 * width, rows), BF16)] * 2 + [((16, width), F32)]
    scratch = [pltpu.VMEM(a.shape, a.dtype) for a, far in zip(first, fetched) if far]
    scratch += [pltpu.VMEM(*out) for out in outs[:4]]
    scratch += [
        pltpu.VMEM((width, rows), F32),
        pltpu.VMEM((width, rows), BF16),
        pltpu.VMEM((hidden_width, rows), BF16),
        pltpu.SemaphoreType.DMA((sum(counts),)),
        pltpu.SemaphoreType.DMA((len(first),)),
        pltpu.SemaphoreType.DMA((4,)),
    ]
    if cutting:
        outs += [((axes[0] * axes[1], 2, 10 * width // axes[0]), F32)]
    if top:
        outs = [((rows, width), BF16)] + outs
        scratch += [
            pltpu.VMEM((hidden_width, rows), F32),
            pltpu.VMEM((rows, hidden_width), BF16),
            pltpu.VMEM((rows, width), F32),
            pltpu.VMEM((rows, width), F32),
            pltpu.VMEM((rows, 128), F32),
            pltpu.VMEM((width, rows), F32),
            pltpu.VMEM((8, rows), F32),
        ]
    else:
        scratch += [pltpu.VMEM((width, rows), BF16), pltpu.VMEM((3, width, rows), BF16)]
    return call(
        kernel,
        "layer_backward",
        [(place, SMEM)]
        + [(chunk.order, SMEM) for chunk, _ in used]
        + [(a, ANY if far else VMEM) for a, far in zip(first, fetched)]
        + [(a, ANY) for a in blocks]
        + ([(before["sums"], VMEM)] if cutting else []),
        outs,
        [pltpu.VMEM(weight_shape(kind, width), BF16) for _, kind in used] + scratch,
        2 * rows * width * width * 13 + 16 * rows * rows * width,
        far=range(1, 5) if top else range(4),
    )


def qkv_backward(grads, chunk):
    width, rows = grads[0].shape
    arrays, count = len(chunk.arrays), chunk.count

    def kernel(order, da, dq, own, received, *refs):
        result, both, total, weight, sems = refs[arrays:]
        loads = Loads(order, chunk, refs[:arrays], "qkv", weight, sems)
        loads.start()
        through_qkv(order, loads, da, dq, own, received, weight, both, total)
        grad = total[...].astype(BF16)
        for index in range(width // 128):
            at = pl.ds(index * 128, 128)
            result[:, at] = grad[index * 128 : (index + 1) * 128].T

    return call(
        kernel,
        "qkv_backward",
        [(chunk.order, SMEM)] + [(g, VMEM) for g in grads] + [(a, ANY) for a in chunk.arrays],
        [((rows, width), BF16)],
        [
            pltpu.VMEM((3, width, rows), BF16),
            pltpu.VMEM((width, rows), F32),
            pltpu.VMEM(weight_shape("qkv", width), BF16),
            pltpu.SemaphoreType.DMA((count,)),
        ],
        2 * rows * width * width * 3,
    )[0]


def everywhere(values):
    total = lax.axis_size("items")
    return lax.all_to_all(jnp.broadcast_to(values, (total, *values.shape)), "items", 0, 0)


def in_rows(entries, cut):
    layers = entries.shape[0]
    grid = entries.reshape(layers, cut, 10)
    singles = jnp.concatenate([grid[..., :4], grid[..., 8:]], axis=2).swapaxes(1, 2)
    hidden = grid[..., 4:8].reshape(layers, -1)
    return jnp.concatenate([singles.reshape(layers, -1), hidden], axis=1)


SINGLES = (0, 1, 2, 3, 8, 9)


def bias_table(parts, norm_gain, width):
    total, layers, _ = parts.shape
    cut = width // total
    if total not in CHIPS:
        singles = parts[..., : 6 * cut].reshape(total, layers, 6, cut)
        singles = singles.transpose(1, 2, 0, 3).reshape(layers, 6, width)
        hidden = parts[..., 6 * cut :].swapaxes(0, 1).reshape(layers, 4, width)
        rows = jnp.concatenate([singles[:, :4], hidden, singles[:, 4:], norm_gain], axis=1)
        rows = jnp.pad(rows, ((0, 0), (0, 116), (0, 0)))
        return list(rows[:, :16]), list(rows.swapaxes(1, 2))

    def kernel(parts_ref, gain_ref, *refs):
        tables, columns, held = refs[:layers], refs[layers : 2 * layers], refs[-1]
        held[...] = jnp.zeros_like(held)
        for layer in range(layers):
            for item in range(total):
                for n, row in enumerate(SINGLES):
                    held[row : row + 1, item * cut : (item + 1) * cut] = parts_ref[
                        item, layer : layer + 1, n * cut : (n + 1) * cut
                    ]
                row, column = divmod(item * 4 * cut, width)
                held[4 + row : 5 + row, column : column + 4 * cut] = parts_ref[
                    item, layer : layer + 1, 6 * cut :
                ]
            held[10:12, :] = gain_ref[layer]
            tables[layer][...] = held[:16, :]
            turn(held, columns[layer])

    outs = call(
        kernel,
        "bias_table",
        [(parts, VMEM), (norm_gain, VMEM)],
        [((16, width), F32)] * layers + [((width, 128), F32)] * layers,
        [pltpu.VMEM((128, width), F32)],
        0,
    )
    return outs[:layers], outs[layers:]


def cut_sums(sums, sent, layer, total, cores):
    cut = sums.shape[1] // total
    for item in range(total):
        row, column = divmod(item * 4 * cut, sums.shape[1])
        for core in range(cores):
            for n, single in enumerate(SINGLES):
                sent[item * cores + core, layer : layer + 1, n * cut : (n + 1) * cut] = sums[
                    single : single + 1, item * cut : (item + 1) * cut
                ]
            sent[item * cores + core, layer : layer + 1, 6 * cut :] = sums[
                4 + row : 5 + row, column : column + 4 * cut
            ]


def bias_parts(sums, width):
    total = lax.axis_size("items")
    singles = jnp.concatenate([sums[:4], sums[8:10]], axis=0)
    singles = singles.reshape(6, total, width // total).swapaxes(0, 1).reshape(total, -1)
    return jnp.concatenate([singles, sums[4:8].reshape(total, -1)], axis=1)


def to_owners(parts):
    total, cores = lax.axis_size("items"), lax.axis_size("seq")
    sent = jnp.broadcast_to(parts.swapaxes(0, 1)[:, None], (total, cores, *parts.shape[::2]))
    return sent.reshape(total * cores, *parts.shape[::2])


def arrange_bias(owned, width):
    layers = owned.shape[0]
    cut = width // lax.axis_size("items")
    singles = owned[:, : 6 * cut].reshape(layers, 6, cut).swapaxes(1, 2)
    hidden = owned[:, 6 * cut :].reshape(layers, cut, 4)
    whole = jnp.concatenate([singles[..., :4], hidden, singles[..., 4:]], axis=2)
    return whole.reshape(layers, -1)


def on_device(
    tokens,
    lengths,
    cotangent,
    qkv_weight,
    out_weight,
    up_weight,
    down_weight,
    norm_gain,
    bias_master,
    first_moment,
    second_moment,
):
    item_count, part_len, width = tokens.shape
    levels = norm_gain.shape[0]
    rows = item_count * part_len
    core = lax.axis_index("seq")
    place = jnp.stack([lengths[0], core * part_len, (1 - core) * part_len]).astype(jnp.int32)
    turned = cotangent.reshape(rows, width).T

    chipped = lax.axis_size("items") in CHIPS
    if chipped:
        gather = Gather(qkv_weight, out_weight, up_weight, down_weight)
    else:
        plain = gather_plainly(qkv_weight, out_weight, up_weight, down_weight)
    state = tokens.reshape(rows, width)
    first = state
    if chipped:
        first, _ = lax.optimization_barrier((state, gather.mine[CHUNKS[0]]))
    state_other = swap_cores(first)
    if chipped:
        gather.computed.append(state_other)
    kept = [{} for _ in range(levels)]
    chunks = {}
    cycles = range(-1, 1 + max(KERNELS))
    for number, (action, level) in [(n, k) for n in cycles for k in (("", 0), *KERNELS.get(n, ()))]:
        if not action:
            if chipped:
                gather.cycle(number)
            if number == 0:
                master = in_rows(bias_master, bias_master.shape[1] // 10)
                if chipped:
                    master, _ = lax.optimization_barrier((master, gather.stages[0]["z"]))
                all_bias = everywhere(master)
                if chipped:
                    gather.computed.append(all_bias)
            if number == 1:
                bias_rows, columns = bias_table(all_bias, norm_gain, width)
                if chipped:
                    gather.computed += [*bias_rows, *columns, turned, place, gather.order]
            continue
        saved, bias = kept[level], bias_rows[level]
        kind = "attn" if action == "attention" else action
        chunk = gather.chunk((level, kind)) if chipped else plain[level, kind]
        chunks[level, kind] = chunk
        if action == "attention":
            (
                saved["p"],
                normed,
                saved["unit1"],
                saved["inverse1"],
                saved["o"],
                saved["q"],
                saved["k"],
                saved["v"],
            ) = attention_forward(place, state, state_other, chunk, bias)
            last = normed
        elif action == "up" and level < levels - 1:
            active, saved["slope"] = up_forward(normed, chunk, bias)
            last = active
        elif level < levels - 1:
            state, saved["unit2"], saved["inverse2"] = down_forward(
                normed, active, chunk, bias
            )
            last = state
            if chipped:
                stage = gather.stages[LAST - 1]
                waits = (stage["xy"], stage["yx"], gather.chunk((1, "attn")).arrays[-1])
                waits += (gather.swap_last(0, ()),)
                last, _ = lax.optimization_barrier((state, waits))
            last = state_other = swap_cores(last)
        if chipped:
            gather.computed.append(last)
            if (action, level) == ("down", 0):
                gather.swap_last(1, state_other)
                gather.swap_far(LAST - 1, state_other)
                gather.after = state_other
            if (action, level) == ("attention", 1):
                gather.swap_last(2, normed)

    axes = (lax.axis_size("items"), lax.axis_size("seq")) if chipped else None
    grads = [None] * levels
    for level in reversed(range(levels)):
        mine = {kind: chunks[level, kind] for kind in ("attn", "up", "down")}
        top = level == levels - 1
        if top:
            before = {"normed": normed, "cotangent": turned}
        else:
            before = {"grads": passed, "chunk": chunks[level + 1, "attn"], "sums": sums}
        outs = layer_backward(
            top,
            place,
            before,
            kept[level],
            mine,
            columns[level],
            bias_rows[level],
            axes,
        )
        if top:
            state, outs = outs[0], outs[1:]
        grad_sum, grad_q, kv_own, kv_other, sums = outs[:5]
        passed = [grad_sum, grad_q, kv_own, swap_cores(kv_other)]
        grads[level] = sums
    if chipped:
        sent = outs[5]
    else:
        sent = to_owners(jnp.stack([bias_parts(sums, width) for sums in grads]))
    layer_out = state.reshape(item_count, part_len, width)
    received = lax.all_to_all(sent, ("items", "seq"), 0, 0)
    input_grad = qkv_backward(passed, mine["attn"])
    received, _ = lax.optimization_barrier((received, input_grad))
    input_grad = input_grad.reshape(item_count, part_len, width)

    bias_grad = arrange_bias(jnp.sum(received, axis=0), width)
    new_first = beta_one * first_moment + (1.0 - beta_one) * bias_grad
    new_second = beta_two * second_moment + (1.0 - beta_two) * bias_grad * bias_grad
    first_hat = new_first / (1.0 - beta_one**STEP)
    second_hat = new_second / (1.0 - beta_two**STEP)
    new_bias = bias_master - learn_rate * first_hat / (jnp.sqrt(second_hat) + adam_eps)
    return (layer_out, input_grad, bias_grad, new_first, new_second, new_bias)


def solution(mesh):
    placed = (
        P("items", "seq", None),
        P("items"),
        P("items", "seq", None),
        P(None, "items", None),
        P(None, "items", None),
        P(None, "items", None),
        P(None, "items", None),
        P(),
        P(None, "items"),
        P(None, "items"),
        P(None, "items"),
    )
    return jax.shard_map(
        on_device,
        mesh=mesh,
        in_specs=placed,
        out_specs=(
            P("items", "seq", None),
            P("items", "seq", None),
            P(None, "items"),
            P(None, "items"),
            P(None, "items"),
            P(None, "items"),
        ),
        check_vma=False,
    )
```

```python
import functools
import math

import jax
import jax.numpy as jnp
from jax import lax
from jax.experimental import pallas as pl
from jax.experimental.pallas import tpu as pltpu
from jax.sharding import PartitionSpec as P

HEAD_DIM = 64
STEP = 10

ln_eps = 1e-12
beta_one = 0.9
beta_two = 0.999
adam_eps = 1e-08
learn_rate = 0.4
masked_score = -1000000000.0

CHIPS = {16: (4, 2, 2)}
CHUNKS = ((0, "attn"), (0, "up"), (0, "down"), (1, "attn"), (1, "up"), (1, "down"))
LAST = len(CHUNKS) - 1
KERNELS = {
    3: (("attention", 0),),
    4: (("up", 0),),
    5: (("down", 0), ("attention", 1)),
    6: (("up", 1), ("down", 1)),
}
SLOTS = 16
TILE = 256
WIDE = 512
STRIP = 32
F32 = jnp.float32
BF16 = jnp.bfloat16
VMEM_BYTES = 56 * 1024 * 1024

VMEM = pl.BlockSpec(memory_space=pltpu.VMEM)
SMEM = pl.BlockSpec(memory_space=pltpu.SMEM)
ANY = pl.BlockSpec(memory_space=pl.ANY)


def own_blocks(qkv_weight, out_weight, up_weight, down_weight):
    levels, rows, width = out_weight.shape
    keys = [(level, kind) for level in range(levels) for kind in ("attn", "up", "down")]
    core = lax.axis_index("seq").astype(jnp.int32).reshape(1)

    def kernel(core_ref, qkv, out, up, down, *refs):
        targets, (held, come, go) = refs[: len(keys)], refs[len(keys) :]
        here = core_ref[0]

        def copies(number, core):
            level, kind = keys[number]
            for half in range(2):
                if kind == "attn" and core == 0:
                    source = qkv.at[level, :, pl.ds(half * width, width)]
                elif kind == "attn":
                    source = out.at[level] if half else qkv.at[level, :, pl.ds(2 * width, width)]
                elif kind == "up":
                    column = pl.multiple_of((2 * here + half) * width, width)
                    source = up.at[level, :, pl.ds(column, width)]
                else:
                    row = pl.multiple_of((2 * here + half) * rows, rows)
                    source = down.at[level, pl.ds(row, rows), :]
                target = held.at[number, pl.ds(half * rows, rows), :]
                yield pltpu.make_async_copy(source, target, come.at[number, half])

        def each(act):
            for number, (_, kind) in enumerate(keys):
                if kind != "attn":
                    act(number, 0)
                    continue
                for side in range(2):
                    pl.when(here == side)(functools.partial(act, number, side))

        def begin(number, side):
            for copy in copies(number, side):
                copy.start()

        def finish(number, side):
            for copy in copies(number, side):
                copy.wait()

        each(begin)
        each(finish)
        leaving = [
            pltpu.make_async_copy(held.at[n], target, go.at[n]) for n, target in enumerate(targets)
        ]
        for copy in leaving:
            copy.start()
        for copy in leaving:
            copy.wait()

    blocks = pl.pallas_call(
        kernel,
        name="own_blocks",
        out_shape=[jax.ShapeDtypeStruct((2 * rows, width), BF16)] * len(keys),
        in_specs=[SMEM] + [ANY] * 4,
        out_specs=[ANY] * len(keys),
        scratch_shapes=[
            pltpu.VMEM((len(keys), 2 * rows, width), BF16),
            pltpu.SemaphoreType.DMA((len(keys), 2)),
            pltpu.SemaphoreType.DMA((len(keys),)),
        ],
        compiler_params=pltpu.CompilerParams(vmem_limit_bytes=VMEM_BYTES),
        cost_estimate=pl.CostEstimate(
            flops=0, bytes_accessed=8 * rows * width * len(keys), transcendentals=0
        ),
    )(core, qkv_weight, out_weight, up_weight, down_weight)
    return dict(zip(keys, blocks))


class Chunk:
    def __init__(self, arrays, runs, order):
        self.arrays, self.runs, self.order = arrays, runs, order
        self.count = sum(len(quarter) for quarter in runs)


def join(blocks, places=None):
    width = blocks[0].shape[1]
    total = sum(block.shape[0] for block in blocks)
    starts = [sum(block.shape[0] for block in blocks[:n]) for n in range(len(blocks))]
    table = [] if places is None else [places]

    def kernel(*refs):
        table_ref, refs = refs[: len(table)], refs[len(table) :]
        sources, (target, held, come, go) = refs[: len(blocks)], refs[len(blocks) :]
        ins, outs = [], []
        for n, (source, start) in enumerate(zip(sources, starts)):
            rows = blocks[n].shape[0]
            span = there = pl.ds(start, rows)
            if table:
                there = pl.ds(pl.multiple_of(table_ref[0][n] * rows, rows), rows)
            ins.append(pltpu.make_async_copy(source, held.at[span], come.at[n]))
            outs.append(pltpu.make_async_copy(held.at[span], target.at[there], go.at[n]))
            ins[-1].start()
        for come_in, go_out in zip(ins, outs):
            come_in.wait()
            go_out.start()
        for go_out in outs:
            go_out.wait()

    return pl.pallas_call(
        kernel,
        name="join",
        out_shape=jax.ShapeDtypeStruct((total, width), BF16),
        in_specs=[SMEM] * len(table) + [ANY] * len(blocks),
        out_specs=ANY,
        scratch_shapes=[
            pltpu.VMEM((total, width), BF16),
            pltpu.SemaphoreType.DMA((len(blocks),)),
            pltpu.SemaphoreType.DMA((len(blocks),)),
        ],
        compiler_params=pltpu.CompilerParams(vmem_limit_bytes=VMEM_BYTES),
        cost_estimate=pl.CostEstimate(
            flops=0, bytes_accessed=4 * total * width, transcendentals=0
        ),
    )(*table, *blocks)


class Gather:
    def __init__(self, *weights):
        self.total = lax.axis_size("items")
        self.depth, _, _ = CHIPS[self.total]
        self.plane = self.total // self.depth
        self.rows = weights[1].shape[1]
        self.mine = own_blocks(*weights)
        here = lax.axis_index("items") % self.plane
        core = lax.axis_index("seq")
        order = [here ^ side for side in range(4)]
        order += [core * 2, core * 2 + 1, 2 - core * 2, 3 - core * 2]
        self.order = jnp.stack(order).astype(jnp.int32)
        self.stages = [{} for _ in CHUNKS]
        self.last, self.computed = [], []

    def over_z(self, block):
        lines = [
            [place + self.plane * z for z in range(self.depth)] for place in range(self.plane)
        ]
        return lax.all_gather(block, "items", axis=0, tiled=True, axis_index_groups=lines)

    def step_z(self, block, step):
        pairs = [(item, (item + step * self.plane) % self.total) for item in range(self.total)]
        return lax.ppermute(block, "items", pairs)

    def line_of(self, parts):
        here = lax.axis_index("items") // self.plane
        places = [(here - step + self.depth) % self.depth for step in range(self.depth)]
        return join(parts, jnp.stack(places).astype(jnp.int32))

    def over(self, bit, block):
        return lax.ppermute(block, "items", [(item, item ^ bit) for item in range(self.total)])

    def across(self, x, y):
        half = x.shape[0] // 2
        return self.over(2, x[:half]), self.over(1, y[half:])

    def joined(self, stage):
        return join([stage[name] for name in ("z", "x", "y", "xy", "yx")])

    def cycle(self, number):
        wanted = {}
        if number == 0:
            wanted["corner"] = self.stages[LAST]["sides"][1:]
        if number == 1:
            wanted["sides"] = self.stages[LAST]["sides"]
        if 0 <= number < LAST - 1:
            wanted["block"] = self.mine[CHUNKS[number + 1]]
        if number == -1:
            wanted["first"] = self.mine[CHUNKS[0]]
            wanted["plane"] = self.mine[CHUNKS[LAST]]
        if LAST - 1 <= number <= LAST:
            wanted["line"] = self.stages[LAST]["lines"][number - LAST + 1]
        for lag in range(4):
            if 0 <= number - lag < LAST:
                wanted["lag%d" % lag] = self.stages[number - lag]
        def put(stage, name, value):
            stage[name] = value
            self.last.append(value)

        if 0 <= number <= LAST:
            self.before = self.last + self.computed
            wanted, _ = lax.optimization_barrier((wanted, self.before))
            self.last, self.computed = [], []
        elif number == -1:
            first = wanted["first"]
            steps = [self.step_z(first, step) for step in range(1, self.depth)]
            put(self.stages[0], "z", self.line_of([first, *steps]))

        if "lag3" in wanted:
            stage = self.stages[number - 3]
            if "joined" not in stage:
                put(stage, "joined", self.joined(wanted["lag3"]))
                wanted["lag3"] = stage
            put(stage, "other", swap_cores(wanted["lag3"]["joined"]))
        if "lag0" in wanted:
            along, stage = wanted["lag0"]["z"], self.stages[number]
            put(stage, "x", self.over(1, along))
            put(stage, "y", self.over(2, along))
        if "lag1" in wanted:
            held, stage = wanted["lag1"], self.stages[number - 1]
            stage["xy"], stage["yx"] = self.across(held["x"], held["y"])
            self.last += [stage["xy"], stage["yx"]]
        if "lag2" in wanted and number < LAST:
            put(self.stages[number - 2], "joined", self.joined(wanted["lag2"]))
        if "block" in wanted:
            put(self.stages[number + 1], "z", self.over_z(wanted["block"]))
        stage = self.stages[LAST]
        if LAST - 1 <= number <= LAST:
            stage.setdefault("z", []).append(self.over_z(wanted["line"]))
            if number < LAST:
                self.last.append(stage["z"][-1])
        if "plane" in wanted:
            own = wanted["plane"]
            x, y = self.over(1, own), self.over(2, own)
            stage["sides"] = [own, x, y]
            self.last += [x, y]
        if number == 0:
            x, y = wanted["corner"]
            stage["sides"] += self.across(x, y)
            self.last += stage["sides"][3:]
        if number == 1:
            _, x, y, xy, yx = wanted["sides"]
            stage["lines"] = [join([x, y[: self.rows]]), join([y[self.rows :], xy, yx])]
            self.last += stage["lines"]
        if 0 <= number < self.depth - 1:
            stage.setdefault("steps", [stage["sides"][0]])
            own, _ = lax.optimization_barrier((stage["steps"][0], self.before))
            stage["steps"].append(self.step_z(own, number + 1))
            self.last.append(stage["steps"][-1])
        if number == self.depth - 1:
            stage["z"] = [self.line_of(stage["steps"])]
            self.last.append(stage["z"][0])
    def swap_far(self, number, after):
        stage = self.stages[number]
        far, _ = lax.optimization_barrier(((stage["xy"], stage["yx"]), after))
        stage["xy2"], stage["yx2"] = [swap_cores(part) for part in far]
        return stage["xy2"], stage["yx2"]

    def swap_last(self, number, after):
        stage = self.stages[LAST]
        block, _ = lax.optimization_barrier((stage["z"][number], after))
        stage.setdefault("z2", []).append(swap_cores(block))
        return stage["z2"][-1]

    def chunk(self, key):
        number = CHUNKS.index(key)
        stage = self.stages[number]
        order = self.order
        if number == LAST:
            arrays = stage["z"] + stage["z2"]
            arrays = [a.reshape(self.depth, -1, self.rows, a.shape[1]) for a in arrays]
            spots = [(0, 0), (0, 1)] + [(1, n) for n in range(3)] + [(2, n) for n in range(3)]
            runs = [
                [
                    (array + spots[2 * side + part][0], spots[2 * side + part][1], 0, side, 0, self.depth)
                    for side in range(4)
                ]
                for array in (0, 3)
                for part in range(2)
            ]
            return Chunk(arrays, runs, order)
        half = self.depth // 2
        places = [(0, 0, self.depth), (1, 0, self.depth), (2, 0, self.depth)]
        places += [(3, 0, half), (3, half, self.depth - half)]
        own = [(n, 0, *place) for n, place in enumerate(places)]
        block = 2 * self.rows
        first = [0, self.depth, 2 * self.depth, 3 * self.depth, 3 * self.depth + half]
        other = [(5, *pair) for pair in ((first[n], *places[n]) for n in range(5))]
        names = ["z", "x", "y", "xy", "yx", "other"]
        if number == LAST - 1:
            late, _ = lax.optimization_barrier(
                (join([stage[name] for name in names[:3]]), self.after)
            )
            stage["other"] = swap_cores(late)
            other[3:] = [(6, 0, *places[3]), (7, 0, *places[4])]
            names += ["xy2", "yx2"]
        elif "other" not in stage:
            stage["other"] = swap_cores(self.joined(stage))
        arrays = [stage[name] for name in names]
        runs = [
            [(array, part, first, side, z, number) for array, first, side, z, number in spans]
            for spans in (own, other)
            for part in range(2)
        ]
        arrays = [a.reshape(a.shape[0] // block, 2, self.rows, a.shape[1]) for a in arrays]
        return Chunk(arrays, runs, order)


def gather_plainly(qkv_weight, out_weight, up_weight, down_weight):
    shards = {}
    for level in range(out_weight.shape[0]):
        shards[level, "attn"] = [qkv_weight[level], out_weight[level]]
        shards[level, "up"] = [up_weight[level]]
        shards[level, "down"] = [down_weight[level]]
    width = out_weight.shape[-1]
    plain = jnp.concatenate([jnp.arange(4), jnp.arange(4)]).astype(jnp.int32)
    rows = width // SLOTS
    runs = [[(c, side, 0, side, 0, 4) for side in range(4)] for c in range(4)]
    done = {}
    for key, parts in shards.items():
        whole = [lax.all_gather(part, "items", axis=0, tiled=True) for part in parts]
        if key[1] == "down":
            cut = whole[0].reshape(4, 4, 4, rows, width)
            arrays = [cut[:, :, c] for c in range(4)]
        else:
            joined = jnp.concatenate(whole, axis=1)
            arrays = [joined[:, width * c : width * (c + 1)] for c in range(4)]
            arrays = [array.reshape(4, 4, rows, width) for array in arrays]
        done[key] = Chunk(arrays, runs, plain)
    return done


def weight_shape(kind, width):
    rows = width // SLOTS
    return {
        "down": (4, 4, 4, rows, width),
        "up": (4, 4, 4, rows, width),
        "attn": (4, 4, 4, rows, width),
        "qkv": (3, 4, 4, rows, width),
        "out": (4, 4, rows, width),
    }[kind]


class Loads:
    def __init__(self, order, chunk, refs, kind, target, sems, first=0):
        self.order, self.chunk, self.refs, self.kind = order, chunk, refs, kind
        self.target, self.sems, self.first = target, sems, first

    def visit(self, act, only=None):
        number = self.first
        for quarter, runs in enumerate(self.chunk.runs):
            if only not in (None, quarter):
                number += len(runs)
                continue
            which = self.order[4 + quarter]

            def run(number=number, runs=runs, which=which):
                for n, (array, part, first, side, z, depth) in enumerate(runs):
                    source = self.refs[array].at[pl.ds(first, depth), part]
                    span, place = pl.ds(z, depth), self.order[side]
                    if self.kind == "down":
                        target = self.target.at[span, place, which]
                    elif self.kind == "out":
                        target = self.target.at[span, place]
                    else:
                        target = self.target.at[which, span, place]
                    act(pltpu.make_async_copy(source, target, self.sems.at[number + n]))

            if self.kind == "out":
                pl.when(which == 3)(run)
            elif self.kind == "qkv":
                pl.when(which != 3)(run)
            else:
                run()
            number += len(runs)

    def start(self):
        self.visit(lambda copy: copy.start())

    def wait(self, only=None):
        self.visit(lambda copy: copy.wait(), only)


def call(kernel, name, operands, outs, scratch, flops, transcendentals=0, far=()):
    moved = sum(a.size * a.dtype.itemsize for a, _ in operands)
    moved += sum(math.prod(s) * jnp.dtype(d).itemsize for s, d in outs)
    return pl.pallas_call(
        kernel,
        name=name,
        out_shape=[jax.ShapeDtypeStruct(s, d) for s, d in outs],
        in_specs=[spec for _, spec in operands],
        out_specs=[ANY if n in far else VMEM for n in range(len(outs))],
        scratch_shapes=scratch,
        compiler_params=pltpu.CompilerParams(vmem_limit_bytes=VMEM_BYTES),
        cost_estimate=pl.CostEstimate(
            flops=int(flops), bytes_accessed=int(moved), transcendentals=int(transcendentals)
        ),
    )(*[a for a, _ in operands])


def nt(left, right):
    return lax.dot_general(left, right, (((1,), (1,)), ((), ())), preferred_element_type=F32)


def tn(left, right):
    return lax.dot_general(left, right, (((0,), (0,)), ((), ())), preferred_element_type=F32)


def nn(left, right):
    return jnp.dot(left, right, preferred_element_type=F32)


def swap_cores(block):
    return lax.ppermute(block, "seq", [(0, 1), (1, 0)])


def tile_at(index, size=TILE):
    return pl.ds(pl.multiple_of(index * size, size), size)


def fold_rows(values):
    return jnp.sum(values.reshape(-1, 8, values.shape[-1]), axis=0)


def column_loop(width, body):
    for index in range(width // WIDE):
        body(pl.ds(index * WIDE, WIDE))


def matrix(weight, *index):
    blocks = weight[index] if index else weight[...]
    return blocks.reshape(-1, blocks.shape[-1])


def columns_of(weight, at, *index):
    rest = weight.ndim - len(index) - 1
    blocks = weight[(*index, *[slice(None)] * rest, at)]
    return blocks.reshape(-1, blocks.shape[-1])


def token_sums(values, counted=None):
    if counted is None:
        counted = jnp.ones((1, values.shape[1]), BF16)
    return nt(jnp.broadcast_to(counted, (8, values.shape[1])), values)[0:1]


def turn(source, target):
    for index in range(source.shape[1] // 128):
        span = pl.ds(index * 128, 128)
        target[span, :] = source[:, span].T


def normalize_strips(rows, source, gain, shift, unit, inverse, result):
    def strip(index, carry):
        at = tile_at(index, STRIP)
        values = source[at, :]
        center = values - jnp.mean(values, axis=-1, keepdims=True)
        spread = jnp.mean(center * center, axis=-1, keepdims=True)
        scale = lax.rsqrt(spread + ln_eps)
        normal = center * scale
        unit[at, :] = normal
        inverse[at, :] = jnp.broadcast_to(scale, (STRIP, inverse.shape[1]))
        result[at, :] = (normal * gain + shift).astype(BF16)
        return carry

    lax.fori_loop(0, rows // STRIP, strip, 0, unroll=4)


def attention_forward(place, state, state_other, chunk, bias_rows):
    rows, width = state.shape
    heads = width // HEAD_DIM
    arrays, count = len(chunk.arrays), chunk.count
    score_scale = 1.0 / math.sqrt(HEAD_DIM)

    def kernel(order, place_ref, state_ref, other_state, bias_ref, *refs):
        prob_hbm, result, unit_out, inverse_out, o_out, q_out, k_out, value = refs[
            arrays : arrays + 8
        ]
        prob_ref, query, key, mixed, total, unit, inverse, states, weight, sems, leave = refs[
            arrays + 8 :
        ]
        loads = Loads(order, chunk, refs[:arrays], "attn", weight, sems)
        loads.start()
        states[:rows, :] = state_ref[...]
        states[rows:, :] = other_state[...]
        spot = lax.broadcasted_iota(jnp.int32, (2 * rows, 1), 0)
        position = jnp.where(spot < rows, place_ref[1] + spot, place_ref[2] + spot - rows)
        live = position < place_ref[0]
        line = lax.broadcasted_iota(jnp.int32, (2 * HEAD_DIM, 1), 0)
        loads.wait(0)
        loads.wait(2)
        pl.when(order[5] != 3)(lambda: loads.wait(1))
        pl.when(order[5] == 3)(lambda: loads.wait(3))

        def project(at):
            query[:, at] = (
                nn(state_ref[...], columns_of(weight, at, 0)) + bias_ref[0:1, at]
            ).astype(BF16)
            key[:, at] = nn(states[...], columns_of(weight, at, 1)).astype(BF16)
            value[:, at] = (nn(states[...], columns_of(weight, at, 2)) + bias_ref[1:2, at]).astype(
                BF16
            )

        column_loop(width, project)
        turn(query, q_out)
        turn(key, k_out)

        spans = [slice(start, start + 128) for start in range(0, 2 * rows, 128)]

        def leaving(index):
            span = pl.ds(2 * index, 2)
            return pltpu.make_async_copy(prob_ref.at[span], prob_hbm.at[span], leave.at[index])

        def pair(index, carry):
            at = tile_at(index, 2 * HEAD_DIM)
            turned = value[:, at].T
            outs = []
            for side in range(2):
                mine = (line // HEAD_DIM == side).astype(F32) * score_scale
                asked = q_out[at, :] * mine.astype(BF16)
                blocks = [nn(key[span, at], asked) for span in spans]
                blocks = [jnp.where(live[s], b, masked_score) for s, b in zip(spans, blocks)]
                tops = [jnp.max(block, axis=0, keepdims=True) for block in blocks]
                top = functools.reduce(jnp.maximum, tops)
                blocks = [jnp.exp(block - top) for block in blocks]
                norm = sum(jnp.sum(block, axis=0, keepdims=True) for block in blocks)
                norm = 1.0 / norm
                weights = jnp.concatenate([(b * norm).astype(BF16) for b in blocks], axis=0)
                prob_ref[2 * index + side] = weights
                outs.append(nn(turned[HEAD_DIM * side : HEAD_DIM * (side + 1)], weights))
            outs = jnp.concatenate(outs, axis=0)
            o_out[at, :] = outs
            mixed[:, at] = outs.T.astype(BF16)
            leaving(index).start()
            return carry

        lax.fori_loop(0, heads // 2, pair, 0, unroll=8)
        pl.when(order[5] != 3)(lambda: loads.wait(3))
        pl.when(order[5] == 3)(lambda: loads.wait(1))

        def column(at):
            total[:, at] = (
                state_ref[:, at].astype(F32)
                + nn(mixed[...], columns_of(weight, at, 3))
                + bias_ref[2:3, at]
            )

        column_loop(width, column)
        normalize_strips(rows, total, bias_ref[10:11, :], bias_ref[3:4, :], unit, inverse, result)
        turn(unit, unit_out)
        inverse_out[...] = inverse[...].T[:8]
        for index in range(heads // 2):
            leaving(index).wait()

    return call(
        kernel,
        "attention_forward",
        [
            (chunk.order, SMEM),
            (place, SMEM),
            (state, VMEM),
            (state_other, VMEM),
            (bias_rows, VMEM),
        ]
        + [(a, ANY) for a in chunk.arrays],
        [
            ((heads, 2 * rows, rows), BF16),
            ((rows, width), BF16),
            ((width, rows), F32),
            ((8, rows), F32),
            ((width, rows), F32),
            ((width, rows), BF16),
            ((width, 2 * rows), BF16),
            ((2 * rows, width), BF16),
        ],
        [
            pltpu.VMEM((heads, 2 * rows, rows), BF16),
            pltpu.VMEM((rows, width), BF16),
            pltpu.VMEM((2 * rows, width), BF16),
            pltpu.VMEM((rows, width), BF16),
            pltpu.VMEM((rows, width), F32),
            pltpu.VMEM((rows, width), F32),
            pltpu.VMEM((rows, 128), F32),
            pltpu.VMEM((2 * rows, width), BF16),
            pltpu.VMEM(weight_shape("attn", width), BF16),
            pltpu.SemaphoreType.DMA((count,)),
            pltpu.SemaphoreType.DMA((heads // 2,)),
        ],
        2 * rows * width * width * 6 + 8 * rows * rows * width,
        heads * rows * rows * 2,
        far=(0,),
    )


def up_part(order, loads, normed_ref, bias_ref, weight, active, slope, then=None):
    width = normed_ref.shape[1]
    for quarter in range(4):
        which = order[4 + quarter]
        loads.wait(quarter)
        if quarter == 1 and then is not None:
            then()

        def column(index, carry, which=which):
            at = tile_at(index)
            there = pl.ds(pl.multiple_of(which * width + index * TILE, TILE), TILE)
            whole = nn(normed_ref[...], columns_of(weight, at, which))
            for start in range(0, whole.shape[0], 128):
                span = slice(start, start + 128)
                hidden = whole[span] + bias_ref[pl.ds(4 + which, 1), at]
                normal = 0.5 * (1.0 + lax.erf(hidden * (1.0 / math.sqrt(2.0))))
                density = jnp.exp(-0.5 * hidden * hidden) * (1.0 / math.sqrt(2.0 * math.pi))
                active[span, there] = (hidden * normal).astype(BF16)
                slope[there, span] = (normal + hidden * density).T
            return carry

        lax.fori_loop(0, width // TILE, column, 0, unroll=4)


def up_forward(normed, chunk, bias_rows):
    rows, width = normed.shape
    arrays, count = len(chunk.arrays), chunk.count
    hidden_width = 4 * width

    def kernel(order, normed_ref, bias_ref, *refs):
        active, slope, weight, sems = refs[arrays:]
        loads = Loads(order, chunk, refs[:arrays], "up", weight, sems)
        loads.start()
        up_part(order, loads, normed_ref, bias_ref, weight, active, slope)

    return call(
        kernel,
        "up_forward",
        [(chunk.order, SMEM), (normed, VMEM), (bias_rows, VMEM)] + [(a, ANY) for a in chunk.arrays],
        [((rows, hidden_width), BF16), ((hidden_width, rows), F32)],
        [pltpu.VMEM(weight_shape("up", width), BF16), pltpu.SemaphoreType.DMA((count,))],
        2 * rows * width * hidden_width,
        2 * rows * hidden_width,
    )


def down_part(
    normed_ref, active_ref, bias_ref, weight, total, unit, inverse, result, unit_out, inverse_out
):
    rows, width = normed_ref.shape

    def column(at):
        total[:, at] = (
            normed_ref[:, at].astype(F32)
            + nn(active_ref[...], columns_of(weight, at))
            + bias_ref[8:9, at]
        )

    column_loop(width, column)
    normalize_strips(rows, total, bias_ref[11:12, :], bias_ref[9:10, :], unit, inverse, result)
    turn(unit, unit_out)
    inverse_out[...] = inverse[...].T[:8]


def down_forward(normed, active, chunk, bias_rows):
    rows, width = normed.shape
    arrays, count = len(chunk.arrays), chunk.count

    def kernel(order, normed_ref, active_ref, bias_ref, *refs):
        result, unit_out, inverse_out, total, unit, inverse, weight, sems = refs[arrays:]
        loads = Loads(order, chunk, refs[:arrays], "down", weight, sems)
        loads.start()
        loads.wait()
        down_part(
            normed_ref,
            active_ref,
            bias_ref,
            weight,
            total,
            unit,
            inverse,
            result,
            unit_out,
            inverse_out,
        )

    return call(
        kernel,
        "down_forward",
        [(chunk.order, SMEM), (normed, VMEM), (active, VMEM), (bias_rows, VMEM)]
        + [(a, ANY) for a in chunk.arrays],
        [((rows, width), BF16), ((width, rows), F32), ((8, rows), F32)],
        [
            pltpu.VMEM((rows, width), F32),
            pltpu.VMEM((rows, width), F32),
            pltpu.VMEM((rows, 128), F32),
            pltpu.VMEM(weight_shape("down", width), BF16),
            pltpu.SemaphoreType.DMA((count,)),
        ],
        2 * rows * width * width * 4,
    )


def norm_backward(upstream, gain, unit, inverse, wide, narrow):
    width, rows = unit.shape
    strips = [pl.ds(index * 128, 128) for index in range(width // 128)]
    mean = jnp.zeros((8, rows), F32)
    lean = jnp.zeros((8, rows), F32)
    for at in strips:
        scaled = upstream(at) * gain(at)
        mean = mean + fold_rows(scaled)
        lean = lean + fold_rows(scaled * unit[at, :])
    mean = jnp.sum(mean, axis=0, keepdims=True) * (1.0 / width)
    lean = jnp.sum(lean, axis=0, keepdims=True) * (1.0 / width)
    for at in strips:
        below = inverse[0:1, :] * (upstream(at) * gain(at) - mean - unit[at, :] * lean)
        wide[at, :] = below
        narrow[at, :] = below.astype(BF16)


def through_qkv(order, loads, da, dq, own, received, weight, grads, total):
    width, rows = da.shape
    grads[0] = dq[...]
    for part in range(2):
        span = pl.ds(part * width, width)
        grads[1 + part] = (own[span, :].astype(F32) + received[span, :].astype(F32)).astype(BF16)
    total[...] = da[...]
    for quarter in range(4):
        which = order[4 + quarter]

        def add(quarter=quarter, which=which):
            loads.wait(quarter)
            for index in range(8):
                at = pl.ds(index * (width // 8), width // 8)
                half = slice(index % 2 * 2, index % 2 * 2 + 2)
                total[at, :] += nn(matrix(weight, which, index // 2, half), grads[which])

        pl.when(which != 3)(add)


def layer_backward(top, place, before, saved, chunks, columns, bias_rows, axes):
    queries, keys, values, prob, mixed = (saved[name] for name in ("q", "k", "v", "p", "o"))
    width, rows = queries.shape
    heads = width // HEAD_DIM
    hidden_width = 4 * width
    score_scale = 1.0 / math.sqrt(HEAD_DIM)
    used = [(chunks["down"], "down"), (chunks["up"], "up"), (chunks["attn"], "out")]
    if top:
        first = [before["normed"], before["cotangent"], bias_rows]
        slope = []
    else:
        used = [(before["chunk"], "qkv")] + used
        first = [*before["grads"], saved["unit2"], saved["inverse2"]]
        slope = [saved["slope"]]
    cutting = not top and axes is not None
    first += [columns, saved["unit1"], saved["inverse1"], mixed, queries, keys, values, prob]
    first += slope
    blocks = [a for chunk, _ in used for a in chunk.arrays]
    counts = [chunk.count for chunk, _ in used]
    fetched = [a.size * a.dtype.itemsize > 2**17 for a in first]

    def kernel(place_ref, *refs):
        refs = list(refs)

        def take(number):
            taken, refs[:] = refs[:number], refs[number:]
            return taken

        orders = take(len(used))
        given = take(len(first))
        sources = [take(len(chunk.arrays)) for chunk, _ in used]
        if cutting:
            (above_sums,) = take(1)
        if top:
            (state_out,) = take(1)
        targets = take(4)
        (sums,) = take(1)
        sent = take(1) if cutting else None
        weights = take(len(used))
        copies = []
        for number, far in enumerate(fetched):
            if far:
                (held,) = take(1)
                copies.append((given[number], held))
                given[number] = held
            else:
                copies.append(None)
        da, dq, kv_own, kv_other, wide, narrow, hidden, sems, extra, leave = take(10)
        loads = []
        for number, (chunk, kind) in enumerate(used):
            loads.append(
                Loads(
                    orders[number],
                    chunk,
                    sources[number],
                    kind,
                    weights[number],
                    sems,
                    sum(counts[:number]),
                )
            )
        copies = [
            pltpu.make_async_copy(*pair, extra.at[number]) if pair else None
            for number, pair in enumerate(copies)
        ]
        start = len(first) - 8 - len(slope)
        late = [start + 3, start + 4, start + 5, start + 6, start + 7]
        if top:
            stages = [([loads[1]], [0]), ([loads[0]], [1, start, start + 1]), ([loads[2]], late)]
        else:
            stages = [
                ([loads[0]], [0, 1, 2, 3]),
                ([loads[1]], [4, start, start + 8]),
                ([loads[2]], [start + 1]),
                ([loads[3]], late),
            ]
        stages = [
            [*weights_in, *[copies[n] for n in numbers if copies[n] is not None]]
            for weights_in, numbers in stages
        ]

        def begin(number):
            if number < len(stages):
                for item in stages[number]:
                    item.start()

        def finish(number, skipped=0):
            for item in stages[number][skipped:]:
                item.wait()
            begin(number + (1 if top else 3))

        begin(0)
        if not top:
            begin(1)
            begin(2)
        down, up, out = weights[-3:]

        if top:
            normed_ref, cotangent_ref, bias_ref = given[:3]
            column_ref, unit1, inverse1, o_ref, q_ref, k_ref, v_ref, prob_ref = given[3:]
            slope_ref, active_ref, total, unit, inverse, unit2, inverse2 = take(7)
            for item in stages[0][1:]:
                item.wait()
            up_part(
                orders[1],
                loads[1],
                normed_ref,
                bias_ref,
                up,
                active_ref,
                slope_ref,
                lambda: begin(1),
            )
            finish(1)
            down_part(
                normed_ref,
                active_ref,
                bias_ref,
                    down,
                total,
                unit,
                inverse,
                state_out,
                unit2,
                inverse2,
            )
            token = lax.broadcasted_iota(jnp.int32, (1, rows), 1) + place_ref[1]
            row_live = (token < place_ref[0]).astype(F32)

            def above_two(at):
                return cotangent_ref[at, :].astype(F32) * row_live

            sums[9:10, :] = token_sums(cotangent_ref[...], row_live.astype(BF16))
        else:
            da_above, dq_above, kv_above, kv_received, unit2, inverse2 = given[:6]
            column_ref, unit1, inverse1, o_ref, q_ref, k_ref, v_ref, prob_ref, slope_ref = given[6:]
            above_ref, both = take(2)
            finish(0, 1)
            through_qkv(
                orders[0],
                loads[0],
                da_above,
                dq_above,
                kv_above,
                kv_received,
                weights[0],
                both,
                wide,
            )
            above_ref[...] = wide[...].astype(BF16)
            finish(1)

            def above_two(at):
                return above_ref[at, :].astype(F32)

            sums[9:10, :] = token_sums(above_ref[...])

        norm_backward(above_two, lambda at: column_ref[at, 11:12], unit2, inverse2, wide, narrow)
        sums[8:9, :] = token_sums(narrow[...])
        piece = width // 8
        for part in range(4):
            for index in range(8):
                there = pl.ds(part * width + index * piece, piece)
                half = slice(index % 2 * 2, index % 2 * 2 + 2)
                grad = nn(matrix(down, part, index // 2, half), narrow[...])
                hidden[there, :] = (grad * slope_ref[there, :]).astype(BF16)
        for part in range(4):
            sums[4 + part : 5 + part, :] = token_sums(hidden[part * width : (part + 1) * width, :])
        if not top:
            finish(len(stages) - 2)
        for index in range(8):
            at = pl.ds(index * piece, piece)
            half = slice(index % 2 * 2, index % 2 * 2 + 2)
            rows_up = [matrix(up, part, index // 2, half) for part in range(4)]
            grad = wide[at, :] + nn(jnp.concatenate(rows_up, axis=1), hidden[...])
            wide[at, :] = grad
            narrow[at, :] = grad.astype(BF16)
        sums[3:4, :] = token_sums(narrow[...])
        norm_backward(
            lambda at: wide[at, :], lambda at: column_ref[at, 10:11], unit1, inverse1, da, narrow
        )
        leaving = [
            pltpu.make_async_copy(held, target, leave.at[n])
            for n, (held, target) in enumerate(zip((da, dq, kv_own, kv_other), targets))
        ]
        leaving[0].start()
        sums[2:3, :] = token_sums(narrow[...])
        finish(len(stages) - 1)
        mixed = hidden.at[pl.ds(0, width)]
        for index in range(8):
            half = slice(index % 2 * 2, index % 2 * 2 + 2)
            made = nn(matrix(out, index // 2, half), narrow[...])
            mixed[pl.ds(index * piece, piece), :] = made.astype(BF16)
        line = lax.broadcasted_iota(jnp.int32, (2 * HEAD_DIM, 1), 0)

        def pair(index, carry):
            at = tile_at(index, 2 * HEAD_DIM)
            grad_out = mixed[at, :]
            value = v_ref[:, at]
            for side in range(2):
                here = pl.ds(
                    pl.multiple_of(index * 2 * HEAD_DIM + side * HEAD_DIM, HEAD_DIM), HEAD_DIM
                )
                low = pl.ds(
                    pl.multiple_of(width + index * 2 * HEAD_DIM + side * HEAD_DIM, HEAD_DIM),
                    HEAD_DIM,
                )
                probs = prob_ref[2 * index + side]
                inner = jnp.sum(mixed[here, :].astype(F32) * o_ref[here, :], axis=0, keepdims=True)
                masked = grad_out * (line // HEAD_DIM == side).astype(F32).astype(BF16)
                grad_s = []
                for block in range(2 * rows // 128):
                    span = slice(block * 128, (block + 1) * 128)
                    grad_p = nn(value[span], masked)
                    grad_s.append((probs[span].astype(F32) * (grad_p - inner)).astype(BF16))
                grad_s = jnp.concatenate(grad_s, axis=0)
                dq[here, :] = (nn(k_ref[here, :], grad_s) * score_scale).astype(BF16)
                grad_k = (nt(q_ref[here, :], grad_s) * score_scale).astype(BF16)
                grad_v = nt(mixed[here, :], probs).astype(BF16)
                kv_own[here, :] = grad_k[:, :rows]
                kv_other[here, :] = grad_k[:, rows:]
                kv_own[low, :] = grad_v[:, :rows]
                kv_other[low, :] = grad_v[:, rows:]
            under = pl.ds(pl.multiple_of(width + index * 2 * HEAD_DIM, HEAD_DIM), 2 * HEAD_DIM)
            for n, held, spans in ((1, dq, (at,)), (2, kv_own, (at, under)), (3, kv_other, (at, under))):
                for span in spans:
                    pltpu.make_async_copy(held.at[span], targets[n].at[span], leave.at[n]).start()
            return carry

        lax.fori_loop(0, heads // 2, pair, 0, unroll=4)
        sums[0:1, :] = token_sums(dq[...])
        sums[1:2, :] = token_sums(kv_own[width:, :]) + token_sums(kv_other[width:, :])
        if cutting:
            cut_sums(sums, sent[0], 0, *axes)
            cut_sums(above_sums, sent[0], 1, *axes)
        for copy in leaving:
            copy.wait()

    outs = [((width, rows), F32), ((width, rows), BF16)]
    outs += [((2 * width, rows), BF16)] * 2 + [((16, width), F32)]
    scratch = [pltpu.VMEM(a.shape, a.dtype) for a, far in zip(first, fetched) if far]
    scratch += [pltpu.VMEM(*out) for out in outs[:4]]
    scratch += [
        pltpu.VMEM((width, rows), F32),
        pltpu.VMEM((width, rows), BF16),
        pltpu.VMEM((hidden_width, rows), BF16),
        pltpu.SemaphoreType.DMA((sum(counts),)),
        pltpu.SemaphoreType.DMA((len(first),)),
        pltpu.SemaphoreType.DMA((4,)),
    ]
    if cutting:
        outs += [((axes[0] * axes[1], 2, 10 * width // axes[0]), F32)]
    if top:
        outs = [((rows, width), BF16)] + outs
        scratch += [
            pltpu.VMEM((hidden_width, rows), F32),
            pltpu.VMEM((rows, hidden_width), BF16),
            pltpu.VMEM((rows, width), F32),
            pltpu.VMEM((rows, width), F32),
            pltpu.VMEM((rows, 128), F32),
            pltpu.VMEM((width, rows), F32),
            pltpu.VMEM((8, rows), F32),
        ]
    else:
        scratch += [pltpu.VMEM((width, rows), BF16), pltpu.VMEM((3, width, rows), BF16)]
    return call(
        kernel,
        "layer_backward",
        [(place, SMEM)]
        + [(chunk.order, SMEM) for chunk, _ in used]
        + [(a, ANY if far else VMEM) for a, far in zip(first, fetched)]
        + [(a, ANY) for a in blocks]
        + ([(before["sums"], VMEM)] if cutting else []),
        outs,
        [pltpu.VMEM(weight_shape(kind, width), BF16) for _, kind in used] + scratch,
        2 * rows * width * width * 13 + 16 * rows * rows * width,
        far=range(1, 5) if top else range(4),
    )


def qkv_backward(grads, chunk):
    width, rows = grads[0].shape
    arrays, count = len(chunk.arrays), chunk.count

    def kernel(order, da, dq, own, received, *refs):
        result, both, total, weight, sems = refs[arrays:]
        loads = Loads(order, chunk, refs[:arrays], "qkv", weight, sems)
        loads.start()
        through_qkv(order, loads, da, dq, own, received, weight, both, total)
        grad = total[...].astype(BF16)
        for index in range(width // 128):
            at = pl.ds(index * 128, 128)
            result[:, at] = grad[index * 128 : (index + 1) * 128].T

    return call(
        kernel,
        "qkv_backward",
        [(chunk.order, SMEM)] + [(g, VMEM) for g in grads] + [(a, ANY) for a in chunk.arrays],
        [((rows, width), BF16)],
        [
            pltpu.VMEM((3, width, rows), BF16),
            pltpu.VMEM((width, rows), F32),
            pltpu.VMEM(weight_shape("qkv", width), BF16),
            pltpu.SemaphoreType.DMA((count,)),
        ],
        2 * rows * width * width * 3,
    )[0]


def everywhere(values):
    total = lax.axis_size("items")
    return lax.all_to_all(jnp.broadcast_to(values, (total, *values.shape)), "items", 0, 0)


def in_rows(entries, cut):
    layers = entries.shape[0]
    grid = entries.reshape(layers, cut, 10)
    singles = jnp.concatenate([grid[..., :4], grid[..., 8:]], axis=2).swapaxes(1, 2)
    hidden = grid[..., 4:8].reshape(layers, -1)
    return jnp.concatenate([singles.reshape(layers, -1), hidden], axis=1)


SINGLES = (0, 1, 2, 3, 8, 9)


def bias_table(parts, norm_gain, width):
    total, layers, _ = parts.shape
    cut = width // total
    if total not in CHIPS:
        singles = parts[..., : 6 * cut].reshape(total, layers, 6, cut)
        singles = singles.transpose(1, 2, 0, 3).reshape(layers, 6, width)
        hidden = parts[..., 6 * cut :].swapaxes(0, 1).reshape(layers, 4, width)
        rows = jnp.concatenate([singles[:, :4], hidden, singles[:, 4:], norm_gain], axis=1)
        rows = jnp.pad(rows, ((0, 0), (0, 116), (0, 0)))
        return list(rows[:, :16]), list(rows.swapaxes(1, 2))

    def kernel(parts_ref, gain_ref, *refs):
        tables, columns, held = refs[:layers], refs[layers : 2 * layers], refs[-1]
        held[...] = jnp.zeros_like(held)
        for layer in range(layers):
            for item in range(total):
                for n, row in enumerate(SINGLES):
                    held[row : row + 1, item * cut : (item + 1) * cut] = parts_ref[
                        item, layer : layer + 1, n * cut : (n + 1) * cut
                    ]
                row, column = divmod(item * 4 * cut, width)
                held[4 + row : 5 + row, column : column + 4 * cut] = parts_ref[
                    item, layer : layer + 1, 6 * cut :
                ]
            held[10:12, :] = gain_ref[layer]
            tables[layer][...] = held[:16, :]
            turn(held, columns[layer])

    outs = call(
        kernel,
        "bias_table",
        [(parts, VMEM), (norm_gain, VMEM)],
        [((16, width), F32)] * layers + [((width, 128), F32)] * layers,
        [pltpu.VMEM((128, width), F32)],
        0,
    )
    return outs[:layers], outs[layers:]


def cut_sums(sums, sent, layer, total, cores):
    cut = sums.shape[1] // total
    for item in range(total):
        row, column = divmod(item * 4 * cut, sums.shape[1])
        for core in range(cores):
            for n, single in enumerate(SINGLES):
                sent[item * cores + core, layer : layer + 1, n * cut : (n + 1) * cut] = sums[
                    single : single + 1, item * cut : (item + 1) * cut
                ]
            sent[item * cores + core, layer : layer + 1, 6 * cut :] = sums[
                4 + row : 5 + row, column : column + 4 * cut
            ]


def bias_parts(sums, width):
    total = lax.axis_size("items")
    singles = jnp.concatenate([sums[:4], sums[8:10]], axis=0)
    singles = singles.reshape(6, total, width // total).swapaxes(0, 1).reshape(total, -1)
    return jnp.concatenate([singles, sums[4:8].reshape(total, -1)], axis=1)


def to_owners(parts):
    total, cores = lax.axis_size("items"), lax.axis_size("seq")
    sent = jnp.broadcast_to(parts.swapaxes(0, 1)[:, None], (total, cores, *parts.shape[::2]))
    return sent.reshape(total * cores, *parts.shape[::2])


def arrange_bias(owned, width):
    layers = owned.shape[0]
    cut = width // lax.axis_size("items")
    singles = owned[:, : 6 * cut].reshape(layers, 6, cut).swapaxes(1, 2)
    hidden = owned[:, 6 * cut :].reshape(layers, cut, 4)
    whole = jnp.concatenate([singles[..., :4], hidden, singles[..., 4:]], axis=2)
    return whole.reshape(layers, -1)


def on_device(
    tokens,
    lengths,
    cotangent,
    qkv_weight,
    out_weight,
    up_weight,
    down_weight,
    norm_gain,
    bias_master,
    first_moment,
    second_moment,
):
    item_count, part_len, width = tokens.shape
    levels = norm_gain.shape[0]
    rows = item_count * part_len
    core = lax.axis_index("seq")
    place = jnp.stack([lengths[0], core * part_len, (1 - core) * part_len]).astype(jnp.int32)
    turned = cotangent.reshape(rows, width).T

    chipped = lax.axis_size("items") in CHIPS
    if chipped:
        gather = Gather(qkv_weight, out_weight, up_weight, down_weight)
    else:
        plain = gather_plainly(qkv_weight, out_weight, up_weight, down_weight)
    state = tokens.reshape(rows, width)
    first = state
    if chipped:
        first, _ = lax.optimization_barrier((state, gather.mine[CHUNKS[0]]))
    state_other = swap_cores(first)
    if chipped:
        gather.computed.append(state_other)
    kept = [{} for _ in range(levels)]
    chunks = {}
    cycles = range(-1, 1 + max(KERNELS))
    for number, (action, level) in [(n, k) for n in cycles for k in (("", 0), *KERNELS.get(n, ()))]:
        if not action:
            if chipped:
                gather.cycle(number)
            if number == 0:
                master = in_rows(bias_master, bias_master.shape[1] // 10)
                if chipped:
                    master, _ = lax.optimization_barrier((master, gather.stages[0]["z"]))
                all_bias = everywhere(master)
                if chipped:
                    gather.computed.append(all_bias)
            if number == 1:
                bias_rows, columns = bias_table(all_bias, norm_gain, width)
                if chipped:
                    gather.computed += [*bias_rows, *columns, turned, place, gather.order]
            continue
        saved, bias = kept[level], bias_rows[level]
        kind = "attn" if action == "attention" else action
        chunk = gather.chunk((level, kind)) if chipped else plain[level, kind]
        chunks[level, kind] = chunk
        if action == "attention":
            (
                saved["p"],
                normed,
                saved["unit1"],
                saved["inverse1"],
                saved["o"],
                saved["q"],
                saved["k"],
                saved["v"],
            ) = attention_forward(place, state, state_other, chunk, bias)
            last = normed
        elif action == "up" and level < levels - 1:
            active, saved["slope"] = up_forward(normed, chunk, bias)
            last = active
        elif level < levels - 1:
            state, saved["unit2"], saved["inverse2"] = down_forward(
                normed, active, chunk, bias
            )
            last = state
            if chipped:
                stage = gather.stages[LAST - 1]
                waits = (stage["xy"], stage["yx"], gather.chunk((1, "attn")).arrays[-1])
                waits += (gather.swap_last(0, ()),)
                last, _ = lax.optimization_barrier((state, waits))
            last = state_other = swap_cores(last)
        if chipped:
            gather.computed.append(last)
            if (action, level) == ("down", 0):
                gather.swap_last(1, state_other)
                gather.swap_far(LAST - 1, state_other)
                gather.after = state_other
            if (action, level) == ("attention", 1):
                gather.swap_last(2, normed)

    axes = (lax.axis_size("items"), lax.axis_size("seq")) if chipped else None
    grads = [None] * levels
    for level in reversed(range(levels)):
        mine = {kind: chunks[level, kind] for kind in ("attn", "up", "down")}
        top = level == levels - 1
        if top:
            before = {"normed": normed, "cotangent": turned}
        else:
            before = {"grads": passed, "chunk": chunks[level + 1, "attn"], "sums": sums}
        outs = layer_backward(
            top,
            place,
            before,
            kept[level],
            mine,
            columns[level],
            bias_rows[level],
            axes,
        )
        if top:
            state, outs = outs[0], outs[1:]
        grad_sum, grad_q, kv_own, kv_other, sums = outs[:5]
        passed = [grad_sum, grad_q, kv_own, swap_cores(kv_other)]
        grads[level] = sums
    if chipped:
        sent = outs[5]
    else:
        sent = to_owners(jnp.stack([bias_parts(sums, width) for sums in grads]))
    layer_out = state.reshape(item_count, part_len, width)
    received = lax.all_to_all(sent, ("items", "seq"), 0, 0)
    input_grad = qkv_backward(passed, mine["attn"])
    received, _ = lax.optimization_barrier((received, input_grad))
    input_grad = input_grad.reshape(item_count, part_len, width)

    bias_grad = arrange_bias(jnp.sum(received, axis=0), width)
    new_first = beta_one * first_moment + (1.0 - beta_one) * bias_grad
    new_second = beta_two * second_moment + (1.0 - beta_two) * bias_grad * bias_grad
    first_hat = new_first / (1.0 - beta_one**STEP)
    second_hat = new_second / (1.0 - beta_two**STEP)
    new_bias = bias_master - learn_rate * first_hat / (jnp.sqrt(second_hat) + adam_eps)
    return (layer_out, input_grad, bias_grad, new_first, new_second, new_bias)


def solution(mesh):
    placed = (
        P("items", "seq", None),
        P("items"),
        P("items", "seq", None),
        P(None, "items", None),
        P(None, "items", None),
        P(None, "items", None),
        P(None, "items", None),
        P(),
        P(None, "items"),
        P(None, "items"),
        P(None, "items"),
    )
    return jax.shard_map(
        on_device,
        mesh=mesh,
        in_specs=placed,
        out_specs=(
            P("items", "seq", None),
            P("items", "seq", None),
            P(None, "items"),
            P(None, "items"),
            P(None, "items"),
            P(None, "items"),
        ),
        check_vma=False,
    )
```
